512 devices in a mesh: gx: 32 (over x_lo, y, core), row: 16 (over x_hi, z).
Axes of the slice: x: 4 (x_hi: 2, x_lo: 2; x = x_hi * 2 + x_lo), y: 8, z: 8, core: 2. Of those that a mesh axis runs over, the one named last changes fastest.
Arguments:
- test_vectors: float32 [2, 5, 64, 256, 128], P(None, None, 'gx', 'row')
- base_coeffs: float32 [101, 64, 256], P(None, 'gx', 'row'), as said below
- panel_set: float32 [512, 10, 10], P(('gx', 'row')), as said below
- owner_index: int32 [1], replicated, may hold values from 0 to 511
Outputs:
- basis: float32 [2, 5, 64, 128, 256], P(None, None, 'gx', 'row')
The draws below stay inside these ranges and needn't reach their ends.
Inputs may be any that keep to these rules, and one draw needn't show every extreme that they name: `owner_index`: the index, with gx slowest, of the device whose panel this window uses. `panel_set`: panels are nonsingular. `base_coeffs`: viscosities are positive.
All inputs are finite; a program needn't handle non-finite values.
Results may differ from the reference program's by a relative error of at most 0.0003.
Values sent between devices are 32-bit elements; how exact they have to be, the bound alone decides.
No kernel may reach another device: no remote copies, remote signals or barrier semaphores. Data moves between devices by JAX's collectives and lax.ppermute only.
A program may use at most 64 MiB of HBM per device.

```python
import math
import jax
import jax.numpy as jnp
from jax import lax

NV = 5
K = 2
STEPS = 2
NT = 128
KV = 10
NX = 64
NR = 256
OWNERS = 512


def draw_test_vectors(key, part):
    key = jax.random.fold_in(key, 11)
    key_base, key_cell = jax.random.split(key, 2)
    x_frac = jnp.arange(NX, dtype=jnp.float32) / max(NX - 1, 1)
    r_frac = jnp.arange(NR, dtype=jnp.float32) / max(NR - 1, 1)
    ramp = jnp.power(3.0, x_frac)[:, None] * jnp.power(3.0, r_frac)[None, :]
    cell_scale = jnp.power(10.0, jax.random.uniform(key_cell, (NX, NR, NT), dtype=jnp.float32))
    amplitude = 0.1 * ramp[:, :, None] * cell_scale
    rough = jax.random.normal(key_base, (K, NV, NX, NR, NT), dtype=jnp.float32)
    return rough * amplitude[None, None]


def draw_base_coeffs(key, part):
    key = jax.random.fold_in(key, 23)
    key_adv, key_react, key_visc = jax.random.split(key, 3)
    n_pair = NV * NV
    advect = 0.15 * jax.random.normal(key_adv, (3 * n_pair, NX, NR), dtype=jnp.float32)
    reaction = 0.1 * jax.random.normal(key_react, (n_pair, NX, NR), dtype=jnp.float32)
    viscous = jnp.exp(jax.random.uniform(key_visc, (1, NX, NR), dtype=jnp.float32, minval=math.log(0.02), maxval=math.log(0.1)))
    return jnp.concatenate([advect, reaction, viscous], axis=0)


def draw_panel_set(key, part):
    key = jax.random.fold_in(key, 37)
    diagonal = 3.0 * jnp.eye(KV, dtype=jnp.float32)[None]
    spread = 0.25 * jax.random.normal(key, (OWNERS, KV, KV), dtype=jnp.float32)
    return diagonal + spread


def setup_inputs(seed: int = 0) -> dict:
    splits = jax.random.split(jax.random.key(seed), 5)
    test_vectors = draw_test_vectors(jax.random.fold_in(splits[4], 71), 0)
    base_coeffs = draw_base_coeffs(jax.random.fold_in(splits[4], 71), 0)
    panel_set = draw_panel_set(jax.random.fold_in(splits[4], 71), 0)
    owner_index = jax.random.randint(splits[3], (1,), 0, OWNERS).astype(jnp.int32)
    return dict(test_vectors=test_vectors, base_coeffs=base_coeffs, panel_set=panel_set, owner_index=owner_index)


def advance(padded, coeffs):
    n_var = padded.shape[1]
    n_pair = n_var * n_var
    advect = coeffs[:3 * n_pair].reshape((3, n_var, n_var) + coeffs.shape[1:])
    reaction = coeffs[3 * n_pair:4 * n_pair].reshape((n_var, n_var) + coeffs.shape[1:])
    viscous = coeffs[4 * n_pair]
    fluxes = jnp.einsum('djixr,kjxrt->dkixrt', advect, padded, precision=lax.Precision.HIGHEST)
    centre = padded[:, :, 1:-1, 1:-1]
    stream = fluxes[0, :, :, 2:, 1:-1] - fluxes[0, :, :, :-2, 1:-1]
    radial = fluxes[1, :, :, 1:-1, 2:] - fluxes[1, :, :, 1:-1, :-2]
    beside_all = fluxes[2, :, :, 1:-1, 1:-1]
    azimuth = jnp.roll(beside_all, -1, axis=4) - jnp.roll(beside_all, 1, axis=4)
    neighbours = padded[:, :, 2:, 1:-1] + padded[:, :, :-2, 1:-1] + padded[:, :, 1:-1, 2:] + padded[:, :, 1:-1, :-2]
    neighbours = neighbours + jnp.roll(centre, -1, axis=4) + jnp.roll(centre, 1, axis=4)
    source = jnp.einsum('jixr,kjxrt->kixrt', reaction[:, :, 1:-1, 1:-1], centre, precision=lax.Precision.HIGHEST)
    return centre + stream + radial + azimuth + viscous[1:-1, 1:-1, None] * (neighbours - 6.0 * centre) + source

def reference(test_vectors, base_coeffs, panel_set, owner_index):
    panel_now = lax.dynamic_index_in_dim(panel_set, owner_index[0].astype(jnp.int32), 0, keepdims=False)
    coeff_pad = jnp.pad(base_coeffs, ((0, 0), (1, 1), (1, 1)))
    field = test_vectors
    for repeat in range(STEPS):
        field = advance(jnp.pad(field, ((0, 0), (0, 0), (1, 1), (1, 1), (0, 0))), coeff_pad)
    sketch = jnp.dot(panel_now, field.reshape(K * NV, -1), precision=lax.Precision.HIGHEST)
    first = sketch[:NV]
    second = sketch[NV:]
    unit_one = first / jnp.sqrt(jnp.sum(first * first))
    projection = jnp.sum(unit_one * second)
    remainder = second - projection * unit_one
    unit_two = remainder / jnp.sqrt(jnp.sum(remainder * remainder))
    scale = math.sqrt(NV * NX * NR * NT)
    basis = jnp.stack([unit_one, unit_two]).reshape(K, NV, NX, NR, NT) * scale
    return basis.transpose(0, 1, 2, 4, 3)
```

```python
import math

import jax
import jax.numpy as jnp
from jax import lax
from jax.sharding import PartitionSpec as P

STEPS = 2


def everyone(value, axis):
    count = lax.axis_size(axis)
    flat = value.reshape(1, 1, -1)
    sent = jnp.broadcast_to(flat, (count,) + flat.shape[1:])
    got = lax.all_to_all(sent, axis, 0, 0, tiled=True)
    return got.reshape((count,) + value.shape)


def with_halo(block, axis, dim, width):
    count = lax.axis_size(axis)
    forward = [(i, i + 1) for i in range(count - 1)]
    backward = [(target, source) for source, target in forward]
    low = lax.ppermute(
        lax.slice_in_dim(block, block.shape[dim] - width, None, axis=dim), axis, forward
    )
    high = lax.ppermute(lax.slice_in_dim(block, 0, width, axis=dim), axis, backward)
    return jnp.concatenate([low, block, high], axis=dim)


def advance(padded, coeffs):
    n_var = padded.shape[1]
    n_pair = n_var * n_var
    advect = coeffs[: 3 * n_pair].reshape((3, n_var, n_var) + coeffs.shape[1:])
    reaction = coeffs[3 * n_pair : 4 * n_pair].reshape((n_var, n_var) + coeffs.shape[1:])
    viscous = coeffs[4 * n_pair]
    fluxes = jnp.einsum("djixr,kjxrt->dkixrt", advect, padded, precision=lax.Precision.HIGHEST)
    centre = padded[:, :, 1:-1, 1:-1]
    stream = fluxes[0, :, :, 2:, 1:-1] - fluxes[0, :, :, :-2, 1:-1]
    radial = fluxes[1, :, :, 1:-1, 2:] - fluxes[1, :, :, 1:-1, :-2]
    beside_all = fluxes[2, :, :, 1:-1, 1:-1]
    azimuth = jnp.roll(beside_all, -1, axis=4) - jnp.roll(beside_all, 1, axis=4)
    neighbours = (
        padded[:, :, 2:, 1:-1]
        + padded[:, :, :-2, 1:-1]
        + padded[:, :, 1:-1, 2:]
        + padded[:, :, 1:-1, :-2]
    )
    neighbours = neighbours + jnp.roll(centre, -1, axis=4) + jnp.roll(centre, 1, axis=4)
    source = jnp.einsum(
        "jixr,kjxrt->kixrt", reaction[:, :, 1:-1, 1:-1], centre, precision=lax.Precision.HIGHEST
    )
    return (
        centre
        + stream
        + radial
        + azimuth
        + viscous[1:-1, 1:-1, None] * (neighbours - 6.0 * centre)
        + source
    )


def safe_ratio(cross, square):
    positive = square > 0
    return jnp.where(positive, cross / jnp.where(positive, square, 1.0), 0.0)


def merged(parts):
    square, cross, rest = parts[:, 0], parts[:, 1], parts[:, 2]
    square_all = jnp.sum(square)
    cross_all = jnp.sum(cross)
    shift = safe_ratio(cross, square) - safe_ratio(cross_all, square_all)
    return jnp.stack([square_all, cross_all, jnp.sum(rest + square * shift * shift)])


def body(test_vectors, base_coeffs, panel_set, owner_index):
    count_x = lax.axis_size("gx")
    count_r = lax.axis_size("row")
    n_vec, n_var, wide_x, wide_r, n_theta = test_vectors.shape
    here = lax.axis_index("gx") * count_r + lax.axis_index("row")
    panel = jnp.where(here == owner_index[0], panel_set[0], 0.0)
    panel = jnp.sum(everyone(panel, "row"), axis=0)
    panel = jnp.sum(everyone(panel, "gx"), axis=0)

    n_coeff = base_coeffs.shape[0]
    n_pair = n_vec * n_var
    field = test_vectors.reshape((n_pair, wide_x, wide_r, n_theta))
    turned = base_coeffs.transpose(1, 2, 0)
    turned = jnp.pad(turned, ((0, 0), (0, 0), (0, n_theta - n_coeff)))
    both = jnp.concatenate([field, turned[None]], axis=0)
    both = with_halo(both, "row", 2, 2)
    both = with_halo(both, "gx", 1, 2)
    coeffs = both[n_pair, :, :, :n_coeff].transpose(2, 0, 1)
    field = both[:n_pair].reshape((n_vec, n_var) + both.shape[1:])
    place_x = lax.axis_index("gx") * wide_x + jnp.arange(-1, wide_x + 1)
    place_r = lax.axis_index("row") * wide_r + jnp.arange(-1, wide_r + 1)
    inside = ((place_x >= 0) & (place_x < wide_x * count_x))[:, None, None] & (
        (place_r >= 0) & (place_r < wide_r * count_r)
    )[None, :, None]
    field = jnp.where(inside, advance(field, coeffs), 0.0)
    field = advance(field, coeffs[:, 1:-1, 1:-1])

    sketch = jnp.dot(panel, field.reshape(n_pair, -1), precision=lax.Precision.HIGHEST)
    first = sketch[:n_var]
    second = sketch[n_var:]
    square = jnp.sum(first * first)
    cross = jnp.sum(first * second)
    rest = second - safe_ratio(cross, square) * first
    triple = jnp.stack([square, cross, jnp.sum(rest * rest)])
    triple = merged(everyone(triple, "gx"))
    triple = merged(everyone(triple, "row"))
    inv_one = 1.0 / jnp.sqrt(triple[0])
    inv_two = 1.0 / jnp.sqrt(triple[2])
    projection = triple[1] * inv_one
    scale = math.sqrt(n_var * wide_x * count_x * wide_r * count_r * n_theta)

    turned = sketch.reshape(n_vec, n_var, wide_x, wide_r, n_theta).transpose(0, 1, 2, 4, 3)
    turned = lax.all_to_all(turned, "row", split_axis=3, concat_axis=4, tiled=True)
    one = (scale * inv_one) * turned[0]
    two = (scale * inv_two) * turned[1] - (scale * inv_two * projection * inv_one) * turned[0]
    return jnp.stack([one, two])


def solution(mesh):
    placed = (
        P(None, None, "gx", "row", None),
        P(None, "gx", "row"),
        P(("gx", "row"), None, None),
        P(),
    )
    return jax.shard_map(
        body,
        mesh=mesh,
        in_specs=placed,
        out_specs=P(None, None, "gx", "row", None),
        check_vma=False,
    )
```

```python
import math

import jax
import jax.numpy as jnp
from jax import lax
from jax.experimental import pallas as pl
from jax.experimental.pallas import tpu as pltpu
from jax.sharding import PartitionSpec as P

STEPS = 2
RIM = 2
LANES = 128
ROWS = 8
RING = 12
HIGH, LOW, SIZE, PANEL = 64, 76, 88, 100


def two_sum(a, b):
    total = a + b
    part = total - a
    return total, (a - (total - part)) + (b - part)


def quick_two_sum(a, b):
    total = a + b
    return total, b - (total - a)


def split(a):
    wide = a * 4097.0
    high = wide - (wide - a)
    return high, a - high


def two_prod(a, b):
    product = a * b
    a_high, a_low = split(a)
    b_high, b_low = split(b)
    return product, ((a_high * b_high - product) + a_high * b_low + a_low * b_high) + a_low * b_low


def pair_add(a, b):
    high, low = two_sum(a[0], b[0])
    return quick_two_sum(high, low + (a[1] + b[1]))


def pair_mul(a, b):
    high, low = two_prod(a[0], b[0])
    return quick_two_sum(high, low + (a[0] * b[1] + a[1] * b[0]))


def pair_scale(a, factor):
    high, low = two_prod(a[0], factor)
    return quick_two_sum(high, low + a[1] * factor)


def pair_roll(a, shift, axis):
    size = a[0].shape[axis]
    return tuple(pltpu.roll(part, shift % size, axis) for part in a)


def pair_tree(pairs):
    while len(pairs) > 1:
        rest = [pairs[-1]] if len(pairs) % 2 else []
        pairs = [pair_add(pairs[i], pairs[i + 1]) for i in range(0, len(pairs) - 1, 2)] + rest
    return pairs[0]


def tree(parts, join):
    while len(parts) > 1:
        rest = [parts[-1]] if len(parts) % 2 else []
        parts = [join(parts[i], parts[i + 1]) for i in range(0, len(parts) - 1, 2)] + rest
    return parts[0]


def lanes_of(shape):
    return lax.broadcasted_iota(jnp.int32, shape, 1)


def roll_lanes(value, shift):
    return pltpu.roll(value, shift % LANES, 1)


def safe_inverse(value):
    positive = value > 0
    return jnp.where(positive, 1.0 / jnp.where(positive, value, 1.0), 0.0)


def merge(tiles):
    size = tree(tiles, jnp.maximum)
    inverse = safe_inverse(size)
    scaled = []
    for tile in tiles:
        ratio = tile * inverse
        ratio = roll_lanes(ratio * ratio, HIGH - SIZE)
        scaled.append(pair_scale((tile, roll_lanes(tile, HIGH - LOW)), ratio))
    return pair_tree(scaled), size, tree(tiles, jnp.add)


def placed_at(lane, start, width, value, other):
    return jnp.where((lane >= start) & (lane < start + width), value, other)


def pack_stats(pair, size, panel):
    lane = lanes_of(size.shape)
    tile = placed_at(lane, HIGH, RING, pair[0], 0.0)
    tile = placed_at(lane, LOW, RING, roll_lanes(pair[1], LOW - HIGH), tile)
    tile = placed_at(lane, SIZE, RING, size, tile)
    return jnp.where(lane >= PANEL, panel, tile)


def march_kernel(
    n_var, wide_x, wide_r, count_x, count_r,
    place_ref, low_ref, mid_ref, high_ref, panel_ref,
    out_ref, rows_ref, now_ref, next_ref, coeff_ref, packed_ref, parts_ref,
):
    n_plane = low_ref.shape[0] - 1
    n_theta = low_ref.shape[-1]
    n_tile = n_theta // ROWS
    deep = wide_r + 2 * RIM
    n_pair = n_var * n_var
    used = (wide_x + 2 * RIM) * deep

    for plane in range(n_plane + 1):
        blocks = [low_ref[plane, x] for x in range(RIM)]
        blocks += [mid_ref[plane, x] for x in range(wide_x)]
        blocks += [high_ref[plane, x] for x in range(RIM)]
        for x, block in enumerate(blocks):
            rows_ref[plane, x * deep : (x + 1) * deep, :] = block
        rows_ref[plane, used:LANES, :] = jnp.zeros((LANES - used, n_theta), jnp.float32)
    for plane in range(n_plane):
        turned = rows_ref[plane].T
        now_ref[plane, ROWS : ROWS + n_theta, :] = turned
        now_ref[plane, ROWS - 1 : ROWS, :] = turned[n_theta - 1 :]
        now_ref[plane, ROWS + n_theta : ROWS + n_theta + 1, :] = turned[:1]
    coeff_ref[: n_theta, :] = rows_ref[n_plane].T
    viscous = coeff_ref[4 * n_pair : 4 * n_pair + 1, :]
    for i in range(n_var):
        own = 3 * n_pair + i * n_var + i
        coeff_ref[own : own + 1, :] = coeff_ref[own : own + 1, :] + (1.0 - 6.0 * viscous)
    for n, shift in enumerate((deep, -deep, 1, -1)):
        coeff_ref[n_theta + n : n_theta + n + 1, :] = roll_lanes(viscous, shift)

    lane = lanes_of((ROWS, LANES))
    at_x = lane // deep - RIM + place_ref[0] * wide_x
    at_r = lane % deep - RIM + place_ref[1] * wide_r
    inside = (at_x >= 0) & (at_x < wide_x * count_x) & (at_r >= 0) & (at_r < wide_r * count_r)
    inside = inside & (lane < used)

    def coeff(index):
        return coeff_ref[index : index + 1, :]

    def advance(source_ref, tile):
        start = ROWS + tile * ROWS
        centre = [source_ref[b, pl.ds(start, ROWS), :] for b in range(n_plane)]
        before = [source_ref[b, pl.ds(start - 1, ROWS), :] for b in range(n_plane)]
        after = [source_ref[b, pl.ds(start + 1, ROWS), :] for b in range(n_plane)]
        differ = [a - b for a, b in zip(after, before)]
        both = [a + b for a, b in zip(after, before)]
        result = [None] * n_plane
        for i in range(n_var):
            for k in range(0, n_plane, n_var):
                stream = radial = local = 0.0
                for j in range(n_var):
                    at = j * n_var + i
                    stream = stream + coeff(at) * centre[k + j]
                    radial = radial + coeff(n_pair + at) * centre[k + j]
                    local = local + coeff(2 * n_pair + at) * differ[k + j]
                    local = local + coeff(3 * n_pair + at) * centre[k + j]
                own = centre[k + i]
                local = local + coeff(4 * n_pair) * both[k + i]
                local = local + roll_lanes(coeff(n_theta) * own + stream, -deep)
                local = local + roll_lanes(coeff(n_theta + 1) * own - stream, deep)
                local = local + roll_lanes(coeff(n_theta + 2) * own + radial, -1)
                local = local + roll_lanes(coeff(n_theta + 3) * own - radial, 1)
                result[k + i] = local
        return result

    def first_step(tile, carry):
        result = advance(now_ref, tile)
        for b in range(n_plane):
            next_ref[b, pl.ds(ROWS + tile * ROWS, ROWS), :] = jnp.where(inside, result[b], 0.0)
        return carry

    lax.fori_loop(0, n_tile, first_step, 0)
    for b in range(n_plane):
        next_ref[b, ROWS - 1 : ROWS, :] = next_ref[b, ROWS + n_theta - 1 : ROWS + n_theta, :]
        next_ref[b, ROWS + n_theta : ROWS + n_theta + 1, :] = next_ref[b, ROWS : ROWS + 1, :]

    group = wide_x * wide_r
    per_vreg = LANES // group
    n_wide = packed_ref.shape[-1] // LANES

    def second_step(tile, largest):
        result = advance(next_ref, tile)
        for v in range(n_wide):
            packed = jnp.zeros((ROWS, LANES), jnp.float32)
            for b in range(v * per_vreg, min((v + 1) * per_vreg, n_plane)):
                for x in range(wide_x):
                    target = (b % per_vreg) * group + x * wide_r
                    shift = target - ((x + RIM) * deep + RIM)
                    packed = placed_at(lane, target, wide_r, roll_lanes(result[b], shift), packed)
            packed_ref[tile, :, v * LANES : (v + 1) * LANES] = packed
            largest = jnp.maximum(largest, jnp.abs(packed))
        return largest

    largest = lax.fori_loop(0, n_tile, second_step, jnp.zeros((ROWS, LANES), jnp.float32))
    largest = jnp.max(largest, axis=1, keepdims=True)
    largest = jnp.max(largest, axis=0, keepdims=True)
    inverse = safe_inverse(jnp.broadcast_to(largest, (ROWS, LANES)))
    largest = jnp.broadcast_to(largest, (ROWS, LANES))

    for tile in range(n_tile):
        for v in range(n_wide):
            high, low = split(packed_ref[tile, :, v * LANES : (v + 1) * LANES] * inverse)
            parts_ref[0, tile, v] = high
            parts_ref[1, tile, v] = low

    def shifted(part, tile, v, s):
        whole, rest = divmod(s, per_vreg)
        value = parts_ref[part, tile, (v + whole) % n_wide]
        if not rest:
            return value
        other = parts_ref[part, tile, (v + whole + 1) % n_wide]
        keep = lane < LANES - rest * group
        return jnp.where(keep, roll_lanes(value, -rest * group), roll_lanes(other, -rest * group))

    pairs = [[None] * n_wide for _ in range(ROWS)]
    zero = jnp.zeros((ROWS, LANES), jnp.float32)
    for s in range(RING // 2 + 1):
        for v in range(n_wide):
            total, error = zero, zero
            for tile in range(n_tile):
                a_high, a_low = parts_ref[0, tile, v], parts_ref[1, tile, v]
                if s:
                    b_high, b_low = shifted(0, tile, v, s), shifted(1, tile, v, s)
                    minor = a_high * b_low + a_low * b_high
                else:
                    b_high, b_low = a_high, a_low
                    minor = 2.0 * a_high * a_low
                total, lost = two_sum(total, a_high * b_high)
                error = error + (lost + (minor + a_low * b_low))
            pairs[s][v] = quick_two_sum(total, error)
    row = lax.broadcasted_iota(jnp.int32, (ROWS, LANES), 0)
    sums = []
    for v in range(n_wide):
        level = [pairs[s][v] if s <= RING // 2 else (zero, zero) for s in range(ROWS)]
        half = ROWS // 2
        while half:
            joined = []
            for s in range(half):
                a, b = level[s], level[s + half]
                front = (row // half) % 2 == 0
                a_turned, b_turned = pair_roll(a, -half, 0), pair_roll(b, half, 0)
                one = tuple(jnp.where(front, p, q) for p, q in zip(a, b_turned))
                two = tuple(jnp.where(front, p, q) for p, q in zip(a_turned, b))
                joined.append(pair_add(one, two))
            level = joined
            half //= 2
        sums.append(level[0])
    step = group // 2
    while step:
        sums = [pair_add(a, pair_roll(a, -step, 1)) for a in sums]
        step //= 2
    gathered = (zero, zero)
    for b in range(RING):
        turned = pair_roll(sums[b // per_vreg], HIGH + b - (b % per_vreg) * group, 1)
        gathered = tuple(jnp.where(lane == HIGH + b, p, q) for p, q in zip(turned, gathered))
    stats = pack_stats(gathered, largest, panel_ref[...])
    last = (n_wide - 1) * LANES
    for tile in range(n_tile):
        out_ref[tile, :, :last] = packed_ref[tile, :, :last]
        out_ref[tile, :, last:] = jnp.where(lane < HIGH, packed_ref[tile, :, last:], stats)


def reduce_kernel(got_ref, out_ref):
    count, _, wide = got_ref.shape
    pair, size, panel = merge([got_ref[n, :, wide - LANES :] for n in range(count)])
    tile = pack_stats(pair, size, panel)
    for n in range(out_ref.shape[0]):
        out_ref[n] = tile


def relay_kernel(n_plane, wide_x, wide_r, got_ref, out_ref):
    count = got_ref.shape[0]
    per_vreg = LANES // wide_r
    lane = lanes_of((ROWS, LANES))
    for g in range(n_plane * wide_x):
        v, slot = divmod(g, per_vreg)
        for half in range(count // per_vreg):
            value = jnp.zeros((ROWS, LANES), jnp.float32)
            for n in range(per_vreg):
                source = got_ref[half * per_vreg + n, :, v * LANES : (v + 1) * LANES]
                turned = roll_lanes(source, (n - slot) * wide_r)
                value = placed_at(lane, n * wide_r, wide_r, turned, value)
            out_ref[g, :, half * LANES : (half + 1) * LANES] = value


def final_kernel(n_var, wide_x, scale, got_ref, cells_ref, out_ref, weight_ref):
    n_plane = 2 * n_var
    tiles = [got_ref[n] for n in range(got_ref.shape[0])]
    pair, size, tile = merge(tiles)
    lane = lanes_of((ROWS, LANES))
    row = lax.broadcasted_iota(jnp.int32, (ROWS, LANES), 0)
    live = row < n_var
    one = jnp.where(live & (lane < n_plane), roll_lanes(tile, -PANEL), 0.0)
    two = jnp.where(live & (lane < n_plane), roll_lanes(tile, -PANEL - n_plane), 0.0)
    left = one + roll_lanes(one, RING) + roll_lanes(two, 2 * RING)
    right = one + roll_lanes(two, RING) + roll_lanes(two, 2 * RING)
    inner = []
    for part in pair:
        at = jnp.where(lane < RING, roll_lanes(part, -HIGH), 0.0)
        inner.append(at + roll_lanes(at, RING) + roll_lanes(at, 2 * RING))
    place = lane % RING

    def turned(value, s):
        if not s:
            return value
        return jnp.where(place < RING - s, roll_lanes(value, -s), roll_lanes(value, RING - s))

    terms = []
    for s in range(RING // 2 + 1):
        left_s, right_s = turned(left, s), turned(right, s)
        term = pair_add(two_prod(left, right_s), two_prod(left_s, right))
        share = 1.0 if s % (RING // 2) else 0.5
        row_s = tuple(share * part[s : s + 1, :] for part in inner)
        terms.append(pair_mul(term, row_s))
    total = pair_tree(terms)
    for shift in (4, 2, 1):
        total = pair_add(total, pair_roll(total, shift, 0))
    total = pair_add(total, pair_roll(total, -RING // 2, 1))
    total = pair_add(total, pair_roll(total, -RING // 4, 1))
    total = pair_tree([total, pair_roll(total, -1, 1), pair_roll(total, -2, 1)])

    def everywhere(part, at):
        return jnp.broadcast_to(part[:, at : at + 1], (ROWS, LANES))

    square, cross, other = (
        tuple(everywhere(part, g * RING) for part in total) for g in range(3)
    )
    ratio = cross[0] / square[0]
    left_over = pair_add(cross, tuple(-p for p in pair_scale(square, ratio)))
    ratio = quick_two_sum(ratio, left_over[0] / square[0])
    rest = pair_add(other, tuple(-p for p in pair_mul(cross, ratio)))
    largest = everywhere(size, SIZE)
    inv_one = scale / jnp.sqrt(square[0]) / largest
    inv_two = scale / jnp.sqrt(rest[0]) / largest
    weight_ref[:ROWS, :] = inv_one * one
    weight_ref[ROWS:, :] = inv_two * two - (inv_two * ratio[0]) * one

    for a in range(n_plane):
        at = (a // n_var) * ROWS + a % n_var
        weights = jnp.broadcast_to(weight_ref[at : at + 1, :], (ROWS, LANES))
        spread = [everywhere(weights, b) for b in range(n_plane)]
        for x in range(wide_x):
            for h in range(cells_ref.shape[-1] // LANES):
                cut = slice(h * LANES, (h + 1) * LANES)
                value = spread[0] * cells_ref[x, :, cut]
                for b in range(1, n_plane):
                    value = value + spread[b] * cells_ref[b * wide_x + x, :, cut]
                out_ref[a * wide_x + x, :, cut] = value


VMEM = pl.BlockSpec(memory_space=pltpu.VMEM)
PARAMS = pltpu.CompilerParams(vmem_limit_bytes=32 * 1024 * 1024)


def with_halo(block, axis, dim, width):
    count = lax.axis_size(axis)
    forward = [(i, i + 1) for i in range(count - 1)]
    backward = [(target, source) for source, target in forward]
    low = lax.ppermute(
        lax.slice_in_dim(block, block.shape[dim] - width, None, axis=dim), axis, forward
    )
    high = lax.ppermute(lax.slice_in_dim(block, 0, width, axis=dim), axis, backward)
    return low, high


def body(test_vectors, base_coeffs, panel_set, owner_index):
    count_x = lax.axis_size("gx")
    count_r = lax.axis_size("row")
    n_vec, n_var, wide_x, wide_r, n_theta = test_vectors.shape
    n_coeff = base_coeffs.shape[0]
    n_plane = n_vec * n_var
    at_x, at_r = lax.axis_index("gx"), lax.axis_index("row")

    panel = panel_set[0] / jnp.max(jnp.abs(panel_set[0]))
    panel = jnp.where(at_x * count_r + at_r == owner_index[0], panel, 0.0)
    panel = jnp.concatenate([panel[:n_var], panel[n_var:]], axis=1)
    panel = jnp.pad(panel, ((0, ROWS - n_var), (PANEL, LANES - PANEL - 2 * n_plane)))

    field = test_vectors.reshape((n_plane, wide_x, wide_r, n_theta))
    turned = base_coeffs.transpose(1, 2, 0)
    turned = jnp.pad(turned, ((0, 0), (0, 0), (0, n_theta - n_coeff)))
    both = jnp.concatenate([field, turned[None]], axis=0)
    low, high = with_halo(both, "row", 2, RIM)
    both = jnp.concatenate([low, both, high], axis=2)
    low, high = with_halo(both, "gx", 1, RIM)

    n_wide = 3
    n_tile = n_theta // ROWS
    sent = pl.pallas_call(
        lambda *refs: march_kernel(n_var, wide_x, wide_r, count_x, count_r, *refs),
        out_shape=jax.ShapeDtypeStruct((n_tile, ROWS, n_wide * LANES), jnp.float32),
        in_specs=[pl.BlockSpec(memory_space=pltpu.SMEM)] + [VMEM] * 4,
        out_specs=VMEM,
        scratch_shapes=[
            pltpu.VMEM((n_plane + 1, LANES, n_theta), jnp.float32),
            pltpu.VMEM((n_plane, n_theta + 2 * ROWS, LANES), jnp.float32),
            pltpu.VMEM((n_plane, n_theta + 2 * ROWS, LANES), jnp.float32),
            pltpu.VMEM((n_theta + ROWS, LANES), jnp.float32),
            pltpu.VMEM((n_tile, ROWS, n_wide * LANES), jnp.float32),
            pltpu.VMEM((2, n_tile, n_wide, ROWS, LANES), jnp.float32),
        ],
        compiler_params=PARAMS,
        name="march",
    )(jnp.stack([at_x, at_r]), low, both, high, panel)
    got = lax.all_to_all(sent, "row", 0, 0, tiled=True)
    stats = pl.pallas_call(
        reduce_kernel,
        out_shape=jax.ShapeDtypeStruct((count_x, ROWS, LANES), jnp.float32),
        in_specs=[VMEM],
        out_specs=VMEM,
        compiler_params=PARAMS,
        name="reduce",
    )(got)
    stats = lax.all_to_all(stats, "gx", 0, 0, tiled=True)
    cells = pl.pallas_call(
        lambda *refs: relay_kernel(n_plane, wide_x, wide_r, *refs),
        out_shape=jax.ShapeDtypeStruct((n_plane * wide_x, ROWS, count_r * wide_r), jnp.float32),
        in_specs=[VMEM],
        out_specs=VMEM,
        compiler_params=PARAMS,
        name="relay",
    )(got)
    scale = math.sqrt(n_var * wide_x * count_x * wide_r * count_r * n_theta)
    basis = pl.pallas_call(
        lambda *refs: final_kernel(n_var, wide_x, scale, *refs),
        out_shape=jax.ShapeDtypeStruct(cells.shape, jnp.float32),
        in_specs=[VMEM, VMEM],
        out_specs=VMEM,
        scratch_shapes=[pltpu.VMEM((2 * ROWS, LANES), jnp.float32)],
        compiler_params=PARAMS,
        name="final",
    )(stats, cells)
    return basis.reshape((n_vec, n_var, wide_x, n_theta // count_r, count_r * wide_r))


def solution(mesh):
    placed = (
        P(None, None, "gx", "row", None),
        P(None, "gx", "row"),
        P(("gx", "row"), None, None),
        P(),
    )
    return jax.shard_map(
        body,
        mesh=mesh,
        in_specs=placed,
        out_specs=P(None, None, "gx", "row", None),
        check_vma=False,
    )
```

```python
import math

import jax
import jax.numpy as jnp
from jax import lax
from jax.experimental import pallas as pl
from jax.experimental.pallas import tpu as pltpu
from jax.sharding import PartitionSpec as P

STEPS = 2
UNROLL = 2
RIM = 2
LANES = 128
ROWS = 8
RING = 12
HIGH, LOW, SIZE, PANEL = 64, 76, 88, 100


def two_sum(a, b):
    total = a + b
    part = total - a
    return total, (a - (total - part)) + (b - part)


def quick_two_sum(a, b):
    total = a + b
    return total, b - (total - a)


def split(a):
    wide = a * 4097.0
    high = wide - (wide - a)
    return high, a - high


def two_prod(a, b):
    product = a * b
    a_high, a_low = split(a)
    b_high, b_low = split(b)
    return product, ((a_high * b_high - product) + a_high * b_low + a_low * b_high) + a_low * b_low


def pair_add(a, b):
    high, low = two_sum(a[0], b[0])
    return quick_two_sum(high, low + (a[1] + b[1]))


def pair_mul(a, b):
    high, low = two_prod(a[0], b[0])
    return quick_two_sum(high, low + (a[0] * b[1] + a[1] * b[0]))


def pair_scale(a, factor):
    high, low = two_prod(a[0], factor)
    return quick_two_sum(high, low + a[1] * factor)


def pair_roll(a, shift, axis):
    size = a[0].shape[axis]
    return tuple(pltpu.roll(part, shift % size, axis) for part in a)


def pair_tree(pairs):
    while len(pairs) > 1:
        rest = [pairs[-1]] if len(pairs) % 2 else []
        pairs = [pair_add(pairs[i], pairs[i + 1]) for i in range(0, len(pairs) - 1, 2)] + rest
    return pairs[0]


def tree(parts, join):
    while len(parts) > 1:
        rest = [parts[-1]] if len(parts) % 2 else []
        parts = [join(parts[i], parts[i + 1]) for i in range(0, len(parts) - 1, 2)] + rest
    return parts[0]


def lanes_of(shape):
    return lax.broadcasted_iota(jnp.int32, shape, 1)


def roll_lanes(value, shift):
    return pltpu.roll(value, shift % LANES, 1)


def safe_inverse(value):
    positive = value > 0
    return jnp.where(positive, 1.0 / jnp.where(positive, value, 1.0), 0.0)


def merge(tiles):
    size = tree(tiles, jnp.maximum)
    inverse = safe_inverse(size)
    scaled = []
    for tile in tiles:
        ratio = tile * inverse
        ratio = roll_lanes(ratio * ratio, HIGH - SIZE)
        scaled.append(pair_scale((tile, roll_lanes(tile, HIGH - LOW)), ratio))
    return pair_tree(scaled), size, tree(tiles, jnp.add)


def placed_at(lane, start, width, value, other):
    return jnp.where((lane >= start) & (lane < start + width), value, other)


def pack_stats(pair, size, panel):
    lane = lanes_of(size.shape)
    tile = placed_at(lane, HIGH, RING, pair[0], 0.0)
    tile = placed_at(lane, LOW, RING, roll_lanes(pair[1], LOW - HIGH), tile)
    tile = placed_at(lane, SIZE, RING, size, tile)
    return jnp.where(lane >= PANEL, panel, tile)


def march_kernel(
    n_var, wide_x, wide_r, count_x,
    place_ref, mid_ref, mate_ref, far_ref, panel_ref,
    out_ref, now_ref, next_ref, coeff_ref, packed_ref, parts_ref,
):
    n_plane = mid_ref.shape[0] - 1
    n_theta = mid_ref.shape[-1]
    n_tile = n_theta // ROWS
    deep = wide_r + 2 * RIM
    n_pair = n_var * n_var
    used = (wide_x + 2 * RIM) * deep

    mate_is_low = jnp.full((RIM * deep, n_theta), place_ref[0] % 2, jnp.int32) == 1

    def turn(plane):
        mate, far = mate_ref[plane], far_ref[plane]
        low = jnp.where(mate_is_low, mate, far)
        high = jnp.where(mate_is_low, far, mate)
        blank = jnp.zeros((LANES - used, n_theta), jnp.float32)
        return jnp.concatenate([low, mid_ref[plane], high, blank], axis=0).T

    for plane in range(n_plane):
        turned = turn(plane)
        now_ref[plane, ROWS : ROWS + n_theta, :] = turned
        now_ref[plane, ROWS - 1 : ROWS, :] = turned[n_theta - 1 :]
        now_ref[plane, ROWS + n_theta : ROWS + n_theta + 1, :] = turned[:1]
    coeff_ref[:n_theta, :] = turn(n_plane)
    viscous = coeff_ref[4 * n_pair : 4 * n_pair + 1, :]
    for i in range(n_var):
        own = 3 * n_pair + i * n_var + i
        coeff_ref[own : own + 1, :] = coeff_ref[own : own + 1, :] + (1.0 - 6.0 * viscous)
    for n, shift in enumerate((deep, -deep, 1, -1)):
        coeff_ref[n_theta + n : n_theta + n + 1, :] = roll_lanes(viscous, shift)

    lane = lanes_of((ROWS, LANES))
    at_x = lane // deep - RIM + place_ref[0] * wide_x
    inside = (at_x >= 0) & (at_x < wide_x * count_x) & (lane < used)
    first = place_ref[1] == 0
    from_above = ~((lane % deep == 2 * RIM - 1) & first)
    from_below = ~((lane % deep == 2 * RIM) & first)

    def coeff(index):
        return coeff_ref[index : index + 1, :]

    def advance(source_ref, tile):
        start = ROWS + tile * ROWS
        centre = [source_ref[b, pl.ds(start, ROWS), :] for b in range(n_plane)]
        before = [source_ref[b, pl.ds(start - 1, ROWS), :] for b in range(n_plane)]
        after = [source_ref[b, pl.ds(start + 1, ROWS), :] for b in range(n_plane)]
        differ = [a - b for a, b in zip(after, before)]
        both = [a + b for a, b in zip(after, before)]
        result = [None] * n_plane
        for i in range(n_var):
            for k in range(0, n_plane, n_var):
                def flux(start, values):
                    return tree([coeff(start + j * n_var + i) * values[k + j] for j in range(n_var)], jnp.add)

                own = centre[k + i]
                stream = flux(0, centre)
                radial = flux(n_pair, centre)
                local = flux(2 * n_pair, differ) + flux(3 * n_pair, centre)
                local = local + coeff(4 * n_pair) * both[k + i]
                above = roll_lanes(coeff(n_theta + 2) * own + radial, -1)
                below = roll_lanes(coeff(n_theta + 3) * own - radial, 1)
                local = local + roll_lanes(coeff(n_theta) * own + stream, -deep)
                local = local + roll_lanes(coeff(n_theta + 1) * own - stream, deep)
                local = local + jnp.where(from_above, above, 0.0) + jnp.where(from_below, below, 0.0)
                result[k + i] = local
        return result

    def first_step(tile, carry):
        result = advance(now_ref, tile)
        for b in range(n_plane):
            next_ref[b, pl.ds(ROWS + tile * ROWS, ROWS), :] = jnp.where(inside, result[b], 0.0)
        return carry

    lax.fori_loop(0, n_tile, first_step, 0, unroll=UNROLL)
    for b in range(n_plane):
        next_ref[b, ROWS - 1 : ROWS, :] = next_ref[b, ROWS + n_theta - 1 : ROWS + n_theta, :]
        next_ref[b, ROWS + n_theta : ROWS + n_theta + 1, :] = next_ref[b, ROWS : ROWS + 1, :]

    group = wide_x * wide_r
    per_vreg = LANES // group
    n_wide = packed_ref.shape[-1] // LANES

    def second_step(tile, largest):
        result = advance(next_ref, tile)
        for v in range(n_wide):
            packed = jnp.zeros((ROWS, LANES), jnp.float32)
            for b in range(v * per_vreg, min((v + 1) * per_vreg, n_plane)):
                for x in range(wide_x):
                    target = (b % per_vreg) * group + x * wide_r
                    shift = target - ((x + RIM) * deep + RIM)
                    packed = placed_at(lane, target, wide_r, roll_lanes(result[b], shift), packed)
            packed_ref[tile, :, v * LANES : (v + 1) * LANES] = packed
            largest = jnp.maximum(largest, jnp.abs(packed))
        return largest

    largest = lax.fori_loop(0, n_tile, second_step, jnp.zeros((ROWS, LANES), jnp.float32), unroll=UNROLL)
    largest = jnp.max(largest, axis=1, keepdims=True)
    largest = jnp.max(largest, axis=0, keepdims=True)
    inverse = safe_inverse(jnp.broadcast_to(largest, (ROWS, LANES)))
    largest = jnp.broadcast_to(largest, (ROWS, LANES))

    for tile in range(n_tile):
        for v in range(n_wide):
            high, low = split(packed_ref[tile, :, v * LANES : (v + 1) * LANES] * inverse)
            parts_ref[0, tile, v] = high
            parts_ref[1, tile, v] = low

    def shifted(part, tile, v, s):
        whole, rest = divmod(s, per_vreg)
        value = parts_ref[part, tile, (v + whole) % n_wide]
        if not rest:
            return value
        other = parts_ref[part, tile, (v + whole + 1) % n_wide]
        keep = lane < LANES - rest * group
        return jnp.where(keep, roll_lanes(value, -rest * group), roll_lanes(other, -rest * group))

    pairs = [[None] * n_wide for _ in range(ROWS)]
    zero = jnp.zeros((ROWS, LANES), jnp.float32)
    for s in range(RING // 2 + 1):
        for v in range(n_wide):
            total, error = zero, zero
            for tile in range(n_tile):
                a_high, a_low = parts_ref[0, tile, v], parts_ref[1, tile, v]
                if s:
                    b_high, b_low = shifted(0, tile, v, s), shifted(1, tile, v, s)
                    minor = a_high * b_low + a_low * b_high
                else:
                    b_high, b_low = a_high, a_low
                    minor = 2.0 * a_high * a_low
                total, lost = two_sum(total, a_high * b_high)
                error = error + (lost + (minor + a_low * b_low))
            pairs[s][v] = quick_two_sum(total, error)
    row = lax.broadcasted_iota(jnp.int32, (ROWS, LANES), 0)
    sums = []
    for v in range(n_wide):
        level = [pairs[s][v] if s <= RING // 2 else (zero, zero) for s in range(ROWS)]
        half = ROWS // 2
        while half:
            joined = []
            for s in range(half):
                a, b = level[s], level[s + half]
                front = (row // half) % 2 == 0
                a_turned, b_turned = pair_roll(a, -half, 0), pair_roll(b, half, 0)
                one = tuple(jnp.where(front, p, q) for p, q in zip(a, b_turned))
                two = tuple(jnp.where(front, p, q) for p, q in zip(a_turned, b))
                joined.append(pair_add(one, two))
            level = joined
            half //= 2
        sums.append(level[0])
    step = group // 2
    while step:
        sums = [pair_add(a, pair_roll(a, -step, 1)) for a in sums]
        step //= 2
    gathered = (zero, zero)
    for b in range(RING):
        turned = pair_roll(sums[b // per_vreg], HIGH + b - (b % per_vreg) * group, 1)
        gathered = tuple(jnp.where(lane == HIGH + b, p, q) for p, q in zip(turned, gathered))
    stats = pack_stats(gathered, largest, panel_ref[...])
    last = (n_wide - 1) * LANES
    for tile in range(n_tile):
        out_ref[tile, :, :last] = packed_ref[tile, :, :last]
        out_ref[tile, :, last:] = jnp.where(lane < HIGH, packed_ref[tile, :, last:], stats)


def reduce_kernel(got_ref, out_ref):
    count, _, wide = got_ref.shape
    pair, size, panel = merge([got_ref[n, :, wide - LANES :] for n in range(count)])
    tile = pack_stats(pair, size, panel)
    for n in range(out_ref.shape[0]):
        out_ref[n] = tile


def relay_kernel(n_plane, wide_x, wide_r, got_ref, out_ref):
    count = got_ref.shape[0]
    per_vreg = LANES // wide_r
    lane = lanes_of((ROWS, LANES))
    for g in range(n_plane * wide_x):
        v, slot = divmod(g, per_vreg)
        halves = []
        for half in range(count // per_vreg):
            value = jnp.zeros((ROWS, LANES), jnp.float32)
            for n in range(per_vreg):
                source = got_ref[half * per_vreg + n, :, v * LANES : (v + 1) * LANES]
                turned = roll_lanes(source, (n - slot) * wide_r)
                value = placed_at(lane, n * wide_r, wide_r, turned, value)
            halves.append(value)
        whole = jnp.concatenate(halves, axis=1)
        out_ref[g] = pltpu.roll(whole, whole.shape[1] - RIM, 1)


def final_kernel(n_var, wide_x, scale, got_ref, cells_ref, out_ref, weight_ref):
    n_plane = 2 * n_var
    tiles = [got_ref[n] for n in range(got_ref.shape[0])]
    pair, size, tile = merge(tiles)
    lane = lanes_of((ROWS, LANES))
    row = lax.broadcasted_iota(jnp.int32, (ROWS, LANES), 0)
    live = row < n_var
    one = jnp.where(live & (lane < n_plane), roll_lanes(tile, -PANEL), 0.0)
    two = jnp.where(live & (lane < n_plane), roll_lanes(tile, -PANEL - n_plane), 0.0)
    left = one + roll_lanes(one, RING) + roll_lanes(two, 2 * RING)
    right = one + roll_lanes(two, RING) + roll_lanes(two, 2 * RING)
    inner = []
    for part in pair:
        at = jnp.where(lane < RING, roll_lanes(part, -HIGH), 0.0)
        inner.append(at + roll_lanes(at, RING) + roll_lanes(at, 2 * RING))
    place = lane % RING

    def turned(value, s):
        if not s:
            return value
        return jnp.where(place < RING - s, roll_lanes(value, -s), roll_lanes(value, RING - s))

    terms = []
    for s in range(RING // 2 + 1):
        left_s, right_s = turned(left, s), turned(right, s)
        term = pair_add(two_prod(left, right_s), two_prod(left_s, right))
        share = 1.0 if s % (RING // 2) else 0.5
        row_s = tuple(share * part[s : s + 1, :] for part in inner)
        terms.append(pair_mul(term, row_s))
    total = pair_tree(terms)
    for shift in (4, 2, 1):
        total = pair_add(total, pair_roll(total, shift, 0))
    total = pair_add(total, pair_roll(total, -RING // 2, 1))
    total = pair_add(total, pair_roll(total, -RING // 4, 1))
    total = pair_tree([total, pair_roll(total, -1, 1), pair_roll(total, -2, 1)])

    def everywhere(part, at):
        return jnp.broadcast_to(part[:, at : at + 1], (ROWS, LANES))

    square, cross, other = (
        tuple(everywhere(part, g * RING) for part in total) for g in range(3)
    )
    ratio = cross[0] / square[0]
    left_over = pair_add(cross, tuple(-p for p in pair_scale(square, ratio)))
    ratio = quick_two_sum(ratio, left_over[0] / square[0])
    rest = pair_add(other, tuple(-p for p in pair_mul(cross, ratio)))
    largest = everywhere(size, SIZE)
    inv_one = scale / jnp.sqrt(square[0]) / largest
    inv_two = scale / jnp.sqrt(rest[0]) / largest
    weight_ref[:ROWS, :] = inv_one * one
    weight_ref[ROWS:, :] = inv_two * two - (inv_two * ratio[0]) * one

    for a in range(n_plane):
        at = (a // n_var) * ROWS + a % n_var
        weights = jnp.broadcast_to(weight_ref[at : at + 1, :], (ROWS, LANES))
        spread = [everywhere(weights, b) for b in range(n_plane)]
        for x in range(wide_x):
            for h in range(cells_ref.shape[-1] // LANES):
                cut = slice(h * LANES, (h + 1) * LANES)
                value = spread[0] * cells_ref[x, :, cut]
                for b in range(1, n_plane):
                    value = value + spread[b] * cells_ref[b * wide_x + x, :, cut]
                out_ref[a * wide_x + x, :, cut] = value


VMEM = pl.BlockSpec(memory_space=pltpu.VMEM)
PARAMS = pltpu.CompilerParams(vmem_limit_bytes=32 * 1024 * 1024)


def body(test_vectors, base_coeffs, panel_set, owner_index):
    count_x = lax.axis_size("gx")
    count_r = lax.axis_size("row")
    n_vec, n_var, wide_x, wide_r, n_theta = test_vectors.shape
    n_coeff = base_coeffs.shape[0]
    n_plane = n_vec * n_var
    at_x, at_r = lax.axis_index("gx"), lax.axis_index("row")

    panel = panel_set[0] / jnp.max(jnp.abs(panel_set[0]))
    panel = jnp.where(at_x * count_r + at_r == owner_index[0], panel, 0.0)
    panel = jnp.concatenate([panel[:n_var], panel[n_var:]], axis=1)
    panel = jnp.pad(panel, ((0, ROWS - n_var), (PANEL, LANES - PANEL - 2 * n_plane)))

    field = test_vectors.reshape((n_plane, wide_x, wide_r, n_theta))
    turned = base_coeffs.transpose(1, 2, 0)
    turned = jnp.pad(turned, ((0, 0), (0, 0), (0, n_theta - n_coeff)))
    ring = [(i, (i + 1) % count_r) for i in range(count_r)]
    edge = jnp.concatenate([field[:, :, -2 * RIM :], turned[None, :, -2 * RIM :]], axis=0)
    edge = lax.ppermute(edge, "row", ring)
    both = jnp.concatenate([field, turned[None]], axis=0)
    both = jnp.concatenate([edge, both], axis=2)
    both = both.reshape((n_plane + 1, wide_x * (wide_r + 2 * RIM), n_theta))
    outer = [(i, i + 1 if i % 2 else i - 1) for i in range(1, count_x - 1)]
    far = lax.ppermute(both, "gx", outer)
    mate = lax.ppermute(both, "gx", [(i, i ^ 1) for i in range(count_x)])

    n_wide = 3
    n_tile = n_theta // ROWS
    sent = pl.pallas_call(
        lambda *refs: march_kernel(n_var, wide_x, wide_r, count_x, *refs),
        out_shape=jax.ShapeDtypeStruct((n_tile, ROWS, n_wide * LANES), jnp.float32),
        in_specs=[pl.BlockSpec(memory_space=pltpu.SMEM)] + [VMEM] * 4,
        out_specs=VMEM,
        scratch_shapes=[
            pltpu.VMEM((n_plane, n_theta + 2 * ROWS, LANES), jnp.float32),
            pltpu.VMEM((n_plane, n_theta + 2 * ROWS, LANES), jnp.float32),
            pltpu.VMEM((n_theta + ROWS, LANES), jnp.float32),
            pltpu.VMEM((n_tile, ROWS, n_wide * LANES), jnp.float32),
            pltpu.VMEM((2, n_tile, n_wide, ROWS, LANES), jnp.float32),
        ],
        compiler_params=PARAMS,
        name="march",
    )(jnp.stack([at_x, at_r]), both, mate, far, panel)
    got = lax.all_to_all(sent, "row", 0, 0, tiled=True)
    stats = pl.pallas_call(
        reduce_kernel,
        out_shape=jax.ShapeDtypeStruct((count_x, ROWS, LANES), jnp.float32),
        in_specs=[VMEM],
        out_specs=VMEM,
        compiler_params=PARAMS,
        name="reduce",
    )(got)
    stats = lax.all_to_all(stats, "gx", 0, 0, tiled=True)
    cells = pl.pallas_call(
        lambda *refs: relay_kernel(n_plane, wide_x, wide_r, *refs),
        out_shape=jax.ShapeDtypeStruct((n_plane * wide_x, ROWS, count_r * wide_r), jnp.float32),
        in_specs=[VMEM],
        out_specs=VMEM,
        compiler_params=PARAMS,
        name="relay",
    )(got)
    scale = math.sqrt(n_var * wide_x * count_x * wide_r * count_r * n_theta)
    basis = pl.pallas_call(
        lambda *refs: final_kernel(n_var, wide_x, scale, *refs),
        out_shape=jax.ShapeDtypeStruct(cells.shape, jnp.float32),
        in_specs=[VMEM, VMEM],
        out_specs=VMEM,
        scratch_shapes=[pltpu.VMEM((2 * ROWS, LANES), jnp.float32)],
        compiler_params=PARAMS,
        name="final",
    )(stats, cells)
    return basis.reshape((n_vec, n_var, wide_x, n_theta // count_r, count_r * wide_r))


def solution(mesh):
    placed = (
        P(None, None, "gx", "row", None),
        P(None, "gx", "row"),
        P(("gx", "row"), None, None),
        P(),
    )
    return jax.shard_map(
        body,
        mesh=mesh,
        in_specs=placed,
        out_specs=P(None, None, "gx", "row", None),
        check_vma=False,
    )
```

```python
import math

import jax
import jax.numpy as jnp
from jax import lax
from jax.experimental import pallas as pl
from jax.experimental.pallas import tpu as pltpu
from jax.sharding import PartitionSpec as P

STEPS = 2
UNROLL = 2
RIM = 2
LANES = 128
ROWS = 8
RING = 12
HIGH, LOW, SIZE, PANEL = 64, 76, 88, 100


def two_sum(a, b):
    total = a + b
    part = total - a
    return total, (a - (total - part)) + (b - part)


def quick_two_sum(a, b):
    total = a + b
    return total, b - (total - a)


def split(a):
    wide = a * 4097.0
    high = wide - (wide - a)
    return high, a - high


def two_prod(a, b):
    product = a * b
    a_high, a_low = split(a)
    b_high, b_low = split(b)
    return product, ((a_high * b_high - product) + a_high * b_low + a_low * b_high) + a_low * b_low


def pair_add(a, b):
    high, low = two_sum(a[0], b[0])
    return quick_two_sum(high, low + (a[1] + b[1]))


def pair_mul(a, b):
    high, low = two_prod(a[0], b[0])
    return quick_two_sum(high, low + (a[0] * b[1] + a[1] * b[0]))


def pair_scale(a, factor):
    high, low = two_prod(a[0], factor)
    return quick_two_sum(high, low + a[1] * factor)


def pair_roll(a, shift, axis):
    size = a[0].shape[axis]
    return tuple(pltpu.roll(part, shift % size, axis) for part in a)


def pair_tree(pairs):
    while len(pairs) > 1:
        rest = [pairs[-1]] if len(pairs) % 2 else []
        pairs = [pair_add(pairs[i], pairs[i + 1]) for i in range(0, len(pairs) - 1, 2)] + rest
    return pairs[0]


def tree(parts, join):
    while len(parts) > 1:
        rest = [parts[-1]] if len(parts) % 2 else []
        parts = [join(parts[i], parts[i + 1]) for i in range(0, len(parts) - 1, 2)] + rest
    return parts[0]


def lanes_of(shape):
    return lax.broadcasted_iota(jnp.int32, shape, 1)


def roll_lanes(value, shift):
    return pltpu.roll(value, shift % LANES, 1)


def safe_inverse(value):
    positive = value > 0
    return jnp.where(positive, 1.0 / jnp.where(positive, value, 1.0), 0.0)


def merge(tiles):
    size = tree(tiles, jnp.maximum)
    inverse = safe_inverse(size)
    scaled = []
    for tile in tiles:
        ratio = tile * inverse
        ratio = roll_lanes(ratio * ratio, HIGH - SIZE)
        scaled.append(pair_scale((tile, roll_lanes(tile, HIGH - LOW)), ratio))
    return pair_tree(scaled), size, tree(tiles, jnp.add)


def placed_at(lane, start, width, value, other):
    return jnp.where((lane >= start) & (lane < start + width), value, other)


def pack_stats(pair, size, panel):
    lane = lanes_of(size.shape)
    tile = placed_at(lane, HIGH, RING, pair[0], 0.0)
    tile = placed_at(lane, LOW, RING, roll_lanes(pair[1], LOW - HIGH), tile)
    tile = placed_at(lane, SIZE, RING, size, tile)
    return jnp.where(lane >= PANEL, panel, tile)


def march_kernel(
    n_var, wide_x, wide_r, count_x,
    place_ref, mid_ref, mate_ref, far_ref, panel_ref,
    out_ref, now_ref, next_ref, coeff_ref, packed_ref, parts_ref,
):
    n_plane = mid_ref.shape[0] - 1
    n_theta = mid_ref.shape[-1]
    n_tile = n_theta // ROWS
    deep = wide_r + 2 * RIM
    n_pair = n_var * n_var
    used = (wide_x + 2 * RIM) * deep

    mate_is_low = jnp.full((RIM * deep, n_theta), place_ref[0] % 2, jnp.int32) == 1

    def turn(plane):
        mate, far = mate_ref[plane], far_ref[plane]
        low = jnp.where(mate_is_low, mate, far)
        high = jnp.where(mate_is_low, far, mate)
        blank = jnp.zeros((LANES - used, n_theta), jnp.float32)
        return jnp.concatenate([low, mid_ref[plane], high, blank], axis=0).T

    for plane in range(n_plane):
        turned = turn(plane)
        now_ref[plane, ROWS : ROWS + n_theta, :] = turned
        now_ref[plane, ROWS - 1 : ROWS, :] = turned[n_theta - 1 :]
        now_ref[plane, ROWS + n_theta : ROWS + n_theta + 1, :] = turned[:1]
    coeff_ref[:n_theta, :] = turn(n_plane)
    viscous = coeff_ref[4 * n_pair : 4 * n_pair + 1, :]
    for i in range(n_var):
        own = 3 * n_pair + i * n_var + i
        coeff_ref[own : own + 1, :] = coeff_ref[own : own + 1, :] + (1.0 - 6.0 * viscous)
    for n, shift in enumerate((deep, -deep, 1, -1)):
        coeff_ref[n_theta + n : n_theta + n + 1, :] = roll_lanes(viscous, shift)

    lane = lanes_of((ROWS, LANES))
    at_x = lane // deep - RIM + place_ref[0] * wide_x
    inside = (at_x >= 0) & (at_x < wide_x * count_x) & (lane < used)
    first = place_ref[1] == 0
    from_above = ~((lane % deep == 2 * RIM - 1) & first)
    from_below = ~((lane % deep == 2 * RIM) & first)

    def coeff(index):
        return coeff_ref[index : index + 1, :]

    def advance(source_ref, tile):
        start = ROWS + tile * ROWS
        centre = [source_ref[b, pl.ds(start, ROWS), :] for b in range(n_plane)]
        before = [source_ref[b, pl.ds(start - 1, ROWS), :] for b in range(n_plane)]
        after = [source_ref[b, pl.ds(start + 1, ROWS), :] for b in range(n_plane)]
        differ = [a - b for a, b in zip(after, before)]
        both = [a + b for a, b in zip(after, before)]
        result = [None] * n_plane
        for i in range(n_var):
            for k in range(0, n_plane, n_var):
                def flux(start, values):
                    return tree([coeff(start + j * n_var + i) * values[k + j] for j in range(n_var)], jnp.add)

                own = centre[k + i]
                stream = flux(0, centre)
                radial = flux(n_pair, centre)
                local = flux(2 * n_pair, differ) + flux(3 * n_pair, centre)
                local = local + coeff(4 * n_pair) * both[k + i]
                above = roll_lanes(coeff(n_theta + 2) * own + radial, -1)
                below = roll_lanes(coeff(n_theta + 3) * own - radial, 1)
                local = local + roll_lanes(coeff(n_theta) * own + stream, -deep)
                local = local + roll_lanes(coeff(n_theta + 1) * own - stream, deep)
                local = local + jnp.where(from_above, above, 0.0) + jnp.where(from_below, below, 0.0)
                result[k + i] = local
        return result

    def first_step(tile, carry):
        result = advance(now_ref, tile)
        for b in range(n_plane):
            next_ref[b, pl.ds(ROWS + tile * ROWS, ROWS), :] = jnp.where(inside, result[b], 0.0)
        return carry

    lax.fori_loop(0, n_tile, first_step, 0, unroll=UNROLL)
    for b in range(n_plane):
        next_ref[b, ROWS - 1 : ROWS, :] = next_ref[b, ROWS + n_theta - 1 : ROWS + n_theta, :]
        next_ref[b, ROWS + n_theta : ROWS + n_theta + 1, :] = next_ref[b, ROWS : ROWS + 1, :]

    group = wide_x * wide_r
    per_vreg = LANES // group
    n_wide = packed_ref.shape[-1] // LANES
    mine = []
    for x in range(wide_x):
        start = (x + RIM) * deep + RIM
        mine.append((lane >= start) & (lane < start + wide_r))

    def second_step(tile, largest):
        result = advance(next_ref, tile)
        for v in range(n_wide):
            pieces = []
            for b in range(v * per_vreg, min((v + 1) * per_vreg, n_plane)):
                for x in range(wide_x):
                    shift = (b % per_vreg) * group + x * wide_r - ((x + RIM) * deep + RIM)
                    pieces.append(roll_lanes(jnp.where(mine[x], result[b], 0.0), shift))
            packed = tree(pieces, jnp.add)
            packed_ref[tile, :, v * LANES : (v + 1) * LANES] = packed
            largest = jnp.maximum(largest, jnp.abs(packed))
        return largest

    largest = lax.fori_loop(0, n_tile, second_step, jnp.zeros((ROWS, LANES), jnp.float32), unroll=UNROLL)
    largest = jnp.max(largest, axis=1, keepdims=True)
    largest = jnp.max(largest, axis=0, keepdims=True)
    inverse = safe_inverse(jnp.broadcast_to(largest, (ROWS, LANES)))
    largest = jnp.broadcast_to(largest, (ROWS, LANES))

    for tile in range(n_tile):
        for v in range(n_wide):
            high, low = split(packed_ref[tile, :, v * LANES : (v + 1) * LANES] * inverse)
            parts_ref[0, tile, v] = high
            parts_ref[1, tile, v] = low

    def shifted(part, tile, v, s):
        whole, rest = divmod(s, per_vreg)
        value = parts_ref[part, tile, (v + whole) % n_wide]
        if not rest:
            return value
        other = parts_ref[part, tile, (v + whole + 1) % n_wide]
        keep = lane < LANES - rest * group
        return jnp.where(keep, roll_lanes(value, -rest * group), roll_lanes(other, -rest * group))

    zero = jnp.zeros((ROWS, LANES), jnp.float32)
    pairs = [[(zero, zero)] * n_wide for _ in range(ROWS)]
    for s in range(RING // 2 + 1):
        for v in range(n_wide):
            if 2 * s == RING and v * per_vreg + s >= n_plane:
                continue
            total, error = zero, zero
            for tile in range(n_tile):
                a_high, a_low = parts_ref[0, tile, v], parts_ref[1, tile, v]
                if s:
                    b_high, b_low = shifted(0, tile, v, s), shifted(1, tile, v, s)
                    minor = a_high * b_low + a_low * b_high
                else:
                    b_high, b_low = a_high, a_low
                    minor = 2.0 * a_high * a_low
                total, lost = two_sum(total, a_high * b_high)
                error = error + (lost + (minor + a_low * b_low))
            pairs[s][v] = quick_two_sum(total, error)
    row = lax.broadcasted_iota(jnp.int32, (ROWS, LANES), 0)
    sums = []
    for v in range(n_wide):
        level = [pairs[s][v] for s in range(ROWS)]
        half = ROWS // 2
        while half:
            joined = []
            for s in range(half):
                a, b = level[s], level[s + half]
                front = (row // half) % 2 == 0
                a_turned, b_turned = pair_roll(a, -half, 0), pair_roll(b, half, 0)
                one = tuple(jnp.where(front, p, q) for p, q in zip(a, b_turned))
                two = tuple(jnp.where(front, p, q) for p, q in zip(a_turned, b))
                joined.append(pair_add(one, two))
            level = joined
            half //= 2
        sums.append(level[0])
    step = group // 2
    while step:
        sums = [pair_add(a, pair_roll(a, -step, 1)) for a in sums]
        step //= 2
    gathered = (zero, zero)
    for b in range(RING):
        turned = pair_roll(sums[b // per_vreg], HIGH + b - (b % per_vreg) * group, 1)
        gathered = tuple(jnp.where(lane == HIGH + b, p, q) for p, q in zip(turned, gathered))
    stats = pack_stats(gathered, largest, panel_ref[...])
    last = (n_wide - 1) * LANES
    for tile in range(n_tile):
        out_ref[tile, :, :last] = packed_ref[tile, :, :last]
        out_ref[tile, :, last:] = jnp.where(lane < HIGH, packed_ref[tile, :, last:], stats)


def prepare_kernel(field_ref, coeff_ref, edge_ref, turned_ref):
    n_plane, _, wide_r, _ = field_ref.shape
    n_coeff = coeff_ref.shape[-1]
    start = wide_r - edge_ref.shape[2]
    edge_ref[:n_plane] = field_ref[:, :, start:, :]
    turned_ref[...] = jnp.zeros_like(turned_ref)
    turned_ref[:, :, :n_coeff] = coeff_ref[...]
    edge_ref[n_plane] = turned_ref[:, start:, :]


def reduce_kernel(got_ref, out_ref):
    count, _, wide = got_ref.shape
    pair, size, panel = merge([got_ref[n, :, wide - LANES :] for n in range(count)])
    tile = pack_stats(pair, size, panel)
    for n in range(out_ref.shape[0]):
        out_ref[n] = tile


def relay_kernel(n_plane, wide_x, wide_r, got_ref, out_ref):
    count = got_ref.shape[0]
    per_vreg = LANES // wide_r
    lane = lanes_of((ROWS, LANES))
    for g in range(n_plane * wide_x):
        v, slot = divmod(g, per_vreg)
        halves = []
        for half in range(count // per_vreg):
            value = jnp.zeros((ROWS, LANES), jnp.float32)
            for n in range(per_vreg):
                source = got_ref[half * per_vreg + n, :, v * LANES : (v + 1) * LANES]
                turned = roll_lanes(source, (n - slot) * wide_r)
                value = placed_at(lane, n * wide_r, wide_r, turned, value)
            halves.append(value)
        whole = jnp.concatenate(halves, axis=1)
        out_ref[g] = pltpu.roll(whole, whole.shape[1] - RIM, 1)


def final_kernel(n_var, wide_x, scale, got_ref, cells_ref, out_ref, weight_ref):
    n_plane = 2 * n_var
    tiles = [got_ref[n] for n in range(got_ref.shape[0])]
    pair, size, tile = merge(tiles)
    lane = lanes_of((ROWS, LANES))
    row = lax.broadcasted_iota(jnp.int32, (ROWS, LANES), 0)
    live = row < n_var
    one = jnp.where(live & (lane < n_plane), roll_lanes(tile, -PANEL), 0.0)
    two = jnp.where(live & (lane < n_plane), roll_lanes(tile, -PANEL - n_plane), 0.0)
    left = one + roll_lanes(one, RING) + roll_lanes(two, 2 * RING)
    right = one + roll_lanes(two, RING) + roll_lanes(two, 2 * RING)
    inner = []
    for part in pair:
        at = jnp.where(lane < RING, roll_lanes(part, -HIGH), 0.0)
        inner.append(at + roll_lanes(at, RING) + roll_lanes(at, 2 * RING))
    place = lane % RING

    def turned(value, s):
        if not s:
            return value
        return jnp.where(place < RING - s, roll_lanes(value, -s), roll_lanes(value, RING - s))

    terms = []
    for s in range(RING // 2 + 1):
        left_s, right_s = turned(left, s), turned(right, s)
        term = pair_add(two_prod(left, right_s), two_prod(left_s, right))
        share = 1.0 if s else 0.5
        row_s = tuple(share * part[s : s + 1, :] for part in inner)
        terms.append(pair_mul(term, row_s))
    total = pair_tree(terms)
    total = pair_tree([pair_roll(total, -b, 1) for b in range(n_plane)])
    for shift in (4, 2, 1):
        total = pair_add(total, pair_roll(total, shift, 0))

    def everywhere(part, at):
        return jnp.broadcast_to(part[:, at : at + 1], (ROWS, LANES))

    square, cross, other = (
        tuple(everywhere(part, g * RING) for part in total) for g in range(3)
    )
    ratio = cross[0] / square[0]
    left_over = pair_add(cross, tuple(-p for p in pair_scale(square, ratio)))
    ratio = quick_two_sum(ratio, left_over[0] / square[0])
    rest = pair_add(other, tuple(-p for p in pair_mul(cross, ratio)))
    largest = everywhere(size, SIZE)
    inv_one = scale / jnp.sqrt(square[0]) / largest
    inv_two = scale / jnp.sqrt(rest[0]) / largest
    weight_ref[:ROWS, :] = inv_one * one
    weight_ref[ROWS:, :] = inv_two * two - (inv_two * ratio[0]) * one

    for a in range(n_plane):
        at = (a // n_var) * ROWS + a % n_var
        weights = jnp.broadcast_to(weight_ref[at : at + 1, :], (ROWS, LANES))
        spread = [everywhere(weights, b) for b in range(n_plane)]
        for x in range(wide_x):
            for h in range(cells_ref.shape[-1] // LANES):
                cut = slice(h * LANES, (h + 1) * LANES)
                value = spread[0] * cells_ref[x, :, cut]
                for b in range(1, n_plane):
                    value = value + spread[b] * cells_ref[b * wide_x + x, :, cut]
                out_ref[a * wide_x + x, :, cut] = value


VMEM = pl.BlockSpec(memory_space=pltpu.VMEM)
PARAMS = pltpu.CompilerParams(vmem_limit_bytes=32 * 1024 * 1024)


def body(test_vectors, base_coeffs, panel_set, owner_index):
    count_x = lax.axis_size("gx")
    count_r = lax.axis_size("row")
    n_vec, n_var, wide_x, wide_r, n_theta = test_vectors.shape
    n_plane = n_vec * n_var
    at_x, at_r = lax.axis_index("gx"), lax.axis_index("row")

    panel = panel_set[0] / jnp.max(jnp.abs(panel_set[0]))
    panel = jnp.where(at_x * count_r + at_r == owner_index[0], panel, 0.0)
    panel = jnp.concatenate([panel[:n_var], panel[n_var:]], axis=1)
    panel = jnp.pad(panel, ((0, ROWS - n_var), (PANEL, LANES - PANEL - 2 * n_plane)))

    field = test_vectors.reshape((n_plane, wide_x, wide_r, n_theta))
    edge, turned = pl.pallas_call(
        prepare_kernel,
        out_shape=(
            jax.ShapeDtypeStruct((n_plane + 1, wide_x, 2 * RIM, n_theta), jnp.float32),
            jax.ShapeDtypeStruct((wide_x, wide_r, n_theta), jnp.float32),
        ),
        in_specs=[VMEM, VMEM],
        out_specs=(VMEM, VMEM),
        compiler_params=PARAMS,
        name="prepare",
    )(field, base_coeffs.transpose(1, 2, 0))
    ring = [(i, (i + 1) % count_r) for i in range(count_r)]
    edge = lax.ppermute(edge, "row", ring)
    both = jnp.concatenate([field, turned[None]], axis=0)
    both = jnp.concatenate([edge, both], axis=2)
    both = both.reshape((n_plane + 1, wide_x * (wide_r + 2 * RIM), n_theta))
    outer = [(i, i + 1 if i % 2 else i - 1) for i in range(1, count_x - 1)]
    far = lax.ppermute(both, "gx", outer)
    mate = lax.ppermute(both, "gx", [(i, i ^ 1) for i in range(count_x)])

    n_wide = 3
    n_tile = n_theta // ROWS
    sent = pl.pallas_call(
        lambda *refs: march_kernel(n_var, wide_x, wide_r, count_x, *refs),
        out_shape=jax.ShapeDtypeStruct((n_tile, ROWS, n_wide * LANES), jnp.float32),
        in_specs=[pl.BlockSpec(memory_space=pltpu.SMEM)] + [VMEM] * 4,
        out_specs=VMEM,
        scratch_shapes=[
            pltpu.VMEM((n_plane, n_theta + 2 * ROWS, LANES), jnp.float32),
            pltpu.VMEM((n_plane, n_theta + 2 * ROWS, LANES), jnp.float32),
            pltpu.VMEM((n_theta + ROWS, LANES), jnp.float32),
            pltpu.VMEM((n_tile, ROWS, n_wide * LANES), jnp.float32),
            pltpu.VMEM((2, n_tile, n_wide, ROWS, LANES), jnp.float32),
        ],
        compiler_params=PARAMS,
        name="march",
    )(jnp.stack([at_x, at_r]), both, mate, far, panel)
    got = lax.all_to_all(sent, "row", 0, 0, tiled=True)
    stats = pl.pallas_call(
        reduce_kernel,
        out_shape=jax.ShapeDtypeStruct((count_x, ROWS, LANES), jnp.float32),
        in_specs=[VMEM],
        out_specs=VMEM,
        compiler_params=PARAMS,
        name="reduce",
    )(got)
    stats = lax.all_to_all(stats, "gx", 0, 0, tiled=True)
    cells = pl.pallas_call(
        lambda *refs: relay_kernel(n_plane, wide_x, wide_r, *refs),
        out_shape=jax.ShapeDtypeStruct((n_plane * wide_x, ROWS, count_r * wide_r), jnp.float32),
        in_specs=[VMEM],
        out_specs=VMEM,
        compiler_params=PARAMS,
        name="relay",
    )(got)
    scale = math.sqrt(n_var * wide_x * count_x * wide_r * count_r * n_theta)
    basis = pl.pallas_call(
        lambda *refs: final_kernel(n_var, wide_x, scale, *refs),
        out_shape=jax.ShapeDtypeStruct(cells.shape, jnp.float32),
        in_specs=[VMEM, VMEM],
        out_specs=VMEM,
        scratch_shapes=[pltpu.VMEM((2 * ROWS, LANES), jnp.float32)],
        compiler_params=PARAMS,
        name="final",
    )(stats, cells)
    return basis.reshape((n_vec, n_var, wide_x, n_theta // count_r, count_r * wide_r))


def solution(mesh):
    placed = (
        P(None, None, "gx", "row", None),
        P(None, "gx", "row"),
        P(("gx", "row"), None, None),
        P(),
    )
    return jax.shard_map(
        body,
        mesh=mesh,
        in_specs=placed,
        out_specs=P(None, None, "gx", "row", None),
        check_vma=False,
    )
```

```python
import math

import jax
import jax.numpy as jnp
from jax import lax
from jax.experimental import pallas as pl
from jax.experimental.pallas import tpu as pltpu
from jax.sharding import PartitionSpec as P

STEPS = 2
UNROLL = 2
RIM = 2
LANES = 128
ROWS = 8
RING = 12
HIGH, LOW, SIZE, PANEL = 64, 76, 88, 100


def two_sum(a, b):
    total = a + b
    part = total - a
    return total, (a - (total - part)) + (b - part)


def quick_two_sum(a, b):
    total = a + b
    return total, b - (total - a)


def split(a):
    wide = a * 4097.0
    high = wide - (wide - a)
    return high, a - high


def two_prod(a, b):
    product = a * b
    a_high, a_low = split(a)
    b_high, b_low = split(b)
    return product, ((a_high * b_high - product) + a_high * b_low + a_low * b_high) + a_low * b_low


def pair_add(a, b):
    high, low = two_sum(a[0], b[0])
    return quick_two_sum(high, low + (a[1] + b[1]))


def pair_mul(a, b):
    high, low = two_prod(a[0], b[0])
    return quick_two_sum(high, low + (a[0] * b[1] + a[1] * b[0]))


def pair_scale(a, factor):
    high, low = two_prod(a[0], factor)
    return quick_two_sum(high, low + a[1] * factor)


def pair_roll(a, shift, axis):
    size = a[0].shape[axis]
    return tuple(pltpu.roll(part, shift % size, axis) for part in a)


def pair_tree(pairs):
    while len(pairs) > 1:
        rest = [pairs[-1]] if len(pairs) % 2 else []
        pairs = [pair_add(pairs[i], pairs[i + 1]) for i in range(0, len(pairs) - 1, 2)] + rest
    return pairs[0]


def tree(parts, join):
    while len(parts) > 1:
        rest = [parts[-1]] if len(parts) % 2 else []
        parts = [join(parts[i], parts[i + 1]) for i in range(0, len(parts) - 1, 2)] + rest
    return parts[0]


def lanes_of(shape):
    return lax.broadcasted_iota(jnp.int32, shape, 1)


def roll_lanes(value, shift):
    return pltpu.roll(value, shift % LANES, 1)


def safe_inverse(value):
    positive = value > 0
    return jnp.where(positive, 1.0 / jnp.where(positive, value, 1.0), 0.0)


def merge(tiles):
    size = tree(tiles, jnp.maximum)
    inverse = safe_inverse(size)
    scaled = []
    for tile in tiles:
        ratio = tile * inverse
        ratio = roll_lanes(ratio * ratio, HIGH - SIZE)
        scaled.append(pair_scale((tile, roll_lanes(tile, HIGH - LOW)), ratio))
    return pair_tree(scaled), size, tree(tiles, jnp.add)


def placed_at(lane, start, width, value, other):
    return jnp.where((lane >= start) & (lane < start + width), value, other)


def pack_stats(pair, size, panel):
    lane = lanes_of(size.shape)
    tile = placed_at(lane, HIGH, RING, pair[0], 0.0)
    tile = placed_at(lane, LOW, RING, roll_lanes(pair[1], LOW - HIGH), tile)
    tile = placed_at(lane, SIZE, RING, size, tile)
    return jnp.where(lane >= PANEL, panel, tile)


def march_kernel(
    n_var, wide_x, wide_r, count_x,
    place_ref, edge_ref, own_ref, mate_edge_ref, mate_ref, far_edge_ref, far_ref, panel_ref,
    out_ref, rows_ref, now_ref, next_ref, coeff_ref, packed_ref, parts_ref,
):
    n_plane = own_ref.shape[0] - 1
    n_theta = own_ref.shape[-1]
    n_tile = n_theta // ROWS
    edge = edge_ref.shape[2]
    deep = wide_r + edge
    n_pair = n_var * n_var
    used = (wide_x + 2 * RIM) * deep

    mate_is_low = place_ref[0] % 2 == 1
    starts = (jnp.where(mate_is_low, 0, RIM + wide_x), jnp.where(mate_is_low, RIM + wide_x, 0))
    places = (
        (RIM, edge_ref, own_ref), (starts[0], mate_edge_ref, mate_ref), (starts[1], far_edge_ref, far_ref)
    )

    def turn(plane):
        for start, rim, inner in places:
            for x in range(wide_x):
                at = (start + x) * deep
                rows_ref[plane, pl.ds(at, edge), :] = rim[plane, x]
                rows_ref[plane, pl.ds(at + edge, wide_r), :] = inner[plane, x]
        rows_ref[plane, used:, :] = jnp.zeros((LANES - used, n_theta), jnp.float32)
        return rows_ref[plane].T

    for plane in range(n_plane):
        turned = turn(plane)
        now_ref[plane, ROWS : ROWS + n_theta, :] = turned
        now_ref[plane, ROWS - 1 : ROWS, :] = turned[n_theta - 1 :]
        now_ref[plane, ROWS + n_theta : ROWS + n_theta + 1, :] = turned[:1]
    coeff_ref[:n_theta, :] = turn(n_plane)
    viscous = coeff_ref[4 * n_pair : 4 * n_pair + 1, :]
    for i in range(n_var):
        own = 3 * n_pair + i * n_var + i
        coeff_ref[own : own + 1, :] = coeff_ref[own : own + 1, :] + (1.0 - 6.0 * viscous)
    for n, shift in enumerate((deep, -deep, 1, -1)):
        coeff_ref[n_theta + n : n_theta + n + 1, :] = roll_lanes(viscous, shift)

    lane = lanes_of((ROWS, LANES))
    at_x = lane // deep - RIM + place_ref[0] * wide_x
    inside = (at_x >= 0) & (at_x < wide_x * count_x) & (lane < used)
    first = place_ref[1] == 0
    from_above = ~((lane % deep == 2 * RIM - 1) & first)
    from_below = ~((lane % deep == 2 * RIM) & first)

    def coeff(index):
        return coeff_ref[index : index + 1, :]

    def advance(source_ref, tile):
        start = ROWS + tile * ROWS
        centre = [source_ref[b, pl.ds(start, ROWS), :] for b in range(n_plane)]
        before = [source_ref[b, pl.ds(start - 1, ROWS), :] for b in range(n_plane)]
        after = [source_ref[b, pl.ds(start + 1, ROWS), :] for b in range(n_plane)]
        differ = [a - b for a, b in zip(after, before)]
        both = [a + b for a, b in zip(after, before)]
        result = [None] * n_plane
        for i in range(n_var):
            for k in range(0, n_plane, n_var):
                def flux(start, values):
                    return tree([coeff(start + j * n_var + i) * values[k + j] for j in range(n_var)], jnp.add)

                own = centre[k + i]
                stream = flux(0, centre)
                radial = flux(n_pair, centre)
                local = flux(2 * n_pair, differ) + flux(3 * n_pair, centre)
                local = local + coeff(4 * n_pair) * both[k + i]
                above = roll_lanes(coeff(n_theta + 2) * own + radial, -1)
                below = roll_lanes(coeff(n_theta + 3) * own - radial, 1)
                local = local + roll_lanes(coeff(n_theta) * own + stream, -deep)
                local = local + roll_lanes(coeff(n_theta + 1) * own - stream, deep)
                local = local + jnp.where(from_above, above, 0.0) + jnp.where(from_below, below, 0.0)
                result[k + i] = local
        return result

    def first_step(tile, carry):
        result = advance(now_ref, tile)
        for b in range(n_plane):
            next_ref[b, pl.ds(ROWS + tile * ROWS, ROWS), :] = jnp.where(inside, result[b], 0.0)
        return carry

    lax.fori_loop(0, n_tile, first_step, 0, unroll=UNROLL)
    for b in range(n_plane):
        next_ref[b, ROWS - 1 : ROWS, :] = next_ref[b, ROWS + n_theta - 1 : ROWS + n_theta, :]
        next_ref[b, ROWS + n_theta : ROWS + n_theta + 1, :] = next_ref[b, ROWS : ROWS + 1, :]

    group = wide_x * wide_r
    per_vreg = LANES // group
    n_wide = packed_ref.shape[-1] // LANES
    at_own = lane - (RIM * deep + RIM)
    mine = (at_own >= 0) & (at_own < wide_x * deep) & (at_own % deep < wide_r)
    head = lane % group < wide_r
    even = lane % (2 * group) < group
    even_tail = (lane + LANES - deep) % (2 * group) < wide_r

    def second_step(tile, largest):
        result = [jnp.where(mine, value, 0.0) for value in advance(next_ref, tile)]
        for v in range(n_wide):
            turned = [
                roll_lanes(result[b], (b % per_vreg) * group - (RIM * deep + RIM))
                for b in range(v * per_vreg, min((v + 1) * per_vreg, n_plane))
            ]
            evens, odds = tree(turned[::2], jnp.add), tree(turned[1::2], jnp.add)
            heads = jnp.where(even, evens, odds)
            tails = jnp.where(even_tail, evens, odds)
            packed = jnp.where(head, heads, roll_lanes(tails, wide_r - deep))
            packed_ref[tile, :, v * LANES : (v + 1) * LANES] = packed
            largest = jnp.maximum(largest, jnp.abs(packed))
        return largest

    largest = lax.fori_loop(0, n_tile, second_step, jnp.zeros((ROWS, LANES), jnp.float32), unroll=UNROLL)
    largest = jnp.max(largest, axis=1, keepdims=True)
    largest = jnp.max(largest, axis=0, keepdims=True)
    inverse = safe_inverse(jnp.broadcast_to(largest, (ROWS, LANES)))
    largest = jnp.broadcast_to(largest, (ROWS, LANES))

    for tile in range(n_tile):
        for v in range(n_wide):
            high, low = split(packed_ref[tile, :, v * LANES : (v + 1) * LANES] * inverse)
            parts_ref[0, tile, v] = high
            parts_ref[1, tile, v] = low

    def shifted(part, tile, v, s):
        whole, rest = divmod(s, per_vreg)
        value = parts_ref[part, tile, (v + whole) % n_wide]
        if not rest:
            return value
        other = parts_ref[part, tile, (v + whole + 1) % n_wide]
        keep = lane < LANES - rest * group
        return jnp.where(keep, roll_lanes(value, -rest * group), roll_lanes(other, -rest * group))

    zero = jnp.zeros((ROWS, LANES), jnp.float32)
    pairs = [[(zero, zero)] * n_wide for _ in range(ROWS)]
    for s in range(RING // 2 + 1):
        for v in range(n_wide):
            if 2 * s == RING and v * per_vreg + s >= n_plane:
                continue
            total, error = zero, zero
            for tile in range(n_tile):
                a_high, a_low = parts_ref[0, tile, v], parts_ref[1, tile, v]
                if s:
                    b_high, b_low = shifted(0, tile, v, s), shifted(1, tile, v, s)
                    minor = a_high * b_low + a_low * b_high
                else:
                    b_high, b_low = a_high, a_low
                    minor = 2.0 * a_high * a_low
                total, lost = two_sum(total, a_high * b_high)
                error = error + (lost + (minor + a_low * b_low))
            pairs[s][v] = quick_two_sum(total, error)
    row = lax.broadcasted_iota(jnp.int32, (ROWS, LANES), 0)
    sums = []
    for v in range(n_wide):
        level = [pairs[s][v] for s in range(ROWS)]
        half = ROWS // 2
        while half:
            joined = []
            for s in range(half):
                a, b = level[s], level[s + half]
                front = (row // half) % 2 == 0
                a_turned, b_turned = pair_roll(a, -half, 0), pair_roll(b, half, 0)
                one = tuple(jnp.where(front, p, q) for p, q in zip(a, b_turned))
                two = tuple(jnp.where(front, p, q) for p, q in zip(a_turned, b))
                joined.append(pair_add(one, two))
            level = joined
            half //= 2
        sums.append(level[0])
    step = group // 2
    while step:
        sums = [pair_add(a, pair_roll(a, -step, 1)) for a in sums]
        step //= 2
    gathered = (zero, zero)
    for b in range(RING):
        turned = pair_roll(sums[b // per_vreg], HIGH + b - (b % per_vreg) * group, 1)
        gathered = tuple(jnp.where(lane == HIGH + b, p, q) for p, q in zip(turned, gathered))
    stats = pack_stats(gathered, largest, panel_ref[...])
    last = (n_wide - 1) * LANES
    for tile in range(n_tile):
        out_ref[tile, :, :last] = packed_ref[tile, :, :last]
        out_ref[tile, :, last:] = jnp.where(lane < HIGH, packed_ref[tile, :, last:], stats)


def reduce_kernel(got_ref, out_ref):
    count, _, wide = got_ref.shape
    pair, size, panel = merge([got_ref[n, :, wide - LANES :] for n in range(count)])
    tile = pack_stats(pair, size, panel)
    for n in range(out_ref.shape[0]):
        out_ref[n] = tile


def relay_kernel(n_plane, wide_x, wide_r, got_ref, out_ref):
    count = got_ref.shape[0]
    per_vreg = LANES // wide_r
    lane = lanes_of((ROWS, LANES))
    for g in range(n_plane * wide_x):
        v, slot = divmod(g, per_vreg)
        halves = []
        for half in range(count // per_vreg):
            value = jnp.zeros((ROWS, LANES), jnp.float32)
            for n in range(per_vreg):
                source = got_ref[half * per_vreg + n, :, v * LANES : (v + 1) * LANES]
                turned = roll_lanes(source, (n - slot) * wide_r)
                value = placed_at(lane, n * wide_r, wide_r, turned, value)
            halves.append(value)
        whole = jnp.concatenate(halves, axis=1)
        out_ref[g] = pltpu.roll(whole, whole.shape[1] - RIM, 1)


def final_kernel(n_var, wide_x, scale, got_ref, cells_ref, out_ref, weight_ref):
    n_plane = 2 * n_var
    tiles = [got_ref[n] for n in range(got_ref.shape[0])]
    pair, size, tile = merge(tiles)
    lane = lanes_of((ROWS, LANES))
    row = lax.broadcasted_iota(jnp.int32, (ROWS, LANES), 0)
    live = row < n_var
    one = jnp.where(live & (lane < n_plane), roll_lanes(tile, -PANEL), 0.0)
    two = jnp.where(live & (lane < n_plane), roll_lanes(tile, -PANEL - n_plane), 0.0)
    left = one + roll_lanes(one, RING) + roll_lanes(two, 2 * RING)
    right = one + roll_lanes(two, RING) + roll_lanes(two, 2 * RING)
    inner = []
    for part in pair:
        at = jnp.where(lane < RING, roll_lanes(part, -HIGH), 0.0)
        inner.append(at + roll_lanes(at, RING) + roll_lanes(at, 2 * RING))
    place = lane % RING

    def turned(value, s):
        if not s:
            return value
        return jnp.where(place < RING - s, roll_lanes(value, -s), roll_lanes(value, RING - s))

    terms = []
    for s in range(RING // 2 + 1):
        left_s, right_s = turned(left, s), turned(right, s)
        term = pair_add(two_prod(left, right_s), two_prod(left_s, right))
        share = 1.0 if s else 0.5
        row_s = tuple(share * part[s : s + 1, :] for part in inner)
        terms.append(pair_mul(term, row_s))
    total = pair_tree(terms)
    total = pair_tree([pair_roll(total, -b, 1) for b in range(n_plane)])
    for shift in (4, 2, 1):
        total = pair_add(total, pair_roll(total, shift, 0))

    def everywhere(part, at):
        return jnp.broadcast_to(part[:, at : at + 1], (ROWS, LANES))

    square, cross, other = (
        tuple(everywhere(part, g * RING) for part in total) for g in range(3)
    )
    ratio = cross[0] / square[0]
    left_over = pair_add(cross, tuple(-p for p in pair_scale(square, ratio)))
    ratio = quick_two_sum(ratio, left_over[0] / square[0])
    rest = pair_add(other, tuple(-p for p in pair_mul(cross, ratio)))
    largest = everywhere(size, SIZE)
    inv_one = scale / jnp.sqrt(square[0]) / largest
    inv_two = scale / jnp.sqrt(rest[0]) / largest
    weight_ref[:ROWS, :] = inv_one * one
    weight_ref[ROWS:, :] = inv_two * two - (inv_two * ratio[0]) * one

    for a in range(n_plane):
        at = (a // n_var) * ROWS + a % n_var
        weights = jnp.broadcast_to(weight_ref[at : at + 1, :], (ROWS, LANES))
        spread = [everywhere(weights, b) for b in range(n_plane)]
        for x in range(wide_x):
            for h in range(cells_ref.shape[-1] // LANES):
                cut = slice(h * LANES, (h + 1) * LANES)
                value = spread[0] * cells_ref[x, :, cut]
                for b in range(1, n_plane):
                    value = value + spread[b] * cells_ref[b * wide_x + x, :, cut]
                out_ref[a * wide_x + x, :, cut] = value


VMEM = pl.BlockSpec(memory_space=pltpu.VMEM)
PARAMS = pltpu.CompilerParams(vmem_limit_bytes=32 * 1024 * 1024)


def body(test_vectors, base_coeffs, panel_set, owner_index):
    count_x = lax.axis_size("gx")
    count_r = lax.axis_size("row")
    n_vec, n_var, wide_x, wide_r, n_theta = test_vectors.shape
    n_plane = n_vec * n_var
    at_x, at_r = lax.axis_index("gx"), lax.axis_index("row")

    panel = panel_set[0] / jnp.max(jnp.abs(panel_set[0]))
    panel = jnp.where(at_x * count_r + at_r == owner_index[0], panel, 0.0)
    panel = jnp.concatenate([panel[:n_var], panel[n_var:]], axis=1)
    panel = jnp.pad(panel, ((0, ROWS - n_var), (PANEL, LANES - PANEL - 2 * n_plane)))

    field = test_vectors.reshape((n_plane, wide_x, wide_r, n_theta))
    def by_cell(coeffs):
        turned = jnp.pad(coeffs.transpose(1, 2, 0), ((0, 0), (0, 0), (0, n_theta - coeffs.shape[0])))
        return turned[None]

    edge = jnp.concatenate([field[:, :, -2 * RIM :], by_cell(base_coeffs[:, :, -2 * RIM :])], axis=0)
    ring = [(i, (i + 1) % count_r) for i in range(count_r)]
    outer = [(i, i + 1 if i % 2 else i - 1) for i in range(1, count_x - 1)]
    inner = [(i, i ^ 1) for i in range(count_x)]
    sent_edge = edge
    edge = lax.ppermute(edge, "row", ring)
    _, coeffs = lax.optimization_barrier((sent_edge, base_coeffs))
    own = jnp.concatenate([field, by_cell(coeffs)], axis=0)
    far = lax.ppermute(own, "gx", outer)
    mate = lax.ppermute(own, "gx", inner)
    far_edge = lax.ppermute(edge, "gx", outer)
    mate_edge = lax.ppermute(edge, "gx", inner)
    n_wide = 3
    n_tile = n_theta // ROWS
    sent = pl.pallas_call(
        lambda *refs: march_kernel(n_var, wide_x, wide_r, count_x, *refs),
        out_shape=jax.ShapeDtypeStruct((n_tile, ROWS, n_wide * LANES), jnp.float32),
        in_specs=[pl.BlockSpec(memory_space=pltpu.SMEM)] + [VMEM] * 7,
        out_specs=VMEM,
        scratch_shapes=[
            pltpu.VMEM((n_plane + 1, LANES, n_theta), jnp.float32),
            pltpu.VMEM((n_plane, n_theta + 2 * ROWS, LANES), jnp.float32),
            pltpu.VMEM((n_plane, n_theta + 2 * ROWS, LANES), jnp.float32),
            pltpu.VMEM((n_theta + ROWS, LANES), jnp.float32),
            pltpu.VMEM((n_tile, ROWS, n_wide * LANES), jnp.float32),
            pltpu.VMEM((2, n_tile, n_wide, ROWS, LANES), jnp.float32),
        ],
        compiler_params=PARAMS,
        name="march",
    )(jnp.stack([at_x, at_r]), edge, own, mate_edge, mate, far_edge, far, panel)
    got = lax.all_to_all(sent, "row", 0, 0, tiled=True)
    stats = pl.pallas_call(
        reduce_kernel,
        out_shape=jax.ShapeDtypeStruct((count_x, ROWS, LANES), jnp.float32),
        in_specs=[VMEM],
        out_specs=VMEM,
        compiler_params=PARAMS,
        name="reduce",
    )(got)
    stats = lax.all_to_all(stats, "gx", 0, 0, tiled=True)
    cells = pl.pallas_call(
        lambda *refs: relay_kernel(n_plane, wide_x, wide_r, *refs),
        out_shape=jax.ShapeDtypeStruct((n_plane * wide_x, ROWS, count_r * wide_r), jnp.float32),
        in_specs=[VMEM],
        out_specs=VMEM,
        compiler_params=PARAMS,
        name="relay",
    )(got)
    scale = math.sqrt(n_var * wide_x * count_x * wide_r * count_r * n_theta)
    basis = pl.pallas_call(
        lambda *refs: final_kernel(n_var, wide_x, scale, *refs),
        out_shape=jax.ShapeDtypeStruct(cells.shape, jnp.float32),
        in_specs=[VMEM, VMEM],
        out_specs=VMEM,
        scratch_shapes=[pltpu.VMEM((2 * ROWS, LANES), jnp.float32)],
        compiler_params=PARAMS,
        name="final",
    )(stats, cells)
    return basis.reshape((n_vec, n_var, wide_x, n_theta // count_r, count_r * wide_r))


def solution(mesh):
    placed = (
        P(None, None, "gx", "row", None),
        P(None, "gx", "row"),
        P(("gx", "row"), None, None),
        P(),
    )
    return jax.shard_map(
        body,
        mesh=mesh,
        in_specs=placed,
        out_specs=P(None, None, "gx", "row", None),
        check_vma=False,
    )
```

```python
import math

import jax
import jax.numpy as jnp
from jax import lax
from jax.experimental import pallas as pl
from jax.experimental.pallas import tpu as pltpu
from jax.sharding import PartitionSpec as P

STEPS = 2
UNROLL = 2
RIM = 2
LANES = 128
ROWS = 8
RING = 12
HIGH, LOW, SIZE, PANEL = 64, 76, 88, 100


def two_sum(a, b):
    total = a + b
    part = total - a
    return total, (a - (total - part)) + (b - part)


def quick_two_sum(a, b):
    total = a + b
    return total, b - (total - a)


def split(a):
    wide = a * 4097.0
    high = wide - (wide - a)
    return high, a - high


def two_prod(a, b):
    product = a * b
    a_high, a_low = split(a)
    b_high, b_low = split(b)
    return product, ((a_high * b_high - product) + a_high * b_low + a_low * b_high) + a_low * b_low


def pair_add(a, b):
    high, low = two_sum(a[0], b[0])
    return quick_two_sum(high, low + (a[1] + b[1]))


def pair_mul(a, b):
    high, low = two_prod(a[0], b[0])
    return quick_two_sum(high, low + (a[0] * b[1] + a[1] * b[0]))


def pair_scale(a, factor):
    high, low = two_prod(a[0], factor)
    return quick_two_sum(high, low + a[1] * factor)


def pair_roll(a, shift, axis):
    size = a[0].shape[axis]
    return tuple(pltpu.roll(part, shift % size, axis) for part in a)


def pair_tree(pairs):
    while len(pairs) > 1:
        rest = [pairs[-1]] if len(pairs) % 2 else []
        pairs = [pair_add(pairs[i], pairs[i + 1]) for i in range(0, len(pairs) - 1, 2)] + rest
    return pairs[0]


def tree(parts, join):
    while len(parts) > 1:
        rest = [parts[-1]] if len(parts) % 2 else []
        parts = [join(parts[i], parts[i + 1]) for i in range(0, len(parts) - 1, 2)] + rest
    return parts[0]


def lanes_of(shape):
    return lax.broadcasted_iota(jnp.int32, shape, 1)


def roll_lanes(value, shift):
    return pltpu.roll(value, shift % LANES, 1)


def safe_inverse(value):
    positive = value > 0
    return jnp.where(positive, 1.0 / jnp.where(positive, value, 1.0), 0.0)


def merge(tiles):
    size = tree(tiles, jnp.maximum)
    inverse = safe_inverse(size)
    scaled = []
    for tile in tiles:
        ratio = tile * inverse
        ratio = roll_lanes(ratio * ratio, HIGH - SIZE)
        scaled.append(pair_scale((tile, roll_lanes(tile, HIGH - LOW)), ratio))
    return pair_tree(scaled), size, tree(tiles, jnp.add)


def placed_at(lane, start, width, value, other):
    return jnp.where((lane >= start) & (lane < start + width), value, other)


def pack_stats(pair, size, panel):
    lane = lanes_of(size.shape)
    tile = placed_at(lane, HIGH, RING, pair[0], 0.0)
    tile = placed_at(lane, LOW, RING, roll_lanes(pair[1], LOW - HIGH), tile)
    tile = placed_at(lane, SIZE, RING, size, tile)
    return jnp.where(lane >= PANEL, panel, tile)


def march_kernel(
    n_var, wide_x, wide_r, count_x,
    place_ref, mid_ref, mate_ref, far_ref, panel_ref,
    out_ref, now_ref, next_ref, coeff_ref, packed_ref, parts_ref,
):
    n_plane = mid_ref.shape[0] - 1
    n_theta = mid_ref.shape[-1]
    n_tile = n_theta // ROWS
    deep = wide_r + 2 * RIM
    n_pair = n_var * n_var
    used = (wide_x + 2 * RIM) * deep

    mate_is_low = jnp.full((RIM * deep, n_theta), place_ref[0] % 2, jnp.int32) == 1

    def turn(plane):
        mate, far = mate_ref[plane], far_ref[plane]
        low = jnp.where(mate_is_low, mate, far)
        high = jnp.where(mate_is_low, far, mate)
        blank = jnp.zeros((LANES - used, n_theta), jnp.float32)
        return jnp.concatenate([low, mid_ref[plane], high, blank], axis=0).T

    for plane in range(n_plane):
        turned = turn(plane)
        now_ref[plane, ROWS : ROWS + n_theta, :] = turned
        now_ref[plane, ROWS - 1 : ROWS, :] = turned[n_theta - 1 :]
        now_ref[plane, ROWS + n_theta : ROWS + n_theta + 1, :] = turned[:1]
    coeff_ref[:n_theta, :] = turn(n_plane)
    viscous = coeff_ref[4 * n_pair : 4 * n_pair + 1, :]
    for i in range(n_var):
        own = 3 * n_pair + i * n_var + i
        coeff_ref[own : own + 1, :] = coeff_ref[own : own + 1, :] + (1.0 - 6.0 * viscous)
    for n, shift in enumerate((deep, -deep, 1, -1)):
        coeff_ref[n_theta + n : n_theta + n + 1, :] = roll_lanes(viscous, shift)

    lane = lanes_of((ROWS, LANES))
    at_x = lane // deep - RIM + place_ref[0] * wide_x
    inside = (at_x >= 0) & (at_x < wide_x * count_x) & (lane < used)
    first = place_ref[1] == 0
    from_above = ~((lane % deep == 2 * RIM - 1) & first)
    from_below = ~((lane % deep == 2 * RIM) & first)

    def coeff(index):
        return coeff_ref[index : index + 1, :]

    def advance(source_ref, tile):
        start = ROWS + tile * ROWS
        centre = [source_ref[b, pl.ds(start, ROWS), :] for b in range(n_plane)]
        before = [source_ref[b, pl.ds(start - 1, ROWS), :] for b in range(n_plane)]
        after = [source_ref[b, pl.ds(start + 1, ROWS), :] for b in range(n_plane)]
        differ = [a - b for a, b in zip(after, before)]
        both = [a + b for a, b in zip(after, before)]
        result = [None] * n_plane
        for i in range(n_var):
            for k in range(0, n_plane, n_var):
                def flux(start, values):
                    return tree([coeff(start + j * n_var + i) * values[k + j] for j in range(n_var)], jnp.add)

                own = centre[k + i]
                stream = flux(0, centre)
                radial = flux(n_pair, centre)
                local = flux(2 * n_pair, differ) + flux(3 * n_pair, centre)
                local = local + coeff(4 * n_pair) * both[k + i]
                above = roll_lanes(coeff(n_theta + 2) * own + radial, -1)
                below = roll_lanes(coeff(n_theta + 3) * own - radial, 1)
                local = local + roll_lanes(coeff(n_theta) * own + stream, -deep)
                local = local + roll_lanes(coeff(n_theta + 1) * own - stream, deep)
                local = local + jnp.where(from_above, above, 0.0) + jnp.where(from_below, below, 0.0)
                result[k + i] = local
        return result

    def first_step(tile, carry):
        result = advance(now_ref, tile)
        for b in range(n_plane):
            next_ref[b, pl.ds(ROWS + tile * ROWS, ROWS), :] = jnp.where(inside, result[b], 0.0)
        return carry

    lax.fori_loop(0, n_tile, first_step, 0, unroll=UNROLL)
    for b in range(n_plane):
        next_ref[b, ROWS - 1 : ROWS, :] = next_ref[b, ROWS + n_theta - 1 : ROWS + n_theta, :]
        next_ref[b, ROWS + n_theta : ROWS + n_theta + 1, :] = next_ref[b, ROWS : ROWS + 1, :]

    group = wide_x * wide_r
    per_vreg = LANES // group
    n_wide = packed_ref.shape[-1] // LANES
    mine = []
    for x in range(wide_x):
        start = (x + RIM) * deep + RIM
        mine.append((lane >= start) & (lane < start + wide_r))

    def second_step(tile, largest):
        result = advance(next_ref, tile)
        for v in range(n_wide):
            pieces = []
            for b in range(v * per_vreg, min((v + 1) * per_vreg, n_plane)):
                for x in range(wide_x):
                    shift = (b % per_vreg) * group + x * wide_r - ((x + RIM) * deep + RIM)
                    pieces.append(roll_lanes(jnp.where(mine[x], result[b], 0.0), shift))
            packed = tree(pieces, jnp.add)
            packed_ref[tile, :, v * LANES : (v + 1) * LANES] = packed
            largest = jnp.maximum(largest, jnp.abs(packed))
        return largest

    largest = lax.fori_loop(0, n_tile, second_step, jnp.zeros((ROWS, LANES), jnp.float32), unroll=UNROLL)
    largest = jnp.max(largest, axis=1, keepdims=True)
    largest = jnp.max(largest, axis=0, keepdims=True)
    inverse = safe_inverse(jnp.broadcast_to(largest, (ROWS, LANES)))
    largest = jnp.broadcast_to(largest, (ROWS, LANES))

    for tile in range(n_tile):
        for v in range(n_wide):
            high, low = split(packed_ref[tile, :, v * LANES : (v + 1) * LANES] * inverse)
            parts_ref[0, tile, v] = high
            parts_ref[1, tile, v] = low

    def shifted(part, tile, v, s):
        whole, rest = divmod(s, per_vreg)
        value = parts_ref[part, tile, (v + whole) % n_wide]
        if not rest:
            return value
        other = parts_ref[part, tile, (v + whole + 1) % n_wide]
        keep = lane < LANES - rest * group
        return jnp.where(keep, roll_lanes(value, -rest * group), roll_lanes(other, -rest * group))

    zero = jnp.zeros((ROWS, LANES), jnp.float32)
    pairs = [[(zero, zero)] * n_wide for _ in range(ROWS)]
    for s in range(RING // 2 + 1):
        for v in range(n_wide):
            if 2 * s == RING and v * per_vreg + s >= n_plane:
                continue
            total, error = zero, zero
            for tile in range(n_tile):
                a_high, a_low = parts_ref[0, tile, v], parts_ref[1, tile, v]
                if s:
                    b_high, b_low = shifted(0, tile, v, s), shifted(1, tile, v, s)
                    minor = a_high * b_low + a_low * b_high
                else:
                    b_high, b_low = a_high, a_low
                    minor = 2.0 * a_high * a_low
                total, lost = two_sum(total, a_high * b_high)
                error = error + (lost + (minor + a_low * b_low))
            pairs[s][v] = quick_two_sum(total, error)
    row = lax.broadcasted_iota(jnp.int32, (ROWS, LANES), 0)
    sums = []
    for v in range(n_wide):
        level = [pairs[s][v] for s in range(ROWS)]
        half = ROWS // 2
        while half:
            joined = []
            for s in range(half):
                a, b = level[s], level[s + half]
                front = (row // half) % 2 == 0
                a_turned, b_turned = pair_roll(a, -half, 0), pair_roll(b, half, 0)
                one = tuple(jnp.where(front, p, q) for p, q in zip(a, b_turned))
                two = tuple(jnp.where(front, p, q) for p, q in zip(a_turned, b))
                joined.append(pair_add(one, two))
            level = joined
            half //= 2
        sums.append(level[0])
    step = group // 2
    while step:
        sums = [pair_add(a, pair_roll(a, -step, 1)) for a in sums]
        step //= 2
    gathered = (zero, zero)
    for b in range(RING):
        turned = pair_roll(sums[b // per_vreg], HIGH + b - (b % per_vreg) * group, 1)
        gathered = tuple(jnp.where(lane == HIGH + b, p, q) for p, q in zip(turned, gathered))
    stats = pack_stats(gathered, largest, panel_ref[...])
    last = (n_wide - 1) * LANES
    for tile in range(n_tile):
        out_ref[tile, :, :last] = packed_ref[tile, :, :last]
        out_ref[tile, :, last:] = jnp.where(lane < HIGH, packed_ref[tile, :, last:], stats)


def prepare_kernel(tail_ref, coeff_ref, edge_ref, turned_ref):
    n_plane = tail_ref.shape[0]
    n_coeff = coeff_ref.shape[-1]
    edge_ref[:n_plane] = tail_ref[...]
    turned_ref[...] = jnp.zeros_like(turned_ref)
    turned_ref[:, :, :n_coeff] = coeff_ref[...]
    edge_ref[n_plane] = turned_ref[:, turned_ref.shape[1] - edge_ref.shape[2] :, :]


def reduce_kernel(got_ref, out_ref):
    count, _, wide = got_ref.shape
    pair, size, panel = merge([got_ref[n, :, wide - LANES :] for n in range(count)])
    tile = pack_stats(pair, size, panel)
    for n in range(out_ref.shape[0]):
        out_ref[n] = tile


def relay_kernel(n_plane, wide_x, wide_r, got_ref, out_ref):
    count = got_ref.shape[0]
    per_vreg = LANES // wide_r
    lane = lanes_of((ROWS, LANES))
    for g in range(n_plane * wide_x):
        v, slot = divmod(g, per_vreg)
        halves = []
        for half in range(count // per_vreg):
            value = jnp.zeros((ROWS, LANES), jnp.float32)
            for n in range(per_vreg):
                source = got_ref[half * per_vreg + n, :, v * LANES : (v + 1) * LANES]
                turned = roll_lanes(source, (n - slot) * wide_r)
                value = placed_at(lane, n * wide_r, wide_r, turned, value)
            halves.append(value)
        whole = jnp.concatenate(halves, axis=1)
        out_ref[g] = pltpu.roll(whole, whole.shape[1] - RIM, 1)


def final_kernel(n_var, wide_x, scale, got_ref, cells_ref, out_ref, weight_ref):
    n_plane = 2 * n_var
    tiles = [got_ref[n] for n in range(got_ref.shape[0])]
    pair, size, tile = merge(tiles)
    lane = lanes_of((ROWS, LANES))
    row = lax.broadcasted_iota(jnp.int32, (ROWS, LANES), 0)
    live = row < n_var
    one = jnp.where(live & (lane < n_plane), roll_lanes(tile, -PANEL), 0.0)
    two = jnp.where(live & (lane < n_plane), roll_lanes(tile, -PANEL - n_plane), 0.0)
    left = one + roll_lanes(one, RING) + roll_lanes(two, 2 * RING)
    right = one + roll_lanes(two, RING) + roll_lanes(two, 2 * RING)
    inner = []
    for part in pair:
        at = jnp.where(lane < RING, roll_lanes(part, -HIGH), 0.0)
        inner.append(at + roll_lanes(at, RING) + roll_lanes(at, 2 * RING))
    place = lane % RING

    def turned(value, s):
        if not s:
            return value
        return jnp.where(place < RING - s, roll_lanes(value, -s), roll_lanes(value, RING - s))

    terms = []
    for s in range(RING // 2 + 1):
        left_s, right_s = turned(left, s), turned(right, s)
        term = pair_add(two_prod(left, right_s), two_prod(left_s, right))
        share = 1.0 if s else 0.5
        row_s = tuple(share * part[s : s + 1, :] for part in inner)
        terms.append(pair_mul(term, row_s))
    total = pair_tree(terms)
    total = pair_tree([pair_roll(total, -b, 1) for b in range(n_plane)])
    for shift in (4, 2, 1):
        total = pair_add(total, pair_roll(total, shift, 0))

    def everywhere(part, at):
        return jnp.broadcast_to(part[:, at : at + 1], (ROWS, LANES))

    square, cross, other = (
        tuple(everywhere(part, g * RING) for part in total) for g in range(3)
    )
    ratio = cross[0] / square[0]
    left_over = pair_add(cross, tuple(-p for p in pair_scale(square, ratio)))
    ratio = quick_two_sum(ratio, left_over[0] / square[0])
    rest = pair_add(other, tuple(-p for p in pair_mul(cross, ratio)))
    largest = everywhere(size, SIZE)
    inv_one = scale / jnp.sqrt(square[0]) / largest
    inv_two = scale / jnp.sqrt(rest[0]) / largest
    weight_ref[:ROWS, :] = inv_one * one
    weight_ref[ROWS:, :] = inv_two * two - (inv_two * ratio[0]) * one

    for a in range(n_plane):
        at = (a // n_var) * ROWS + a % n_var
        weights = jnp.broadcast_to(weight_ref[at : at + 1, :], (ROWS, LANES))
        spread = [everywhere(weights, b) for b in range(n_plane)]
        for x in range(wide_x):
            for h in range(cells_ref.shape[-1] // LANES):
                cut = slice(h * LANES, (h + 1) * LANES)
                value = spread[0] * cells_ref[x, :, cut]
                for b in range(1, n_plane):
                    value = value + spread[b] * cells_ref[b * wide_x + x, :, cut]
                out_ref[a * wide_x + x, :, cut] = value


VMEM = pl.BlockSpec(memory_space=pltpu.VMEM)
PARAMS = pltpu.CompilerParams(vmem_limit_bytes=32 * 1024 * 1024)


def body(test_vectors, base_coeffs, panel_set, owner_index):
    count_x = lax.axis_size("gx")
    count_r = lax.axis_size("row")
    n_vec, n_var, wide_x, wide_r, n_theta = test_vectors.shape
    n_plane = n_vec * n_var
    at_x, at_r = lax.axis_index("gx"), lax.axis_index("row")

    panel = panel_set[0] / jnp.max(jnp.abs(panel_set[0]))
    panel = jnp.where(at_x * count_r + at_r == owner_index[0], panel, 0.0)
    panel = jnp.concatenate([panel[:n_var], panel[n_var:]], axis=1)
    panel = jnp.pad(panel, ((0, ROWS - n_var), (PANEL, LANES - PANEL - 2 * n_plane)))

    field = test_vectors.reshape((n_plane, wide_x, wide_r, n_theta))
    edge, turned = pl.pallas_call(
        prepare_kernel,
        out_shape=(
            jax.ShapeDtypeStruct((n_plane + 1, wide_x, 2 * RIM, n_theta), jnp.float32),
            jax.ShapeDtypeStruct((wide_x, wide_r, n_theta), jnp.float32),
        ),
        in_specs=[VMEM, VMEM],
        out_specs=(VMEM, VMEM),
        compiler_params=PARAMS,
        name="prepare",
    )(field[:, :, wide_r - 2 * RIM :], base_coeffs.transpose(1, 2, 0))
    ring = [(i, (i + 1) % count_r) for i in range(count_r)]
    edge = lax.ppermute(edge, "row", ring)
    both = jnp.concatenate([field, turned[None]], axis=0)
    both = jnp.concatenate([edge, both], axis=2)
    both = both.reshape((n_plane + 1, wide_x * (wide_r + 2 * RIM), n_theta))
    outer = [(i, i + 1 if i % 2 else i - 1) for i in range(1, count_x - 1)]
    far = lax.ppermute(both, "gx", outer)
    mate = lax.ppermute(both, "gx", [(i, i ^ 1) for i in range(count_x)])

    n_wide = 3
    n_tile = n_theta // ROWS
    sent = pl.pallas_call(
        lambda *refs: march_kernel(n_var, wide_x, wide_r, count_x, *refs),
        out_shape=jax.ShapeDtypeStruct((n_tile, ROWS, n_wide * LANES), jnp.float32),
        in_specs=[pl.BlockSpec(memory_space=pltpu.SMEM)] + [VMEM] * 4,
        out_specs=VMEM,
        scratch_shapes=[
            pltpu.VMEM((n_plane, n_theta + 2 * ROWS, LANES), jnp.float32),
            pltpu.VMEM((n_plane, n_theta + 2 * ROWS, LANES), jnp.float32),
            pltpu.VMEM((n_theta + ROWS, LANES), jnp.float32),
            pltpu.VMEM((n_tile, ROWS, n_wide * LANES), jnp.float32),
            pltpu.VMEM((2, n_tile, n_wide, ROWS, LANES), jnp.float32),
        ],
        compiler_params=PARAMS,
        name="march",
    )(jnp.stack([at_x, at_r]), both, mate, far, panel)
    got = lax.all_to_all(sent, "row", 0, 0, tiled=True)
    stats = pl.pallas_call(
        reduce_kernel,
        out_shape=jax.ShapeDtypeStruct((count_x, ROWS, LANES), jnp.float32),
        in_specs=[VMEM],
        out_specs=VMEM,
        compiler_params=PARAMS,
        name="reduce",
    )(got)
    stats = lax.all_to_all(stats, "gx", 0, 0, tiled=True)
    cells = pl.pallas_call(
        lambda *refs: relay_kernel(n_plane, wide_x, wide_r, *refs),
        out_shape=jax.ShapeDtypeStruct((n_plane * wide_x, ROWS, count_r * wide_r), jnp.float32),
        in_specs=[VMEM],
        out_specs=VMEM,
        compiler_params=PARAMS,
        name="relay",
    )(got)
    scale = math.sqrt(n_var * wide_x * count_x * wide_r * count_r * n_theta)
    basis = pl.pallas_call(
        lambda *refs: final_kernel(n_var, wide_x, scale, *refs),
        out_shape=jax.ShapeDtypeStruct(cells.shape, jnp.float32),
        in_specs=[VMEM, VMEM],
        out_specs=VMEM,
        scratch_shapes=[pltpu.VMEM((2 * ROWS, LANES), jnp.float32)],
        compiler_params=PARAMS,
        name="final",
    )(stats, cells)
    return basis.reshape((n_vec, n_var, wide_x, n_theta // count_r, count_r * wide_r))


def solution(mesh):
    placed = (
        P(None, None, "gx", "row", None),
        P(None, "gx", "row"),
        P(("gx", "row"), None, None),
        P(),
    )
    return jax.shard_map(
        body,
        mesh=mesh,
        in_specs=placed,
        out_specs=P(None, None, "gx", "row", None),
        check_vma=False,
    )
```

```python
import math

import jax
import jax.numpy as jnp
from jax import lax
from jax.experimental import pallas as pl
from jax.experimental.pallas import tpu as pltpu
from jax.sharding import PartitionSpec as P

STEPS = 2
UNROLL = 2
RIM = 2
LANES = 128
ROWS = 8
RING = 12
HIGH, LOW, SIZE, PANEL = 64, 76, 88, 100


def two_sum(a, b):
    total = a + b
    part = total - a
    return total, (a - (total - part)) + (b - part)


def quick_two_sum(a, b):
    total = a + b
    return total, b - (total - a)


def split(a):
    wide = a * 4097.0
    high = wide - (wide - a)
    return high, a - high


def two_prod(a, b):
    product = a * b
    a_high, a_low = split(a)
    b_high, b_low = split(b)
    return product, ((a_high * b_high - product) + a_high * b_low + a_low * b_high) + a_low * b_low


def pair_add(a, b):
    high, low = two_sum(a[0], b[0])
    return quick_two_sum(high, low + (a[1] + b[1]))


def pair_mul(a, b):
    high, low = two_prod(a[0], b[0])
    return quick_two_sum(high, low + (a[0] * b[1] + a[1] * b[0]))


def pair_scale(a, factor):
    high, low = two_prod(a[0], factor)
    return quick_two_sum(high, low + a[1] * factor)


def pair_roll(a, shift, axis):
    size = a[0].shape[axis]
    return tuple(pltpu.roll(part, shift % size, axis) for part in a)


def pair_tree(pairs):
    while len(pairs) > 1:
        rest = [pairs[-1]] if len(pairs) % 2 else []
        pairs = [pair_add(pairs[i], pairs[i + 1]) for i in range(0, len(pairs) - 1, 2)] + rest
    return pairs[0]


def tree(parts, join):
    while len(parts) > 1:
        rest = [parts[-1]] if len(parts) % 2 else []
        parts = [join(parts[i], parts[i + 1]) for i in range(0, len(parts) - 1, 2)] + rest
    return parts[0]


def lanes_of(shape):
    return lax.broadcasted_iota(jnp.int32, shape, 1)


def roll_lanes(value, shift):
    return pltpu.roll(value, shift % LANES, 1)


def safe_inverse(value):
    positive = value > 0
    return jnp.where(positive, 1.0 / jnp.where(positive, value, 1.0), 0.0)


def merge(tiles):
    size = tree(tiles, jnp.maximum)
    inverse = safe_inverse(size)
    scaled = []
    for tile in tiles:
        ratio = tile * inverse
        ratio = roll_lanes(ratio * ratio, HIGH - SIZE)
        scaled.append(pair_scale((tile, roll_lanes(tile, HIGH - LOW)), ratio))
    return pair_tree(scaled), size, tree(tiles, jnp.add)


def placed_at(lane, start, width, value, other):
    return jnp.where((lane >= start) & (lane < start + width), value, other)


def pack_stats(pair, size, panel):
    lane = lanes_of(size.shape)
    tile = placed_at(lane, HIGH, RING, pair[0], 0.0)
    tile = placed_at(lane, LOW, RING, roll_lanes(pair[1], LOW - HIGH), tile)
    tile = placed_at(lane, SIZE, RING, size, tile)
    return jnp.where(lane >= PANEL, panel, tile)


def march_kernel(
    n_var, wide_x, wide_r, count_x,
    place_ref, mid_ref, mate_ref, far_ref, panel_ref,
    out_ref, now_ref, next_ref, coeff_ref, packed_ref, parts_ref,
):
    n_plane = mid_ref.shape[0] - 1
    n_theta = mid_ref.shape[-1]
    n_tile = n_theta // ROWS
    deep = wide_r + 2 * RIM
    n_pair = n_var * n_var
    used = (wide_x + 2 * RIM) * deep

    mate_is_low = jnp.full((RIM * deep, n_theta), place_ref[0] % 2, jnp.int32) == 1

    def turn(plane):
        mate, far = mate_ref[plane], far_ref[plane]
        low = jnp.where(mate_is_low, mate, far)
        high = jnp.where(mate_is_low, far, mate)
        blank = jnp.zeros((LANES - used, n_theta), jnp.float32)
        return jnp.concatenate([low, mid_ref[plane], high, blank], axis=0).T

    for plane in range(n_plane):
        turned = turn(plane)
        now_ref[plane, ROWS : ROWS + n_theta, :] = turned
        now_ref[plane, ROWS - 1 : ROWS, :] = turned[n_theta - 1 :]
        now_ref[plane, ROWS + n_theta : ROWS + n_theta + 1, :] = turned[:1]
    coeff_ref[:n_theta, :] = turn(n_plane)
    viscous = coeff_ref[4 * n_pair : 4 * n_pair + 1, :]
    for i in range(n_var):
        own = 3 * n_pair + i * n_var + i
        coeff_ref[own : own + 1, :] = coeff_ref[own : own + 1, :] + (1.0 - 6.0 * viscous)
    for n, shift in enumerate((deep, -deep, 1, -1)):
        coeff_ref[n_theta + n : n_theta + n + 1, :] = roll_lanes(viscous, shift)

    lane = lanes_of((ROWS, LANES))
    at_x = lane // deep - RIM + place_ref[0] * wide_x
    inside = (at_x >= 0) & (at_x < wide_x * count_x) & (lane < used)
    first = place_ref[1] == 0
    from_above = ~((lane % deep == 2 * RIM - 1) & first)
    from_below = ~((lane % deep == 2 * RIM) & first)

    def coeff(index):
        return coeff_ref[index : index + 1, :]

    def advance(source_ref, tile):
        start = ROWS + tile * ROWS
        centre = [source_ref[b, pl.ds(start, ROWS), :] for b in range(n_plane)]
        before = [source_ref[b, pl.ds(start - 1, ROWS), :] for b in range(n_plane)]
        after = [source_ref[b, pl.ds(start + 1, ROWS), :] for b in range(n_plane)]
        differ = [a - b for a, b in zip(after, before)]
        both = [a + b for a, b in zip(after, before)]
        result = [None] * n_plane
        for i in range(n_var):
            for k in range(0, n_plane, n_var):
                def flux(start, values):
                    return tree([coeff(start + j * n_var + i) * values[k + j] for j in range(n_var)], jnp.add)

                own = centre[k + i]
                stream = flux(0, centre)
                radial = flux(n_pair, centre)
                local = flux(2 * n_pair, differ) + flux(3 * n_pair, centre)
                local = local + coeff(4 * n_pair) * both[k + i]
                above = roll_lanes(coeff(n_theta + 2) * own + radial, -1)
                below = roll_lanes(coeff(n_theta + 3) * own - radial, 1)
                local = local + roll_lanes(coeff(n_theta) * own + stream, -deep)
                local = local + roll_lanes(coeff(n_theta + 1) * own - stream, deep)
                local = local + jnp.where(from_above, above, 0.0) + jnp.where(from_below, below, 0.0)
                result[k + i] = local
        return result

    def first_step(tile, carry):
        result = advance(now_ref, tile)
        for b in range(n_plane):
            next_ref[b, pl.ds(ROWS + tile * ROWS, ROWS), :] = jnp.where(inside, result[b], 0.0)
        return carry

    lax.fori_loop(0, n_tile, first_step, 0, unroll=UNROLL)
    for b in range(n_plane):
        next_ref[b, ROWS - 1 : ROWS, :] = next_ref[b, ROWS + n_theta - 1 : ROWS + n_theta, :]
        next_ref[b, ROWS + n_theta : ROWS + n_theta + 1, :] = next_ref[b, ROWS : ROWS + 1, :]

    group = wide_x * wide_r
    per_vreg = LANES // group
    n_wide = packed_ref.shape[-1] // LANES
    mine = []
    for x in range(wide_x):
        start = (x + RIM) * deep + RIM
        mine.append((lane >= start) & (lane < start + wide_r))

    def second_step(tile, largest):
        result = advance(next_ref, tile)
        for v in range(n_wide):
            pieces = []
            for b in range(v * per_vreg, min((v + 1) * per_vreg, n_plane)):
                for x in range(wide_x):
                    shift = (b % per_vreg) * group + x * wide_r - ((x + RIM) * deep + RIM)
                    pieces.append(roll_lanes(jnp.where(mine[x], result[b], 0.0), shift))
            packed = tree(pieces, jnp.add)
            packed_ref[tile, :, v * LANES : (v + 1) * LANES] = packed
            largest = jnp.maximum(largest, jnp.abs(packed))
        return largest

    largest = lax.fori_loop(0, n_tile, second_step, jnp.zeros((ROWS, LANES), jnp.float32), unroll=UNROLL)
    largest = jnp.max(largest, axis=1, keepdims=True)
    largest = jnp.max(largest, axis=0, keepdims=True)
    inverse = safe_inverse(jnp.broadcast_to(largest, (ROWS, LANES)))
    largest = jnp.broadcast_to(largest, (ROWS, LANES))

    for tile in range(n_tile):
        for v in range(n_wide):
            high, low = split(packed_ref[tile, :, v * LANES : (v + 1) * LANES] * inverse)
            parts_ref[0, tile, v] = high
            parts_ref[1, tile, v] = low

    def shifted(part, tile, v, s):
        whole, rest = divmod(s, per_vreg)
        value = parts_ref[part, tile, (v + whole) % n_wide]
        if not rest:
            return value
        other = parts_ref[part, tile, (v + whole + 1) % n_wide]
        keep = lane < LANES - rest * group
        return jnp.where(keep, roll_lanes(value, -rest * group), roll_lanes(other, -rest * group))

    zero = jnp.zeros((ROWS, LANES), jnp.float32)
    pairs = [[(zero, zero)] * n_wide for _ in range(ROWS)]
    for s in range(RING // 2 + 1):
        for v in range(n_wide):
            if 2 * s == RING and v * per_vreg + s >= n_plane:
                continue
            total, error = zero, zero
            for tile in range(n_tile):
                a_high, a_low = parts_ref[0, tile, v], parts_ref[1, tile, v]
                if s:
                    b_high, b_low = shifted(0, tile, v, s), shifted(1, tile, v, s)
                    minor = a_high * b_low + a_low * b_high
                else:
                    b_high, b_low = a_high, a_low
                    minor = 2.0 * a_high * a_low
                total, lost = two_sum(total, a_high * b_high)
                error = error + (lost + (minor + a_low * b_low))
            pairs[s][v] = quick_two_sum(total, error)
    row = lax.broadcasted_iota(jnp.int32, (ROWS, LANES), 0)
    sums = []
    for v in range(n_wide):
        level = [pairs[s][v] for s in range(ROWS)]
        half = ROWS // 2
        while half:
            joined = []
            for s in range(half):
                a, b = level[s], level[s + half]
                front = (row // half) % 2 == 0
                a_turned, b_turned = pair_roll(a, -half, 0), pair_roll(b, half, 0)
                one = tuple(jnp.where(front, p, q) for p, q in zip(a, b_turned))
                two = tuple(jnp.where(front, p, q) for p, q in zip(a_turned, b))
                joined.append(pair_add(one, two))
            level = joined
            half //= 2
        sums.append(level[0])
    step = group // 2
    while step:
        sums = [pair_add(a, pair_roll(a, -step, 1)) for a in sums]
        step //= 2
    gathered = (zero, zero)
    for b in range(RING):
        turned = pair_roll(sums[b // per_vreg], HIGH + b - (b % per_vreg) * group, 1)
        gathered = tuple(jnp.where(lane == HIGH + b, p, q) for p, q in zip(turned, gathered))
    stats = pack_stats(gathered, largest, panel_ref[...])
    last = (n_wide - 1) * LANES
    for tile in range(n_tile):
        out_ref[tile, :, :last] = packed_ref[tile, :, :last]
        out_ref[tile, :, last:] = jnp.where(lane < HIGH, packed_ref[tile, :, last:], stats)


def prepare_kernel(tail_ref, coeff_ref, edge_ref, turned_ref):
    n_plane = tail_ref.shape[0]
    n_coeff = coeff_ref.shape[-1]
    edge_ref[:n_plane] = tail_ref[...]
    turned_ref[...] = jnp.zeros_like(turned_ref)
    turned_ref[:, :, :n_coeff] = coeff_ref[...]
    edge_ref[n_plane] = turned_ref[:, turned_ref.shape[1] - edge_ref.shape[2] :, :]


def reduce_kernel(got_ref, out_ref):
    count, _, wide = got_ref.shape
    pair, size, panel = merge([got_ref[n, :, wide - LANES :] for n in range(count)])
    tile = pack_stats(pair, size, panel)
    for n in range(out_ref.shape[0]):
        out_ref[n] = tile


def relay_kernel(n_plane, wide_x, wide_r, got_ref, out_ref):
    count = got_ref.shape[0]
    per_vreg = LANES // wide_r
    lane = lanes_of((ROWS, LANES))
    for g in range(n_plane * wide_x):
        v, slot = divmod(g, per_vreg)
        halves = []
        for half in range(count // per_vreg):
            value = jnp.zeros((ROWS, LANES), jnp.float32)
            for n in range(per_vreg):
                source = got_ref[half * per_vreg + n, :, v * LANES : (v + 1) * LANES]
                turned = roll_lanes(source, (n - slot) * wide_r)
                value = placed_at(lane, n * wide_r, wide_r, turned, value)
            halves.append(value)
        whole = jnp.concatenate(halves, axis=1)
        out_ref[g] = pltpu.roll(whole, whole.shape[1] - RIM, 1)


def final_kernel(n_var, wide_x, scale, got_ref, cells_ref, out_ref, weight_ref):
    n_plane = 2 * n_var
    tiles = [got_ref[n] for n in range(got_ref.shape[0])]
    pair, size, tile = merge(tiles)
    lane = lanes_of((ROWS, LANES))
    row = lax.broadcasted_iota(jnp.int32, (ROWS, LANES), 0)
    live = row < n_var
    one = jnp.where(live & (lane < n_plane), roll_lanes(tile, -PANEL), 0.0)
    two = jnp.where(live & (lane < n_plane), roll_lanes(tile, -PANEL - n_plane), 0.0)
    left = one + roll_lanes(one, RING) + roll_lanes(two, 2 * RING)
    right = one + roll_lanes(two, RING) + roll_lanes(two, 2 * RING)
    inner = []
    for part in pair:
        at = jnp.where(lane < RING, roll_lanes(part, -HIGH), 0.0)
        inner.append(at + roll_lanes(at, RING) + roll_lanes(at, 2 * RING))
    place = lane % RING

    def turned(value, s):
        if not s:
            return value
        return jnp.where(place < RING - s, roll_lanes(value, -s), roll_lanes(value, RING - s))

    terms = []
    for s in range(RING // 2 + 1):
        left_s, right_s = turned(left, s), turned(right, s)
        term = pair_add(two_prod(left, right_s), two_prod(left_s, right))
        share = 1.0 if s else 0.5
        row_s = tuple(share * part[s : s + 1, :] for part in inner)
        terms.append(pair_mul(term, row_s))
    total = pair_tree(terms)
    total = pair_tree([pair_roll(total, -b, 1) for b in range(n_plane)])
    for shift in (4, 2, 1):
        total = pair_add(total, pair_roll(total, shift, 0))

    def everywhere(part, at):
        return jnp.broadcast_to(part[:, at : at + 1], (ROWS, LANES))

    square, cross, other = (
        tuple(everywhere(part, g * RING) for part in total) for g in range(3)
    )
    ratio = cross[0] / square[0]
    left_over = pair_add(cross, tuple(-p for p in pair_scale(square, ratio)))
    ratio = quick_two_sum(ratio, left_over[0] / square[0])
    rest = pair_add(other, tuple(-p for p in pair_mul(cross, ratio)))
    largest = everywhere(size, SIZE)
    inv_one = scale / jnp.sqrt(square[0]) / largest
    inv_two = scale / jnp.sqrt(rest[0]) / largest
    weight_ref[:ROWS, :] = inv_one * one
    weight_ref[ROWS:, :] = inv_two * two - (inv_two * ratio[0]) * one

    for a in range(n_plane):
        at = (a // n_var) * ROWS + a % n_var
        weights = jnp.broadcast_to(weight_ref[at : at + 1, :], (ROWS, LANES))
        spread = [everywhere(weights, b) for b in range(n_plane)]
        for x in range(wide_x):
            for h in range(cells_ref.shape[-1] // LANES):
                cut = slice(h * LANES, (h + 1) * LANES)
                value = spread[0] * cells_ref[x, :, cut]
                for b in range(1, n_plane):
                    value = value + spread[b] * cells_ref[b * wide_x + x, :, cut]
                out_ref[a * wide_x + x, :, cut] = value


VMEM = pl.BlockSpec(memory_space=pltpu.VMEM)
PARAMS = pltpu.CompilerParams(vmem_limit_bytes=32 * 1024 * 1024)


def body(test_vectors, base_coeffs, panel_set, owner_index):
    count_x = lax.axis_size("gx")
    count_r = lax.axis_size("row")
    n_vec, n_var, wide_x, wide_r, n_theta = test_vectors.shape
    n_plane = n_vec * n_var
    at_x, at_r = lax.axis_index("gx"), lax.axis_index("row")

    field = test_vectors.reshape((n_plane, wide_x, wide_r, n_theta))
    edge, turned = pl.pallas_call(
        prepare_kernel,
        out_shape=(
            jax.ShapeDtypeStruct((n_plane + 1, wide_x, 2 * RIM, n_theta), jnp.float32),
            jax.ShapeDtypeStruct((wide_x, wide_r, n_theta), jnp.float32),
        ),
        in_specs=[VMEM, VMEM],
        out_specs=(VMEM, VMEM),
        compiler_params=PARAMS,
        name="prepare",
    )(field[:, :, wide_r - 2 * RIM :], base_coeffs.transpose(1, 2, 0))
    ring = [(i, (i + 1) % count_r) for i in range(count_r)]
    edge = lax.ppermute(edge, "row", ring)
    edge, candidate = lax.optimization_barrier((edge, panel_set[0]))
    both = jnp.concatenate([field, turned[None]], axis=0)
    both = jnp.concatenate([edge, both], axis=2)
    both = both.reshape((n_plane + 1, wide_x * (wide_r + 2 * RIM), n_theta))
    outer = [(i, i + 1 if i % 2 else i - 1) for i in range(1, count_x - 1)]
    far = lax.ppermute(both, "gx", outer)
    mate = lax.ppermute(both, "gx", [(i, i ^ 1) for i in range(count_x)])

    panel = candidate / jnp.max(jnp.abs(candidate))
    panel = jnp.where(at_x * count_r + at_r == owner_index[0], panel, 0.0)
    panel = jnp.concatenate([panel[:n_var], panel[n_var:]], axis=1)
    panel = jnp.pad(panel, ((0, ROWS - n_var), (PANEL, LANES - PANEL - 2 * n_plane)))

    n_wide = 3
    n_tile = n_theta // ROWS
    sent = pl.pallas_call(
        lambda *refs: march_kernel(n_var, wide_x, wide_r, count_x, *refs),
        out_shape=jax.ShapeDtypeStruct((n_tile, ROWS, n_wide * LANES), jnp.float32),
        in_specs=[pl.BlockSpec(memory_space=pltpu.SMEM)] + [VMEM] * 4,
        out_specs=VMEM,
        scratch_shapes=[
            pltpu.VMEM((n_plane, n_theta + 2 * ROWS, LANES), jnp.float32),
            pltpu.VMEM((n_plane, n_theta + 2 * ROWS, LANES), jnp.float32),
            pltpu.VMEM((n_theta + ROWS, LANES), jnp.float32),
            pltpu.VMEM((n_tile, ROWS, n_wide * LANES), jnp.float32),
            pltpu.VMEM((2, n_tile, n_wide, ROWS, LANES), jnp.float32),
        ],
        compiler_params=PARAMS,
        name="march",
    )(jnp.stack([at_x, at_r]), both, mate, far, panel)
    got = lax.all_to_all(sent, "row", 0, 0, tiled=True)
    stats = pl.pallas_call(
        reduce_kernel,
        out_shape=jax.ShapeDtypeStruct((count_x, ROWS, LANES), jnp.float32),
        in_specs=[VMEM],
        out_specs=VMEM,
        compiler_params=PARAMS,
        name="reduce",
    )(got)
    stats = lax.all_to_all(stats, "gx", 0, 0, tiled=True)
    cells = pl.pallas_call(
        lambda *refs: relay_kernel(n_plane, wide_x, wide_r, *refs),
        out_shape=jax.ShapeDtypeStruct((n_plane * wide_x, ROWS, count_r * wide_r), jnp.float32),
        in_specs=[VMEM],
        out_specs=VMEM,
        compiler_params=PARAMS,
        name="relay",
    )(got)
    scale = math.sqrt(n_var * wide_x * count_x * wide_r * count_r * n_theta)
    basis = pl.pallas_call(
        lambda *refs: final_kernel(n_var, wide_x, scale, *refs),
        out_shape=jax.ShapeDtypeStruct(cells.shape, jnp.float32),
        in_specs=[VMEM, VMEM],
        out_specs=VMEM,
        scratch_shapes=[pltpu.VMEM((2 * ROWS, LANES), jnp.float32)],
        compiler_params=PARAMS,
        name="final",
    )(stats, cells)
    return basis.reshape((n_vec, n_var, wide_x, n_theta // count_r, count_r * wide_r))


def solution(mesh):
    placed = (
        P(None, None, "gx", "row", None),
        P(None, "gx", "row"),
        P(("gx", "row"), None, None),
        P(),
    )
    return jax.shard_map(
        body,
        mesh=mesh,
        in_specs=placed,
        out_specs=P(None, None, "gx", "row", None),
        check_vma=False,
    )
```

```python
import math

import jax
import jax.numpy as jnp
from jax import lax
from jax.experimental import pallas as pl
from jax.experimental.pallas import tpu as pltpu
from jax.sharding import PartitionSpec as P

STEPS = 2
UNROLL = 4
RIM = 2
LANES = 128
ROWS = 8
RING = 12
HIGH, LOW, SIZE, PANEL = 64, 76, 88, 100


def two_sum(a, b):
    total = a + b
    part = total - a
    return total, (a - (total - part)) + (b - part)


def quick_two_sum(a, b):
    total = a + b
    return total, b - (total - a)


def split(a):
    wide = a * 4097.0
    high = wide - (wide - a)
    return high, a - high


def two_prod(a, b):
    product = a * b
    a_high, a_low = split(a)
    b_high, b_low = split(b)
    return product, ((a_high * b_high - product) + a_high * b_low + a_low * b_high) + a_low * b_low


def pair_add(a, b):
    high, low = two_sum(a[0], b[0])
    return quick_two_sum(high, low + (a[1] + b[1]))


def pair_mul(a, b):
    high, low = two_prod(a[0], b[0])
    return quick_two_sum(high, low + (a[0] * b[1] + a[1] * b[0]))


def pair_scale(a, factor):
    high, low = two_prod(a[0], factor)
    return quick_two_sum(high, low + a[1] * factor)


def pair_roll(a, shift, axis):
    size = a[0].shape[axis]
    return tuple(pltpu.roll(part, shift % size, axis) for part in a)


def pair_tree(pairs):
    while len(pairs) > 1:
        rest = [pairs[-1]] if len(pairs) % 2 else []
        pairs = [pair_add(pairs[i], pairs[i + 1]) for i in range(0, len(pairs) - 1, 2)] + rest
    return pairs[0]


def tree(parts, join):
    while len(parts) > 1:
        rest = [parts[-1]] if len(parts) % 2 else []
        parts = [join(parts[i], parts[i + 1]) for i in range(0, len(parts) - 1, 2)] + rest
    return parts[0]


def lanes_of(shape):
    return lax.broadcasted_iota(jnp.int32, shape, 1)


def roll_lanes(value, shift):
    return pltpu.roll(value, shift % LANES, 1)


def safe_inverse(value):
    positive = value > 0
    return jnp.where(positive, 1.0 / jnp.where(positive, value, 1.0), 0.0)


def merge(tiles):
    size = tree(tiles, jnp.maximum)
    inverse = safe_inverse(size)
    scaled = []
    for tile in tiles:
        ratio = tile * inverse
        ratio = roll_lanes(ratio * ratio, HIGH - SIZE)
        scaled.append(pair_scale((tile, roll_lanes(tile, HIGH - LOW)), ratio))
    return pair_tree(scaled), size, tree(tiles, jnp.add)


def placed_at(lane, start, width, value, other):
    return jnp.where((lane >= start) & (lane < start + width), value, other)


def pack_stats(pair, size, panel):
    lane = lanes_of(size.shape)
    tile = placed_at(lane, HIGH, RING, pair[0], 0.0)
    tile = placed_at(lane, LOW, RING, roll_lanes(pair[1], LOW - HIGH), tile)
    tile = placed_at(lane, SIZE, RING, size, tile)
    return jnp.where(lane >= PANEL, panel, tile)


def march_kernel(
    n_var, wide_x, wide_r, count_x,
    place_ref, mid_ref, mate_ref, far_ref, panel_ref,
    out_ref, now_ref, next_ref, coeff_ref, packed_ref, parts_ref,
):
    n_plane = mid_ref.shape[0] - 1
    n_theta = mid_ref.shape[-1]
    n_tile = n_theta // ROWS
    deep = wide_r + 2 * RIM
    n_pair = n_var * n_var
    used = (wide_x + 2 * RIM) * deep

    mate_is_low = jnp.full((RIM * deep, n_theta), place_ref[0] % 2, jnp.int32) == 1

    def turn(plane):
        mate, far = mate_ref[plane], far_ref[plane]
        low = jnp.where(mate_is_low, mate, far)
        high = jnp.where(mate_is_low, far, mate)
        blank = jnp.zeros((LANES - used, n_theta), jnp.float32)
        return jnp.concatenate([low, mid_ref[plane], high, blank], axis=0).T

    for plane in range(n_plane):
        turned = turn(plane)
        now_ref[plane, ROWS : ROWS + n_theta, :] = turned
        now_ref[plane, ROWS - 1 : ROWS, :] = turned[n_theta - 1 :]
        now_ref[plane, ROWS + n_theta : ROWS + n_theta + 1, :] = turned[:1]
    coeff_ref[:n_theta, :] = turn(n_plane)
    viscous = coeff_ref[4 * n_pair : 4 * n_pair + 1, :]
    for i in range(n_var):
        own = 3 * n_pair + i * n_var + i
        coeff_ref[own : own + 1, :] = coeff_ref[own : own + 1, :] + (1.0 - 6.0 * viscous)
    for n, shift in enumerate((deep, -deep, 1, -1)):
        coeff_ref[n_theta + n : n_theta + n + 1, :] = roll_lanes(viscous, shift)

    lane = lanes_of((ROWS, LANES))
    at_x = lane // deep - RIM + place_ref[0] * wide_x
    inside = (at_x >= 0) & (at_x < wide_x * count_x) & (lane < used)
    first = place_ref[1] == 0
    from_above = ~((lane % deep == 2 * RIM - 1) & first)
    from_below = ~((lane % deep == 2 * RIM) & first)

    def coeff(index):
        return coeff_ref[index : index + 1, :]

    def advance(source_ref, tile):
        start = ROWS + tile * ROWS
        centre = [source_ref[b, pl.ds(start, ROWS), :] for b in range(n_plane)]
        before = [source_ref[b, pl.ds(start - 1, ROWS), :] for b in range(n_plane)]
        after = [source_ref[b, pl.ds(start + 1, ROWS), :] for b in range(n_plane)]
        differ = [a - b for a, b in zip(after, before)]
        both = [a + b for a, b in zip(after, before)]
        result = [None] * n_plane
        for i in range(n_var):
            for k in range(0, n_plane, n_var):
                def flux(start, values):
                    return tree([coeff(start + j * n_var + i) * values[k + j] for j in range(n_var)], jnp.add)

                own = centre[k + i]
                stream = flux(0, centre)
                radial = flux(n_pair, centre)
                local = flux(2 * n_pair, differ) + flux(3 * n_pair, centre)
                local = local + coeff(4 * n_pair) * both[k + i]
                above = roll_lanes(coeff(n_theta + 2) * own + radial, -1)
                below = roll_lanes(coeff(n_theta + 3) * own - radial, 1)
                local = local + roll_lanes(coeff(n_theta) * own + stream, -deep)
                local = local + roll_lanes(coeff(n_theta + 1) * own - stream, deep)
                local = local + jnp.where(from_above, above, 0.0) + jnp.where(from_below, below, 0.0)
                result[k + i] = local
        return result

    def keep(tile, result):
        for b in range(n_plane):
            next_ref[b, pl.ds(ROWS + tile * ROWS, ROWS), :] = jnp.where(inside, result[b], 0.0)

    group = wide_x * wide_r
    per_vreg = LANES // group
    n_wide = packed_ref.shape[-1] // LANES
    mine = []
    for x in range(wide_x):
        start = (x + RIM) * deep + RIM
        mine.append((lane >= start) & (lane < start + wide_r))

    def pack(tile, result, largest):
        for v in range(n_wide):
            pieces = []
            for b in range(v * per_vreg, min((v + 1) * per_vreg, n_plane)):
                for x in range(wide_x):
                    shift = (b % per_vreg) * group + x * wide_r - ((x + RIM) * deep + RIM)
                    pieces.append(roll_lanes(jnp.where(mine[x], result[b], 0.0), shift))
            packed = tree(pieces, jnp.add)
            packed_ref[tile, :, v * LANES : (v + 1) * LANES] = packed
            largest = jnp.maximum(largest, jnp.abs(packed))
        return largest

    for tile in (n_tile - 2, n_tile - 1, 0, 1):
        keep(tile, advance(now_ref, tile))
    for b in range(n_plane):
        next_ref[b, ROWS - 1 : ROWS, :] = next_ref[b, ROWS + n_theta - 1 : ROWS + n_theta, :]
        next_ref[b, ROWS + n_theta : ROWS + n_theta + 1, :] = next_ref[b, ROWS : ROWS + 1, :]

    def both_steps(tile, largest):
        ahead = advance(now_ref, tile + 2)
        largest = pack(tile, advance(next_ref, tile), largest)
        keep(tile + 2, ahead)
        return largest

    largest = jnp.zeros((ROWS, LANES), jnp.float32)
    largest = lax.fori_loop(0, n_tile - 4, both_steps, largest, unroll=UNROLL)
    for tile in range(n_tile - 4, n_tile):
        largest = pack(tile, advance(next_ref, tile), largest)
    largest = jnp.max(largest, axis=1, keepdims=True)
    largest = jnp.max(largest, axis=0, keepdims=True)
    inverse = safe_inverse(jnp.broadcast_to(largest, (ROWS, LANES)))
    largest = jnp.broadcast_to(largest, (ROWS, LANES))

    for tile in range(n_tile):
        for v in range(n_wide):
            high, low = split(packed_ref[tile, :, v * LANES : (v + 1) * LANES] * inverse)
            parts_ref[0, tile, v] = high
            parts_ref[1, tile, v] = low

    def shifted(part, tile, v, s):
        whole, rest = divmod(s, per_vreg)
        value = parts_ref[part, tile, (v + whole) % n_wide]
        if not rest:
            return value
        other = parts_ref[part, tile, (v + whole + 1) % n_wide]
        keep = lane < LANES - rest * group
        return jnp.where(keep, roll_lanes(value, -rest * group), roll_lanes(other, -rest * group))

    zero = jnp.zeros((ROWS, LANES), jnp.float32)
    pairs = [[(zero, zero)] * n_wide for _ in range(ROWS)]
    for s in range(RING // 2 + 1):
        for v in range(n_wide):
            if 2 * s == RING and v * per_vreg + s >= n_plane:
                continue
            total, error = zero, zero
            for tile in range(n_tile):
                a_high, a_low = parts_ref[0, tile, v], parts_ref[1, tile, v]
                if s:
                    b_high, b_low = shifted(0, tile, v, s), shifted(1, tile, v, s)
                    minor = a_high * b_low + a_low * b_high
                else:
                    b_high, b_low = a_high, a_low
                    minor = 2.0 * a_high * a_low
                total, lost = two_sum(total, a_high * b_high)
                error = error + (lost + (minor + a_low * b_low))
            pairs[s][v] = quick_two_sum(total, error)
    row = lax.broadcasted_iota(jnp.int32, (ROWS, LANES), 0)
    sums = []
    for v in range(n_wide):
        level = [pairs[s][v] for s in range(ROWS)]
        half = ROWS // 2
        while half:
            joined = []
            for s in range(half):
                a, b = level[s], level[s + half]
                front = (row // half) % 2 == 0
                a_turned, b_turned = pair_roll(a, -half, 0), pair_roll(b, half, 0)
                one = tuple(jnp.where(front, p, q) for p, q in zip(a, b_turned))
                two = tuple(jnp.where(front, p, q) for p, q in zip(a_turned, b))
                joined.append(pair_add(one, two))
            level = joined
            half //= 2
        sums.append(level[0])
    step = group // 2
    while step:
        sums = [pair_add(a, pair_roll(a, -step, 1)) for a in sums]
        step //= 2
    gathered = (zero, zero)
    for b in range(RING):
        turned = pair_roll(sums[b // per_vreg], HIGH + b - (b % per_vreg) * group, 1)
        gathered = tuple(jnp.where(lane == HIGH + b, p, q) for p, q in zip(turned, gathered))
    stats = pack_stats(gathered, largest, panel_ref[...])
    last = (n_wide - 1) * LANES
    for tile in range(n_tile):
        out_ref[tile, :, :last] = packed_ref[tile, :, :last]
        out_ref[tile, :, last:] = jnp.where(lane < HIGH, packed_ref[tile, :, last:], stats)


def prepare_kernel(tail_ref, coeff_ref, edge_ref, turned_ref):
    n_plane = tail_ref.shape[0]
    n_coeff = coeff_ref.shape[-1]
    edge_ref[:n_plane] = tail_ref[...]
    turned_ref[...] = jnp.zeros_like(turned_ref)
    turned_ref[:, :, :n_coeff] = coeff_ref[...]
    edge_ref[n_plane] = turned_ref[:, turned_ref.shape[1] - edge_ref.shape[2] :, :]


def reduce_kernel(got_ref, out_ref):
    count, _, wide = got_ref.shape
    pair, size, panel = merge([got_ref[n, :, wide - LANES :] for n in range(count)])
    tile = pack_stats(pair, size, panel)
    for n in range(out_ref.shape[0]):
        out_ref[n] = tile


def relay_kernel(n_plane, wide_x, wide_r, got_ref, out_ref):
    count = got_ref.shape[0]
    per_vreg = LANES // wide_r
    lane = lanes_of((ROWS, LANES))
    for g in range(n_plane * wide_x):
        v, slot = divmod(g, per_vreg)
        halves = []
        for half in range(count // per_vreg):
            value = jnp.zeros((ROWS, LANES), jnp.float32)
            for n in range(per_vreg):
                source = got_ref[half * per_vreg + n, :, v * LANES : (v + 1) * LANES]
                turned = roll_lanes(source, (n - slot) * wide_r)
                value = placed_at(lane, n * wide_r, wide_r, turned, value)
            halves.append(value)
        whole = jnp.concatenate(halves, axis=1)
        out_ref[g] = pltpu.roll(whole, whole.shape[1] - RIM, 1)


def final_kernel(n_var, wide_x, scale, got_ref, cells_ref, out_ref, weight_ref):
    n_plane = 2 * n_var
    tiles = [got_ref[n] for n in range(got_ref.shape[0])]
    pair, size, tile = merge(tiles)
    lane = lanes_of((ROWS, LANES))
    row = lax.broadcasted_iota(jnp.int32, (ROWS, LANES), 0)
    live = row < n_var
    one = jnp.where(live & (lane < n_plane), roll_lanes(tile, -PANEL), 0.0)
    two = jnp.where(live & (lane < n_plane), roll_lanes(tile, -PANEL - n_plane), 0.0)
    left = one + roll_lanes(one, RING) + roll_lanes(two, 2 * RING)
    right = one + roll_lanes(two, RING) + roll_lanes(two, 2 * RING)
    inner = []
    for part in pair:
        at = jnp.where(lane < RING, roll_lanes(part, -HIGH), 0.0)
        inner.append(at + roll_lanes(at, RING) + roll_lanes(at, 2 * RING))
    place = lane % RING

    def turned(value, s):
        if not s:
            return value
        return jnp.where(place < RING - s, roll_lanes(value, -s), roll_lanes(value, RING - s))

    terms = []
    for s in range(RING // 2 + 1):
        left_s, right_s = turned(left, s), turned(right, s)
        term = pair_add(two_prod(left, right_s), two_prod(left_s, right))
        share = 1.0 if s else 0.5
        row_s = tuple(share * part[s : s + 1, :] for part in inner)
        terms.append(pair_mul(term, row_s))
    total = pair_tree(terms)
    total = pair_tree([pair_roll(total, -b, 1) for b in range(n_plane)])
    for shift in (4, 2, 1):
        total = pair_add(total, pair_roll(total, shift, 0))

    def everywhere(part, at):
        return jnp.broadcast_to(part[:, at : at + 1], (ROWS, LANES))

    square, cross, other = (
        tuple(everywhere(part, g * RING) for part in total) for g in range(3)
    )
    ratio = cross[0] / square[0]
    left_over = pair_add(cross, tuple(-p for p in pair_scale(square, ratio)))
    ratio = quick_two_sum(ratio, left_over[0] / square[0])
    rest = pair_add(other, tuple(-p for p in pair_mul(cross, ratio)))
    largest = everywhere(size, SIZE)
    inv_one = scale / jnp.sqrt(square[0]) / largest
    inv_two = scale / jnp.sqrt(rest[0]) / largest
    weight_ref[:ROWS, :] = inv_one * one
    weight_ref[ROWS:, :] = inv_two * two - (inv_two * ratio[0]) * one

    for a in range(n_plane):
        at = (a // n_var) * ROWS + a % n_var
        weights = jnp.broadcast_to(weight_ref[at : at + 1, :], (ROWS, LANES))
        spread = [everywhere(weights, b) for b in range(n_plane)]
        for x in range(wide_x):
            for h in range(cells_ref.shape[-1] // LANES):
                cut = slice(h * LANES, (h + 1) * LANES)
                value = spread[0] * cells_ref[x, :, cut]
                for b in range(1, n_plane):
                    value = value + spread[b] * cells_ref[b * wide_x + x, :, cut]
                out_ref[a * wide_x + x, :, cut] = value


VMEM = pl.BlockSpec(memory_space=pltpu.VMEM)
PARAMS = pltpu.CompilerParams(vmem_limit_bytes=32 * 1024 * 1024)


def body(test_vectors, base_coeffs, panel_set, owner_index):
    count_x = lax.axis_size("gx")
    count_r = lax.axis_size("row")
    n_vec, n_var, wide_x, wide_r, n_theta = test_vectors.shape
    n_plane = n_vec * n_var
    at_x, at_r = lax.axis_index("gx"), lax.axis_index("row")

    field = test_vectors.reshape((n_plane, wide_x, wide_r, n_theta))
    edge, turned = pl.pallas_call(
        prepare_kernel,
        out_shape=(
            jax.ShapeDtypeStruct((n_plane + 1, wide_x, 2 * RIM, n_theta), jnp.float32),
            jax.ShapeDtypeStruct((wide_x, wide_r, n_theta), jnp.float32),
        ),
        in_specs=[VMEM, VMEM],
        out_specs=(VMEM, VMEM),
        compiler_params=PARAMS,
        name="prepare",
    )(field[:, :, wide_r - 2 * RIM :], base_coeffs.transpose(1, 2, 0))
    ring = [(i, (i + 1) % count_r) for i in range(count_r)]
    edge = lax.ppermute(edge, "row", ring)
    edge, candidate = lax.optimization_barrier((edge, panel_set[0]))
    both = jnp.concatenate([field, turned[None]], axis=0)
    both = jnp.concatenate([edge, both], axis=2)
    both = both.reshape((n_plane + 1, wide_x * (wide_r + 2 * RIM), n_theta))
    outer = [(i, i + 1 if i % 2 else i - 1) for i in range(1, count_x - 1)]
    far = lax.ppermute(both, "gx", outer)
    mate = lax.ppermute(both, "gx", [(i, i ^ 1) for i in range(count_x)])

    panel = candidate / jnp.max(jnp.abs(candidate))
    panel = jnp.where(at_x * count_r + at_r == owner_index[0], panel, 0.0)
    panel = jnp.concatenate([panel[:n_var], panel[n_var:]], axis=1)
    panel = jnp.pad(panel, ((0, ROWS - n_var), (PANEL, LANES - PANEL - 2 * n_plane)))

    n_wide = 3
    n_tile = n_theta // ROWS
    sent = pl.pallas_call(
        lambda *refs: march_kernel(n_var, wide_x, wide_r, count_x, *refs),
        out_shape=jax.ShapeDtypeStruct((n_tile, ROWS, n_wide * LANES), jnp.float32),
        in_specs=[pl.BlockSpec(memory_space=pltpu.SMEM)] + [VMEM] * 4,
        out_specs=VMEM,
        scratch_shapes=[
            pltpu.VMEM((n_plane, n_theta + 2 * ROWS, LANES), jnp.float32),
            pltpu.VMEM((n_plane, n_theta + 2 * ROWS, LANES), jnp.float32),
            pltpu.VMEM((n_theta + ROWS, LANES), jnp.float32),
            pltpu.VMEM((n_tile, ROWS, n_wide * LANES), jnp.float32),
            pltpu.VMEM((2, n_tile, n_wide, ROWS, LANES), jnp.float32),
        ],
        compiler_params=PARAMS,
        name="march",
    )(jnp.stack([at_x, at_r]), both, mate, far, panel)
    got = lax.all_to_all(sent, "row", 0, 0, tiled=True)
    stats = pl.pallas_call(
        reduce_kernel,
        out_shape=jax.ShapeDtypeStruct((count_x, ROWS, LANES), jnp.float32),
        in_specs=[VMEM],
        out_specs=VMEM,
        compiler_params=PARAMS,
        name="reduce",
    )(got)
    stats = lax.all_to_all(stats, "gx", 0, 0, tiled=True)
    cells = pl.pallas_call(
        lambda *refs: relay_kernel(n_plane, wide_x, wide_r, *refs),
        out_shape=jax.ShapeDtypeStruct((n_plane * wide_x, ROWS, count_r * wide_r), jnp.float32),
        in_specs=[VMEM],
        out_specs=VMEM,
        compiler_params=PARAMS,
        name="relay",
    )(got)
    scale = math.sqrt(n_var * wide_x * count_x * wide_r * count_r * n_theta)
    basis = pl.pallas_call(
        lambda *refs: final_kernel(n_var, wide_x, scale, *refs),
        out_shape=jax.ShapeDtypeStruct(cells.shape, jnp.float32),
        in_specs=[VMEM, VMEM],
        out_specs=VMEM,
        scratch_shapes=[pltpu.VMEM((2 * ROWS, LANES), jnp.float32)],
        compiler_params=PARAMS,
        name="final",
    )(stats, cells)
    return basis.reshape((n_vec, n_var, wide_x, n_theta // count_r, count_r * wide_r))


def solution(mesh):
    placed = (
        P(None, None, "gx", "row", None),
        P(None, "gx", "row"),
        P(("gx", "row"), None, None),
        P(),
    )
    return jax.shard_map(
        body,
        mesh=mesh,
        in_specs=placed,
        out_specs=P(None, None, "gx", "row", None),
        check_vma=False,
    )
```

```python
import math

import jax
import jax.numpy as jnp
from jax import lax
from jax.experimental import pallas as pl
from jax.experimental.pallas import tpu as pltpu
from jax.sharding import PartitionSpec as P

STEPS = 2
UNROLL = 12
RIM = 2
LANES = 128
ROWS = 8
RING = 12
HIGH, LOW, SIZE, PANEL = 64, 76, 88, 100


def two_sum(a, b):
    total = a + b
    part = total - a
    return total, (a - (total - part)) + (b - part)


def quick_two_sum(a, b):
    total = a + b
    return total, b - (total - a)


def split(a):
    wide = a * 4097.0
    high = wide - (wide - a)
    return high, a - high


def two_prod(a, b):
    product = a * b
    a_high, a_low = split(a)
    b_high, b_low = split(b)
    return product, ((a_high * b_high - product) + a_high * b_low + a_low * b_high) + a_low * b_low


def pair_add(a, b):
    high, low = two_sum(a[0], b[0])
    return quick_two_sum(high, low + (a[1] + b[1]))


def pair_mul(a, b):
    high, low = two_prod(a[0], b[0])
    return quick_two_sum(high, low + (a[0] * b[1] + a[1] * b[0]))


def pair_scale(a, factor):
    high, low = two_prod(a[0], factor)
    return quick_two_sum(high, low + a[1] * factor)


def pair_roll(a, shift, axis):
    size = a[0].shape[axis]
    return tuple(pltpu.roll(part, shift % size, axis) for part in a)


def pair_tree(pairs):
    while len(pairs) > 1:
        rest = [pairs[-1]] if len(pairs) % 2 else []
        pairs = [pair_add(pairs[i], pairs[i + 1]) for i in range(0, len(pairs) - 1, 2)] + rest
    return pairs[0]


def tree(parts, join):
    while len(parts) > 1:
        rest = [parts[-1]] if len(parts) % 2 else []
        parts = [join(parts[i], parts[i + 1]) for i in range(0, len(parts) - 1, 2)] + rest
    return parts[0]


def lanes_of(shape):
    return lax.broadcasted_iota(jnp.int32, shape, 1)


def roll_lanes(value, shift):
    return pltpu.roll(value, shift % LANES, 1)


def safe_inverse(value):
    positive = value > 0
    return jnp.where(positive, 1.0 / jnp.where(positive, value, 1.0), 0.0)


def merge(tiles):
    size = tree(tiles, jnp.maximum)
    inverse = safe_inverse(size)
    scaled = []
    for tile in tiles:
        ratio = tile * inverse
        ratio = roll_lanes(ratio * ratio, HIGH - SIZE)
        scaled.append(pair_scale((tile, roll_lanes(tile, HIGH - LOW)), ratio))
    return pair_tree(scaled), size, tree(tiles, jnp.add)


def placed_at(lane, start, width, value, other):
    return jnp.where((lane >= start) & (lane < start + width), value, other)


def pack_stats(pair, size, panel):
    lane = lanes_of(size.shape)
    tile = placed_at(lane, HIGH, RING, pair[0], 0.0)
    tile = placed_at(lane, LOW, RING, roll_lanes(pair[1], LOW - HIGH), tile)
    tile = placed_at(lane, SIZE, RING, size, tile)
    return jnp.where(lane >= PANEL, panel, tile)


def march_kernel(
    n_var, wide_x, wide_r, count_x,
    place_ref, mid_ref, mate_ref, far_ref, panel_ref,
    out_ref, now_ref, next_ref, coeff_ref, packed_ref, parts_ref,
):
    n_plane = mid_ref.shape[0] - 1
    n_theta = mid_ref.shape[-1]
    n_tile = n_theta // ROWS
    deep = wide_r + 2 * RIM
    n_pair = n_var * n_var
    used = (wide_x + 2 * RIM) * deep

    mate_is_low = jnp.full((RIM * deep, n_theta), place_ref[0] % 2, jnp.int32) == 1

    def turn(plane):
        mate, far = mate_ref[plane], far_ref[plane]
        low = jnp.where(mate_is_low, mate, far)
        high = jnp.where(mate_is_low, far, mate)
        blank = jnp.zeros((LANES - used, n_theta), jnp.float32)
        return jnp.concatenate([low, mid_ref[plane], high, blank], axis=0).T

    for plane in range(n_plane):
        turned = turn(plane)
        now_ref[plane, ROWS : ROWS + n_theta, :] = turned
        now_ref[plane, ROWS - 1 : ROWS, :] = turned[n_theta - 1 :]
        now_ref[plane, ROWS + n_theta : ROWS + n_theta + 1, :] = turned[:1]
    coeff_ref[:n_theta, :] = turn(n_plane)
    viscous = coeff_ref[4 * n_pair : 4 * n_pair + 1, :]
    for i in range(n_var):
        own = 3 * n_pair + i * n_var + i
        coeff_ref[own : own + 1, :] = coeff_ref[own : own + 1, :] + (1.0 - 6.0 * viscous)
    for n, shift in enumerate((deep, -deep, 1, -1)):
        coeff_ref[n_theta + n : n_theta + n + 1, :] = roll_lanes(viscous, shift)

    lane = lanes_of((ROWS, LANES))
    at_x = lane // deep - RIM + place_ref[0] * wide_x
    inside = (at_x >= 0) & (at_x < wide_x * count_x) & (lane < used)
    first = place_ref[1] == 0
    from_above = ~((lane % deep == 2 * RIM - 1) & first)
    from_below = ~((lane % deep == 2 * RIM) & first)

    def coeff(index):
        return coeff_ref[index : index + 1, :]

    def advance(source_ref, tile):
        start = ROWS + tile * ROWS
        centre = [source_ref[b, pl.ds(start, ROWS), :] for b in range(n_plane)]
        before = [source_ref[b, pl.ds(start - 1, ROWS), :] for b in range(n_plane)]
        after = [source_ref[b, pl.ds(start + 1, ROWS), :] for b in range(n_plane)]
        differ = [a - b for a, b in zip(after, before)]
        both = [a + b for a, b in zip(after, before)]
        result = [None] * n_plane
        for i in range(n_var):
            for k in range(0, n_plane, n_var):
                def flux(start, values):
                    return tree([coeff(start + j * n_var + i) * values[k + j] for j in range(n_var)], jnp.add)

                own = centre[k + i]
                stream = flux(0, centre)
                radial = flux(n_pair, centre)
                local = flux(2 * n_pair, differ) + flux(3 * n_pair, centre)
                local = local + coeff(4 * n_pair) * both[k + i]
                above = roll_lanes(coeff(n_theta + 2) * own + radial, -1)
                below = roll_lanes(coeff(n_theta + 3) * own - radial, 1)
                local = local + roll_lanes(coeff(n_theta) * own + stream, -deep)
                local = local + roll_lanes(coeff(n_theta + 1) * own - stream, deep)
                local = local + jnp.where(from_above, above, 0.0) + jnp.where(from_below, below, 0.0)
                result[k + i] = local
        return result

    def keep(tile, result):
        for b in range(n_plane):
            next_ref[b, pl.ds(ROWS + tile * ROWS, ROWS), :] = jnp.where(inside, result[b], 0.0)

    group = wide_x * wide_r
    per_vreg = LANES // group
    n_wide = packed_ref.shape[-1] // LANES
    mine = []
    for x in range(wide_x):
        start = (x + RIM) * deep + RIM
        mine.append((lane >= start) & (lane < start + wide_r))

    def pack(tile, result, largest):
        for v in range(n_wide):
            pieces = []
            for b in range(v * per_vreg, min((v + 1) * per_vreg, n_plane)):
                for x in range(wide_x):
                    shift = (b % per_vreg) * group + x * wide_r - ((x + RIM) * deep + RIM)
                    pieces.append(roll_lanes(jnp.where(mine[x], result[b], 0.0), shift))
            packed = tree(pieces, jnp.add)
            packed_ref[tile, :, v * LANES : (v + 1) * LANES] = packed
            largest = jnp.maximum(largest, jnp.abs(packed))
        return largest

    for tile in (n_tile - 2, n_tile - 1, 0, 1):
        keep(tile, advance(now_ref, tile))
    for b in range(n_plane):
        next_ref[b, ROWS - 1 : ROWS, :] = next_ref[b, ROWS + n_theta - 1 : ROWS + n_theta, :]
        next_ref[b, ROWS + n_theta : ROWS + n_theta + 1, :] = next_ref[b, ROWS : ROWS + 1, :]

    def both_steps(tile, largest):
        ahead = advance(now_ref, tile + 2)
        largest = pack(tile, advance(next_ref, tile), largest)
        keep(tile + 2, ahead)
        return largest

    largest = jnp.zeros((ROWS, LANES), jnp.float32)
    largest = lax.fori_loop(0, n_tile - 4, both_steps, largest, unroll=UNROLL)
    for tile in range(n_tile - 4, n_tile):
        largest = pack(tile, advance(next_ref, tile), largest)
    largest = jnp.max(largest, axis=1, keepdims=True)
    largest = jnp.max(largest, axis=0, keepdims=True)
    inverse = safe_inverse(jnp.broadcast_to(largest, (ROWS, LANES)))
    largest = jnp.broadcast_to(largest, (ROWS, LANES))

    for tile in range(n_tile):
        for v in range(n_wide):
            high, low = split(packed_ref[tile, :, v * LANES : (v + 1) * LANES] * inverse)
            parts_ref[0, tile, v] = high
            parts_ref[1, tile, v] = low

    def shifted(part, tile, v, s):
        whole, rest = divmod(s, per_vreg)
        value = parts_ref[part, tile, (v + whole) % n_wide]
        if not rest:
            return value
        other = parts_ref[part, tile, (v + whole + 1) % n_wide]
        keep = lane < LANES - rest * group
        return jnp.where(keep, roll_lanes(value, -rest * group), roll_lanes(other, -rest * group))

    zero = jnp.zeros((ROWS, LANES), jnp.float32)
    pairs = [[(zero, zero)] * n_wide for _ in range(ROWS)]
    for s in range(RING // 2 + 1):
        for v in range(n_wide):
            if 2 * s == RING and v * per_vreg + s >= n_plane:
                continue
            total, error = zero, zero
            for tile in range(n_tile):
                a_high, a_low = parts_ref[0, tile, v], parts_ref[1, tile, v]
                if s:
                    b_high, b_low = shifted(0, tile, v, s), shifted(1, tile, v, s)
                    minor = a_high * b_low + a_low * b_high
                else:
                    b_high, b_low = a_high, a_low
                    minor = 2.0 * a_high * a_low
                total, lost = two_sum(total, a_high * b_high)
                error = error + (lost + (minor + a_low * b_low))
            pairs[s][v] = quick_two_sum(total, error)
    row = lax.broadcasted_iota(jnp.int32, (ROWS, LANES), 0)
    sums = []
    for v in range(n_wide):
        level = [pairs[s][v] for s in range(ROWS)]
        half = ROWS // 2
        while half:
            joined = []
            for s in range(half):
                a, b = level[s], level[s + half]
                front = (row // half) % 2 == 0
                a_turned, b_turned = pair_roll(a, -half, 0), pair_roll(b, half, 0)
                one = tuple(jnp.where(front, p, q) for p, q in zip(a, b_turned))
                two = tuple(jnp.where(front, p, q) for p, q in zip(a_turned, b))
                joined.append(pair_add(one, two))
            level = joined
            half //= 2
        sums.append(level[0])
    step = group // 2
    while step:
        sums = [pair_add(a, pair_roll(a, -step, 1)) for a in sums]
        step //= 2
    gathered = (zero, zero)
    for b in range(RING):
        turned = pair_roll(sums[b // per_vreg], HIGH + b - (b % per_vreg) * group, 1)
        gathered = tuple(jnp.where(lane == HIGH + b, p, q) for p, q in zip(turned, gathered))
    stats = pack_stats(gathered, largest, panel_ref[...])
    last = (n_wide - 1) * LANES
    for tile in range(n_tile):
        out_ref[tile, :, :last] = packed_ref[tile, :, :last]
        out_ref[tile, :, last:] = jnp.where(lane < HIGH, packed_ref[tile, :, last:], stats)


def prepare_kernel(tail_ref, coeff_ref, edge_ref, turned_ref):
    n_plane = tail_ref.shape[0]
    n_coeff = coeff_ref.shape[-1]
    edge_ref[:n_plane] = tail_ref[...]
    turned_ref[...] = jnp.zeros_like(turned_ref)
    turned_ref[:, :, :n_coeff] = coeff_ref[...]
    edge_ref[n_plane] = turned_ref[:, turned_ref.shape[1] - edge_ref.shape[2] :, :]


def reduce_kernel(got_ref, out_ref):
    count, _, wide = got_ref.shape
    pair, size, panel = merge([got_ref[n, :, wide - LANES :] for n in range(count)])
    tile = pack_stats(pair, size, panel)
    for n in range(out_ref.shape[0]):
        out_ref[n] = tile


def relay_kernel(n_plane, wide_x, wide_r, got_ref, out_ref):
    count = got_ref.shape[0]
    per_vreg = LANES // wide_r
    lane = lanes_of((ROWS, LANES))
    for g in range(n_plane * wide_x):
        v, slot = divmod(g, per_vreg)
        halves = []
        for half in range(count // per_vreg):
            value = jnp.zeros((ROWS, LANES), jnp.float32)
            for n in range(per_vreg):
                source = got_ref[half * per_vreg + n, :, v * LANES : (v + 1) * LANES]
                turned = roll_lanes(source, (n - slot) * wide_r)
                value = placed_at(lane, n * wide_r, wide_r, turned, value)
            halves.append(value)
        whole = jnp.concatenate(halves, axis=1)
        out_ref[g] = pltpu.roll(whole, whole.shape[1] - RIM, 1)


def final_kernel(n_var, wide_x, scale, got_ref, cells_ref, out_ref, weight_ref):
    n_plane = 2 * n_var
    tiles = [got_ref[n] for n in range(got_ref.shape[0])]
    pair, size, tile = merge(tiles)
    lane = lanes_of((ROWS, LANES))
    row = lax.broadcasted_iota(jnp.int32, (ROWS, LANES), 0)
    live = row < n_var
    one = jnp.where(live & (lane < n_plane), roll_lanes(tile, -PANEL), 0.0)
    two = jnp.where(live & (lane < n_plane), roll_lanes(tile, -PANEL - n_plane), 0.0)
    left = one + roll_lanes(one, RING) + roll_lanes(two, 2 * RING)
    right = one + roll_lanes(two, RING) + roll_lanes(two, 2 * RING)
    inner = []
    for part in pair:
        at = jnp.where(lane < RING, roll_lanes(part, -HIGH), 0.0)
        inner.append(at + roll_lanes(at, RING) + roll_lanes(at, 2 * RING))
    place = lane % RING

    def turned(value, s):
        if not s:
            return value
        return jnp.where(place < RING - s, roll_lanes(value, -s), roll_lanes(value, RING - s))

    terms = []
    for s in range(RING // 2 + 1):
        left_s, right_s = turned(left, s), turned(right, s)
        term = pair_add(two_prod(left, right_s), two_prod(left_s, right))
        share = 1.0 if s else 0.5
        row_s = tuple(share * part[s : s + 1, :] for part in inner)
        terms.append(pair_mul(term, row_s))
    total = pair_tree(terms)
    total = pair_tree([pair_roll(total, -b, 1) for b in range(n_plane)])
    for shift in (4, 2, 1):
        total = pair_add(total, pair_roll(total, shift, 0))

    def everywhere(part, at):
        return jnp.broadcast_to(part[:, at : at + 1], (ROWS, LANES))

    square, cross, other = (
        tuple(everywhere(part, g * RING) for part in total) for g in range(3)
    )
    ratio = cross[0] / square[0]
    left_over = pair_add(cross, tuple(-p for p in pair_scale(square, ratio)))
    ratio = quick_two_sum(ratio, left_over[0] / square[0])
    rest = pair_add(other, tuple(-p for p in pair_mul(cross, ratio)))
    largest = everywhere(size, SIZE)
    inv_one = scale / jnp.sqrt(square[0]) / largest
    inv_two = scale / jnp.sqrt(rest[0]) / largest
    weight_ref[:ROWS, :] = inv_one * one
    weight_ref[ROWS:, :] = inv_two * two - (inv_two * ratio[0]) * one

    for a in range(n_plane):
        at = (a // n_var) * ROWS + a % n_var
        weights = jnp.broadcast_to(weight_ref[at : at + 1, :], (ROWS, LANES))
        spread = [everywhere(weights, b) for b in range(n_plane)]
        for x in range(wide_x):
            for h in range(cells_ref.shape[-1] // LANES):
                cut = slice(h * LANES, (h + 1) * LANES)
                value = spread[0] * cells_ref[x, :, cut]
                for b in range(1, n_plane):
                    value = value + spread[b] * cells_ref[b * wide_x + x, :, cut]
                out_ref[a * wide_x + x, :, cut] = value


VMEM = pl.BlockSpec(memory_space=pltpu.VMEM)
PARAMS = pltpu.CompilerParams(vmem_limit_bytes=32 * 1024 * 1024)


def body(test_vectors, base_coeffs, panel_set, owner_index):
    count_x = lax.axis_size("gx")
    count_r = lax.axis_size("row")
    n_vec, n_var, wide_x, wide_r, n_theta = test_vectors.shape
    n_plane = n_vec * n_var
    at_x, at_r = lax.axis_index("gx"), lax.axis_index("row")

    field = test_vectors.reshape((n_plane, wide_x, wide_r, n_theta))
    edge, turned = pl.pallas_call(
        prepare_kernel,
        out_shape=(
            jax.ShapeDtypeStruct((n_plane + 1, wide_x, 2 * RIM, n_theta), jnp.float32),
            jax.ShapeDtypeStruct((wide_x, wide_r, n_theta), jnp.float32),
        ),
        in_specs=[VMEM, VMEM],
        out_specs=(VMEM, VMEM),
        compiler_params=PARAMS,
        name="prepare",
    )(field[:, :, wide_r - 2 * RIM :], base_coeffs.transpose(1, 2, 0))
    ring = [(i, (i + 1) % count_r) for i in range(count_r)]
    edge = lax.ppermute(edge, "row", ring)
    edge, candidate = lax.optimization_barrier((edge, panel_set[0]))
    both = jnp.concatenate([field, turned[None]], axis=0)
    both = jnp.concatenate([edge, both], axis=2)
    both = both.reshape((n_plane + 1, wide_x * (wide_r + 2 * RIM), n_theta))
    outer = [(i, i + 1 if i % 2 else i - 1) for i in range(1, count_x - 1)]
    far = lax.ppermute(both, "gx", outer)
    mate = lax.ppermute(both, "gx", [(i, i ^ 1) for i in range(count_x)])

    panel = candidate / jnp.max(jnp.abs(candidate))
    panel = jnp.where(at_x * count_r + at_r == owner_index[0], panel, 0.0)
    panel = jnp.concatenate([panel[:n_var], panel[n_var:]], axis=1)
    panel = jnp.pad(panel, ((0, ROWS - n_var), (PANEL, LANES - PANEL - 2 * n_plane)))

    n_wide = 3
    n_tile = n_theta // ROWS
    sent = pl.pallas_call(
        lambda *refs: march_kernel(n_var, wide_x, wide_r, count_x, *refs),
        out_shape=jax.ShapeDtypeStruct((n_tile, ROWS, n_wide * LANES), jnp.float32),
        in_specs=[pl.BlockSpec(memory_space=pltpu.SMEM)] + [VMEM] * 4,
        out_specs=VMEM,
        scratch_shapes=[
            pltpu.VMEM((n_plane, n_theta + 2 * ROWS, LANES), jnp.float32),
            pltpu.VMEM((n_plane, n_theta + 2 * ROWS, LANES), jnp.float32),
            pltpu.VMEM((n_theta + ROWS, LANES), jnp.float32),
            pltpu.VMEM((n_tile, ROWS, n_wide * LANES), jnp.float32),
            pltpu.VMEM((2, n_tile, n_wide, ROWS, LANES), jnp.float32),
        ],
        compiler_params=PARAMS,
        name="march",
    )(jnp.stack([at_x, at_r]), both, mate, far, panel)
    got = lax.all_to_all(sent, "row", 0, 0, tiled=True)
    stats = pl.pallas_call(
        reduce_kernel,
        out_shape=jax.ShapeDtypeStruct((count_x, ROWS, LANES), jnp.float32),
        in_specs=[VMEM],
        out_specs=VMEM,
        compiler_params=PARAMS,
        name="reduce",
    )(got)
    stats = lax.all_to_all(stats, "gx", 0, 0, tiled=True)
    cells = pl.pallas_call(
        lambda *refs: relay_kernel(n_plane, wide_x, wide_r, *refs),
        out_shape=jax.ShapeDtypeStruct((n_plane * wide_x, ROWS, count_r * wide_r), jnp.float32),
        in_specs=[VMEM],
        out_specs=VMEM,
        compiler_params=PARAMS,
        name="relay",
    )(got)
    scale = math.sqrt(n_var * wide_x * count_x * wide_r * count_r * n_theta)
    basis = pl.pallas_call(
        lambda *refs: final_kernel(n_var, wide_x, scale, *refs),
        out_shape=jax.ShapeDtypeStruct(cells.shape, jnp.float32),
        in_specs=[VMEM, VMEM],
        out_specs=VMEM,
        scratch_shapes=[pltpu.VMEM((2 * ROWS, LANES), jnp.float32)],
        compiler_params=PARAMS,
        name="final",
    )(stats, cells)
    return basis.reshape((n_vec, n_var, wide_x, n_theta // count_r, count_r * wide_r))


def solution(mesh):
    placed = (
        P(None, None, "gx", "row", None),
        P(None, "gx", "row"),
        P(("gx", "row"), None, None),
        P(),
    )
    return jax.shard_map(
        body,
        mesh=mesh,
        in_specs=placed,
        out_specs=P(None, None, "gx", "row", None),
        check_vma=False,
    )
```

```python
import math

import jax
import jax.numpy as jnp
from jax import lax
from jax.experimental import pallas as pl
from jax.experimental.pallas import tpu as pltpu
from jax.sharding import PartitionSpec as P

STEPS = 2
UNROLL = 12
RIM = 2
LANES = 128
ROWS = 8
RING = 12
HIGH, LOW, SIZE, PANEL = 64, 76, 88, 100


def two_sum(a, b):
    total = a + b
    part = total - a
    return total, (a - (total - part)) + (b - part)


def quick_two_sum(a, b):
    total = a + b
    return total, b - (total - a)


def split(a):
    wide = a * 4097.0
    high = wide - (wide - a)
    return high, a - high


def two_prod(a, b):
    product = a * b
    a_high, a_low = split(a)
    b_high, b_low = split(b)
    return product, ((a_high * b_high - product) + a_high * b_low + a_low * b_high) + a_low * b_low


def pair_add(a, b):
    high, low = two_sum(a[0], b[0])
    return quick_two_sum(high, low + (a[1] + b[1]))


def pair_mul(a, b):
    high, low = two_prod(a[0], b[0])
    return quick_two_sum(high, low + (a[0] * b[1] + a[1] * b[0]))


def pair_scale(a, factor):
    high, low = two_prod(a[0], factor)
    return quick_two_sum(high, low + a[1] * factor)


def pair_roll(a, shift, axis):
    size = a[0].shape[axis]
    return tuple(pltpu.roll(part, shift % size, axis) for part in a)


def pair_tree(pairs):
    while len(pairs) > 1:
        rest = [pairs[-1]] if len(pairs) % 2 else []
        pairs = [pair_add(pairs[i], pairs[i + 1]) for i in range(0, len(pairs) - 1, 2)] + rest
    return pairs[0]


def tree(parts, join):
    while len(parts) > 1:
        rest = [parts[-1]] if len(parts) % 2 else []
        parts = [join(parts[i], parts[i + 1]) for i in range(0, len(parts) - 1, 2)] + rest
    return parts[0]


def lanes_of(shape):
    return lax.broadcasted_iota(jnp.int32, shape, 1)


def roll_lanes(value, shift):
    return pltpu.roll(value, shift % LANES, 1)


def safe_inverse(value):
    positive = value > 0
    return jnp.where(positive, 1.0 / jnp.where(positive, value, 1.0), 0.0)


def merge(tiles):
    size = tree(tiles, jnp.maximum)
    inverse = safe_inverse(size)
    scaled = []
    for tile in tiles:
        ratio = tile * inverse
        ratio = roll_lanes(ratio * ratio, HIGH - SIZE)
        scaled.append(pair_scale((tile, roll_lanes(tile, HIGH - LOW)), ratio))
    return pair_tree(scaled), size, tree(tiles, jnp.add)


def placed_at(lane, start, width, value, other):
    return jnp.where((lane >= start) & (lane < start + width), value, other)


def pack_stats(pair, size, panel):
    lane = lanes_of(size.shape)
    tile = placed_at(lane, HIGH, RING, pair[0], 0.0)
    tile = placed_at(lane, LOW, RING, roll_lanes(pair[1], LOW - HIGH), tile)
    tile = placed_at(lane, SIZE, RING, size, tile)
    return jnp.where(lane >= PANEL, panel, tile)


def march_kernel(
    n_var, wide_x, wide_r, count_x,
    place_ref, mid_ref, mate_ref, far_ref, panel_ref,
    out_ref, now_ref, next_ref, coeff_ref, packed_ref, parts_ref,
):
    n_plane = mid_ref.shape[0] - 1
    n_theta = mid_ref.shape[-1]
    n_tile = n_theta // ROWS
    deep = wide_r + 2 * RIM
    n_pair = n_var * n_var
    used = (wide_x + 2 * RIM) * deep

    mate_is_low = jnp.full((RIM * deep, n_theta), place_ref[0] % 2, jnp.int32) == 1

    def turn(plane):
        mate, far = mate_ref[plane], far_ref[plane]
        low = jnp.where(mate_is_low, mate, far)
        high = jnp.where(mate_is_low, far, mate)
        blank = jnp.zeros((LANES - used, n_theta), jnp.float32)
        return jnp.concatenate([low, mid_ref[plane], high, blank], axis=0).T

    for plane in range(n_plane):
        turned = turn(plane)
        now_ref[plane, ROWS : ROWS + n_theta, :] = turned
        now_ref[plane, ROWS - 1 : ROWS, :] = turned[n_theta - 1 :]
        now_ref[plane, ROWS + n_theta : ROWS + n_theta + 1, :] = turned[:1]
    coeff_ref[:n_theta, :] = turn(n_plane)
    viscous = coeff_ref[4 * n_pair : 4 * n_pair + 1, :]
    for i in range(n_var):
        own = 3 * n_pair + i * n_var + i
        coeff_ref[own : own + 1, :] = coeff_ref[own : own + 1, :] + (1.0 - 6.0 * viscous)
    for n, shift in enumerate((deep, -deep, 1, -1)):
        coeff_ref[n_theta + n : n_theta + n + 1, :] = roll_lanes(viscous, shift)

    lane = lanes_of((ROWS, LANES))
    at_x = lane // deep - RIM + place_ref[0] * wide_x
    inside = (at_x >= 0) & (at_x < wide_x * count_x) & (lane < used)
    first = place_ref[1] == 0
    from_above = ~((lane % deep == 2 * RIM - 1) & first)
    from_below = ~((lane % deep == 2 * RIM) & first)

    def coeff(index):
        return coeff_ref[index : index + 1, :]

    def advance(source_ref, tile):
        start = ROWS + tile * ROWS
        centre = [source_ref[b, pl.ds(start, ROWS), :] for b in range(n_plane)]
        before = [source_ref[b, pl.ds(start - 1, ROWS), :] for b in range(n_plane)]
        after = [source_ref[b, pl.ds(start + 1, ROWS), :] for b in range(n_plane)]
        differ = [a - b for a, b in zip(after, before)]
        both = [a + b for a, b in zip(after, before)]
        result = [None] * n_plane
        for i in range(n_var):
            for k in range(0, n_plane, n_var):
                def flux(start, values):
                    return tree([coeff(start + j * n_var + i) * values[k + j] for j in range(n_var)], jnp.add)

                own = centre[k + i]
                stream = flux(0, centre)
                radial = flux(n_pair, centre)
                local = flux(2 * n_pair, differ) + flux(3 * n_pair, centre)
                local = local + coeff(4 * n_pair) * both[k + i]
                above = roll_lanes(coeff(n_theta + 2) * own + radial, -1)
                below = roll_lanes(coeff(n_theta + 3) * own - radial, 1)
                local = local + roll_lanes(coeff(n_theta) * own + stream, -deep)
                local = local + roll_lanes(coeff(n_theta + 1) * own - stream, deep)
                local = local + jnp.where(from_above, above, 0.0) + jnp.where(from_below, below, 0.0)
                result[k + i] = local
        return result

    def keep(tile, result):
        for b in range(n_plane):
            next_ref[b, pl.ds(ROWS + tile * ROWS, ROWS), :] = jnp.where(inside, result[b], 0.0)

    group = wide_x * wide_r
    per_vreg = LANES // group
    n_wide = packed_ref.shape[-1] // LANES
    mine = []
    for x in range(wide_x):
        start = (x + RIM) * deep + RIM
        mine.append((lane >= start) & (lane < start + wide_r))

    def pack(tile, result, largest):
        for v in range(n_wide):
            pieces = []
            for b in range(v * per_vreg, min((v + 1) * per_vreg, n_plane)):
                for x in range(wide_x):
                    shift = (b % per_vreg) * group + x * wide_r - ((x + RIM) * deep + RIM)
                    pieces.append(roll_lanes(jnp.where(mine[x], result[b], 0.0), shift))
            packed = tree(pieces, jnp.add)
            packed_ref[tile, :, v * LANES : (v + 1) * LANES] = packed
            largest = jnp.maximum(largest, jnp.abs(packed))
        return largest

    for tile in (n_tile - 2, n_tile - 1, 0, 1):
        keep(tile, advance(now_ref, tile))
    for b in range(n_plane):
        next_ref[b, ROWS - 1 : ROWS, :] = next_ref[b, ROWS + n_theta - 1 : ROWS + n_theta, :]
        next_ref[b, ROWS + n_theta : ROWS + n_theta + 1, :] = next_ref[b, ROWS : ROWS + 1, :]

    def both_steps(tile, largest):
        ahead = advance(now_ref, tile + 2)
        largest = pack(tile, advance(next_ref, tile), largest)
        keep(tile + 2, ahead)
        return largest

    largest = jnp.zeros((ROWS, LANES), jnp.float32)
    largest = lax.fori_loop(0, n_tile - 4, both_steps, largest, unroll=UNROLL)
    for tile in range(n_tile - 4, n_tile):
        largest = pack(tile, advance(next_ref, tile), largest)
    largest = jnp.max(largest, axis=1, keepdims=True)
    largest = jnp.max(largest, axis=0, keepdims=True)
    inverse = safe_inverse(jnp.broadcast_to(largest, (ROWS, LANES)))
    largest = jnp.broadcast_to(largest, (ROWS, LANES))

    for tile in range(n_tile):
        for v in range(n_wide):
            high, low = split(packed_ref[tile, :, v * LANES : (v + 1) * LANES] * inverse)
            parts_ref[0, tile, v] = high
            parts_ref[1, tile, v] = low

    def shifted(part, tile, v, s):
        whole, rest = divmod(s, per_vreg)
        value = parts_ref[part, tile, (v + whole) % n_wide]
        if not rest:
            return value
        other = parts_ref[part, tile, (v + whole + 1) % n_wide]
        keep = lane < LANES - rest * group
        return jnp.where(keep, roll_lanes(value, -rest * group), roll_lanes(other, -rest * group))

    zero = jnp.zeros((ROWS, LANES), jnp.float32)
    pairs = [[(zero, zero)] * n_wide for _ in range(ROWS)]
    for s in range(RING // 2 + 1):
        for v in range(n_wide):
            if 2 * s == RING and v * per_vreg + s >= n_plane:
                continue
            total, error = zero, zero
            for tile in range(n_tile):
                a_high, a_low = parts_ref[0, tile, v], parts_ref[1, tile, v]
                if s:
                    b_high, b_low = shifted(0, tile, v, s), shifted(1, tile, v, s)
                    minor = a_high * b_low + a_low * b_high
                else:
                    b_high, b_low = a_high, a_low
                    minor = 2.0 * a_high * a_low
                total, lost = two_sum(total, a_high * b_high)
                error = error + (lost + (minor + a_low * b_low))
            pairs[s][v] = quick_two_sum(total, error)
    row = lax.broadcasted_iota(jnp.int32, (ROWS, LANES), 0)
    sums = []
    for v in range(n_wide):
        level = [pairs[s][v] for s in range(ROWS)]
        half = ROWS // 2
        while half:
            joined = []
            for s in range(half):
                a, b = level[s], level[s + half]
                front = (row // half) % 2 == 0
                a_turned, b_turned = pair_roll(a, -half, 0), pair_roll(b, half, 0)
                one = tuple(jnp.where(front, p, q) for p, q in zip(a, b_turned))
                two = tuple(jnp.where(front, p, q) for p, q in zip(a_turned, b))
                joined.append(pair_add(one, two))
            level = joined
            half //= 2
        sums.append(level[0])
    step = group // 2
    while step:
        sums = [pair_add(a, pair_roll(a, -step, 1)) for a in sums]
        step //= 2
    gathered = (zero, zero)
    for b in range(RING):
        turned = pair_roll(sums[b // per_vreg], HIGH + b - (b % per_vreg) * group, 1)
        gathered = tuple(jnp.where(lane == HIGH + b, p, q) for p, q in zip(turned, gathered))
    stats = pack_stats(gathered, largest, panel_ref[...])
    last = (n_wide - 1) * LANES
    for tile in range(n_tile):
        out_ref[tile, :, :last] = packed_ref[tile, :, :last]
        out_ref[tile, :, last:] = jnp.where(lane < HIGH, packed_ref[tile, :, last:], stats)


def prepare_kernel(tail_ref, coeff_ref, edge_ref, turned_ref):
    n_plane = tail_ref.shape[0]
    n_coeff = coeff_ref.shape[-1]
    edge_ref[:n_plane] = tail_ref[...]
    turned_ref[...] = jnp.zeros_like(turned_ref)
    turned_ref[:, :, :n_coeff] = coeff_ref[...]
    edge_ref[n_plane] = turned_ref[:, turned_ref.shape[1] - edge_ref.shape[2] :, :]


def reduce_kernel(got_ref, out_ref):
    count, _, wide = got_ref.shape
    pair, size, panel = merge([got_ref[n, :, wide - LANES :] for n in range(count)])
    tile = pack_stats(pair, size, panel)
    half = ROWS // 2
    folded = jnp.where(lanes_of(tile.shape) < HIGH, roll_lanes(tile, HIGH), pltpu.roll(tile, half, 0))
    for n in range(out_ref.shape[0]):
        out_ref[n] = folded[:half]


def relay_kernel(n_plane, wide_x, wide_r, got_ref, out_ref):
    count = got_ref.shape[0]
    per_vreg = LANES // wide_r
    lane = lanes_of((ROWS, LANES))
    for g in range(n_plane * wide_x):
        v, slot = divmod(g, per_vreg)
        halves = []
        for half in range(count // per_vreg):
            value = jnp.zeros((ROWS, LANES), jnp.float32)
            for n in range(per_vreg):
                source = got_ref[half * per_vreg + n, :, v * LANES : (v + 1) * LANES]
                turned = roll_lanes(source, (n - slot) * wide_r)
                value = placed_at(lane, n * wide_r, wide_r, turned, value)
            halves.append(value)
        whole = jnp.concatenate(halves, axis=1)
        out_ref[g] = pltpu.roll(whole, whole.shape[1] - RIM, 1)


def final_kernel(n_var, wide_x, scale, got_ref, cells_ref, out_ref, weight_ref):
    n_plane = 2 * n_var
    upper = lax.broadcasted_iota(jnp.int32, (ROWS, LANES), 0) < ROWS // 2
    tiles = []
    for n in range(got_ref.shape[0]):
        twice = jnp.concatenate([got_ref[n], got_ref[n]], axis=0)
        tiles.append(jnp.where(upper, roll_lanes(twice, HIGH), twice))
    pair, size, tile = merge(tiles)
    lane = lanes_of((ROWS, LANES))
    row = lax.broadcasted_iota(jnp.int32, (ROWS, LANES), 0)
    live = row < n_var
    one = jnp.where(live & (lane < n_plane), roll_lanes(tile, -PANEL), 0.0)
    two = jnp.where(live & (lane < n_plane), roll_lanes(tile, -PANEL - n_plane), 0.0)
    left = one + roll_lanes(one, RING) + roll_lanes(two, 2 * RING)
    right = one + roll_lanes(two, RING) + roll_lanes(two, 2 * RING)
    inner = []
    for part in pair:
        at = jnp.where(lane < RING, roll_lanes(part, -HIGH), 0.0)
        inner.append(at + roll_lanes(at, RING) + roll_lanes(at, 2 * RING))
    place = lane % RING

    def turned(value, s):
        if not s:
            return value
        return jnp.where(place < RING - s, roll_lanes(value, -s), roll_lanes(value, RING - s))

    terms = []
    for s in range(RING // 2 + 1):
        left_s, right_s = turned(left, s), turned(right, s)
        term = pair_add(two_prod(left, right_s), two_prod(left_s, right))
        share = 1.0 if s else 0.5
        row_s = tuple(share * part[s : s + 1, :] for part in inner)
        terms.append(pair_mul(term, row_s))
    total = pair_tree(terms)
    total = pair_tree([pair_roll(total, -b, 1) for b in range(n_plane)])
    for shift in (4, 2, 1):
        total = pair_add(total, pair_roll(total, shift, 0))

    def everywhere(part, at):
        return jnp.broadcast_to(part[:, at : at + 1], (ROWS, LANES))

    square, cross, other = (
        tuple(everywhere(part, g * RING) for part in total) for g in range(3)
    )
    ratio = cross[0] / square[0]
    left_over = pair_add(cross, tuple(-p for p in pair_scale(square, ratio)))
    ratio = quick_two_sum(ratio, left_over[0] / square[0])
    rest = pair_add(other, tuple(-p for p in pair_mul(cross, ratio)))
    largest = everywhere(size, SIZE)
    inv_one = scale / jnp.sqrt(square[0]) / largest
    inv_two = scale / jnp.sqrt(rest[0]) / largest
    weight_ref[:ROWS, :] = inv_one * one
    weight_ref[ROWS:, :] = inv_two * two - (inv_two * ratio[0]) * one

    for a in range(n_plane):
        at = (a // n_var) * ROWS + a % n_var
        weights = jnp.broadcast_to(weight_ref[at : at + 1, :], (ROWS, LANES))
        spread = [everywhere(weights, b) for b in range(n_plane)]
        for x in range(wide_x):
            for h in range(cells_ref.shape[-1] // LANES):
                cut = slice(h * LANES, (h + 1) * LANES)
                value = spread[0] * cells_ref[x, :, cut]
                for b in range(1, n_plane):
                    value = value + spread[b] * cells_ref[b * wide_x + x, :, cut]
                out_ref[a * wide_x + x, :, cut] = value


VMEM = pl.BlockSpec(memory_space=pltpu.VMEM)
PARAMS = pltpu.CompilerParams(vmem_limit_bytes=32 * 1024 * 1024)


def body(test_vectors, base_coeffs, panel_set, owner_index):
    count_x = lax.axis_size("gx")
    count_r = lax.axis_size("row")
    n_vec, n_var, wide_x, wide_r, n_theta = test_vectors.shape
    n_plane = n_vec * n_var
    at_x, at_r = lax.axis_index("gx"), lax.axis_index("row")

    field = test_vectors.reshape((n_plane, wide_x, wide_r, n_theta))
    edge, turned = pl.pallas_call(
        prepare_kernel,
        out_shape=(
            jax.ShapeDtypeStruct((n_plane + 1, wide_x, 2 * RIM, n_theta), jnp.float32),
            jax.ShapeDtypeStruct((wide_x, wide_r, n_theta), jnp.float32),
        ),
        in_specs=[VMEM, VMEM],
        out_specs=(VMEM, VMEM),
        compiler_params=PARAMS,
        name="prepare",
    )(field[:, :, wide_r - 2 * RIM :], base_coeffs.transpose(1, 2, 0))
    ring = [(i, (i + 1) % count_r) for i in range(count_r)]
    edge = lax.ppermute(edge, "row", ring)
    edge, candidate = lax.optimization_barrier((edge, panel_set[0]))
    both = jnp.concatenate([field, turned[None]], axis=0)
    both = jnp.concatenate([edge, both], axis=2)
    both = both.reshape((n_plane + 1, wide_x * (wide_r + 2 * RIM), n_theta))
    outer = [(i, i + 1 if i % 2 else i - 1) for i in range(1, count_x - 1)]
    far = lax.ppermute(both, "gx", outer)
    mate = lax.ppermute(both, "gx", [(i, i ^ 1) for i in range(count_x)])

    panel = candidate / jnp.max(jnp.abs(candidate))
    panel = jnp.where(at_x * count_r + at_r == owner_index[0], panel, 0.0)
    panel = jnp.concatenate([panel[:n_var], panel[n_var:]], axis=1)
    panel = jnp.pad(panel, ((0, ROWS - n_var), (PANEL, LANES - PANEL - 2 * n_plane)))

    n_wide = 3
    n_tile = n_theta // ROWS
    sent = pl.pallas_call(
        lambda *refs: march_kernel(n_var, wide_x, wide_r, count_x, *refs),
        out_shape=jax.ShapeDtypeStruct((n_tile, ROWS, n_wide * LANES), jnp.float32),
        in_specs=[pl.BlockSpec(memory_space=pltpu.SMEM)] + [VMEM] * 4,
        out_specs=VMEM,
        scratch_shapes=[
            pltpu.VMEM((n_plane, n_theta + 2 * ROWS, LANES), jnp.float32),
            pltpu.VMEM((n_plane, n_theta + 2 * ROWS, LANES), jnp.float32),
            pltpu.VMEM((n_theta + ROWS, LANES), jnp.float32),
            pltpu.VMEM((n_tile, ROWS, n_wide * LANES), jnp.float32),
            pltpu.VMEM((2, n_tile, n_wide, ROWS, LANES), jnp.float32),
        ],
        compiler_params=PARAMS,
        name="march",
    )(jnp.stack([at_x, at_r]), both, mate, far, panel)
    got = lax.all_to_all(sent, "row", 0, 0, tiled=True)
    stats = pl.pallas_call(
        reduce_kernel,
        out_shape=jax.ShapeDtypeStruct((count_x, ROWS // 2, LANES), jnp.float32),
        in_specs=[VMEM],
        out_specs=VMEM,
        compiler_params=PARAMS,
        name="reduce",
    )(got)
    stats = lax.all_to_all(stats, "gx", 0, 0, tiled=True)
    cells = pl.pallas_call(
        lambda *refs: relay_kernel(n_plane, wide_x, wide_r, *refs),
        out_shape=jax.ShapeDtypeStruct((n_plane * wide_x, ROWS, count_r * wide_r), jnp.float32),
        in_specs=[VMEM],
        out_specs=VMEM,
        compiler_params=PARAMS,
        name="relay",
    )(got)
    scale = math.sqrt(n_var * wide_x * count_x * wide_r * count_r * n_theta)
    basis = pl.pallas_call(
        lambda *refs: final_kernel(n_var, wide_x, scale, *refs),
        out_shape=jax.ShapeDtypeStruct(cells.shape, jnp.float32),
        in_specs=[VMEM, VMEM],
        out_specs=VMEM,
        scratch_shapes=[pltpu.VMEM((2 * ROWS, LANES), jnp.float32)],
        compiler_params=PARAMS,
        name="final",
    )(stats, cells)
    return basis.reshape((n_vec, n_var, wide_x, n_theta // count_r, count_r * wide_r))


def solution(mesh):
    placed = (
        P(None, None, "gx", "row", None),
        P(None, "gx", "row"),
        P(("gx", "row"), None, None),
        P(),
    )
    return jax.shard_map(
        body,
        mesh=mesh,
        in_specs=placed,
        out_specs=P(None, None, "gx", "row", None),
        check_vma=False,
    )
```
